256 devices in a mesh: group: 4 (over x), bulk: 64 (over y, z, core).
Axes of the slice: x: 4, y: 4, z: 8, core: 2. Of those that a mesh axis runs over, the one named last changes fastest.
Arguments:
- right_sides: float32 [32, 524288], P(None, ('group', 'bulk')), may hold values from -6 to 6
- points: float32 [3, 524288], P(None, ('group', 'bulk')), may hold values from 0 to 4
- basis: float32 [2048, 64, 256], P(('group', 'bulk')), may hold values from -0.375 to 0.375
- transfer: float32 [3840, 64, 64], P(('group', 'bulk')), may hold values from -0.5 to 0.5
- skeleton: float32 [3840, 3, 64], P(('group', 'bulk')), may hold values from 0 to 2
- near_list: int32 [2048, 8], P(('group', 'bulk')), may hold values from 0 to 2047, as said below
- near_count: int32 [2048], P(('group', 'bulk')), may hold values from 0 to 8
- inter_list: int32 [3840, 8], P(('group', 'bulk')), may hold values from 0 to 2047, as said below
- inter_count: int32 [3840], P(('group', 'bulk')), may hold values from 0 to 8
- upper_transfer: float32 [256, 64, 64], replicated, may hold values from -0.5 to 0.5
- upper_skeleton: float32 [256, 3, 64], replicated, may hold values from 0 to 2
- upper_list: int32 [256, 8], replicated, may hold values from 0 to 255, as said below
- upper_count: int32 [256], replicated, may hold values from 0 to 8, as said below
Outputs:
- product: float32 [32, 524288], P(None, ('group', 'bulk'))
The draws below stay inside these ranges and needn't reach their ends.
Inputs may be any that keep to these rules, and one draw needn't show every extreme that they name: `near_list`: row t holds distinct leaves other than t at most 4 leaves away; only the first near_count[t] entries count, the rest are in range and are ignored. `inter_list`: A node's row holds distinct other nodes of its level, each of the first inter_count entries at most max(m // 2, 1) places away where m is the level's nodes on one device; only the first inter_count entries count, the rest are in range and are ignored. `upper_list`: row h holds distinct other heap nodes of h's level; at levels with more nodes than there are indices of group, they lie below the same ancestor at the level that has one node per index of group. Only the first upper_count entries count, the rest are in range and are ignored. `upper_count`: entries 0 and 1 are 0.
All inputs are finite; a program needn't handle non-finite values.
Results may differ from the reference program's by a relative error of at most 0.0003.
Values sent between devices are 32-bit elements; how exact they have to be, the bound alone decides.
A program may use at most 128 MiB of HBM per device.

```python
import jax
import jax.numpy as jnp
from jax import lax

LEAF = 256
RANK = 64
RHS = 32
NEAR = 8
NI = 8
LPD = 8
NL = 2048
NPTS = 524288
LNODES = 3840
HALF = 4
N_GROUP = 4
N_BULK = 64
DEVICES = 256


sheet_columns = 64


sheet_scale = 0.0625


sheet_depth = 0.5


def choose(base_key, sources, usable, limit, keep_count):
    row_count = sources.shape[0]
    candidate_count = sources.shape[1]
    score_key, count_key = jax.random.split(base_key)
    scores = jax.random.randint(score_key, (row_count, candidate_count), 0, 1 << 20) * candidate_count + jnp.arange(candidate_count)[None, :]
    scores = jnp.where(usable, scores, (1 << 20) * candidate_count + candidate_count)
    ordering = jnp.argsort(scores, axis=1, stable=True)[:, :keep_count]
    picked = jnp.take_along_axis(sources, ordering, axis=1)
    available = jnp.sum(usable.astype(jnp.int32), axis=1)
    wanted = jax.random.randint(count_key, (row_count,), 0, keep_count + 1)
    counts = jnp.minimum(jnp.minimum(wanted, limit), available)
    return (picked, counts)


def near_tables(key):
    base_key = jax.random.fold_in(key, 11)
    pick_key, dense_key = jax.random.split(base_key)
    offsets = jnp.concatenate([jnp.arange(-HALF, 0), jnp.arange(1, HALF + 1)])
    leaf_ids = jnp.arange(NL)
    sources = leaf_ids[:, None] + offsets[None, :]
    usable = (sources >= 0) & (sources < NL)
    density = jnp.repeat(jax.random.randint(dense_key, (DEVICES,), 1, NEAR + 1), LPD)
    picked, counts = choose(pick_key, sources, usable, density, NEAR)
    return (jnp.clip(picked, 0, NL - 1).astype(jnp.int32), counts.astype(jnp.int32))


def local_tables(key):
    base_key = jax.random.fold_in(key, 23)
    slot_count = 2 * LPD - 1
    node_rows = jnp.arange(DEVICES * slot_count)
    owner_device = node_rows // slot_count
    slot_index = node_rows % slot_count
    level_size = jnp.ones_like(node_rows)
    position = jnp.zeros_like(node_rows)
    for depth_level in range(LPD.bit_length()):
        node_count = LPD >> depth_level
        offset = 2 * LPD - 2 * node_count
        inside = (slot_index >= offset) & (slot_index < offset + node_count)
        level_size = jnp.where(inside, node_count, level_size)
        position = jnp.where(inside, slot_index - offset, position)
    reach_nodes = jnp.maximum(level_size // 2, 1)
    farthest = max(LPD // 2, 1)
    offsets = jnp.concatenate([jnp.arange(-farthest, 0), jnp.arange(1, farthest + 1)])
    global_index = owner_device * level_size + position
    sources = global_index[:, None] + offsets[None, :]
    level_end = DEVICES * level_size
    usable = (jnp.abs(offsets)[None, :] <= reach_nodes[:, None]) & (sources >= 0) & (sources < level_end[:, None])
    picked, counts = choose(base_key, sources, usable, NI, NI)
    picked = jnp.clip(picked, 0, (level_end - 1)[:, None])
    return (picked.astype(jnp.int32), counts.astype(jnp.int32))


def upper_tables(key):
    base_key = jax.random.fold_in(key, 37)
    heap_index = jnp.arange(DEVICES)
    top_levels = N_GROUP.bit_length() - 1
    depth_level = jnp.zeros_like(heap_index)
    for bit_power in range(1, DEVICES.bit_length() - 1):
        depth_level = depth_level + (heap_index >= 1 << bit_power).astype(depth_level.dtype)
    level_start = jnp.left_shift(1, depth_level)
    block_size = jnp.where(depth_level >= top_levels, jnp.left_shift(1, jnp.maximum(depth_level - top_levels, 0)), level_start)
    position = heap_index - level_start
    block_start = position // block_size * block_size
    widest = max(N_BULK // 2, NI)
    candidate = jnp.arange(widest)
    sources = level_start[:, None] + block_start[:, None] + candidate[None, :]
    usable = (candidate[None, :] < block_size[:, None]) & (sources != heap_index[:, None]) & (heap_index[:, None] >= 2)
    picked, counts = choose(base_key, sources, usable, NI, NI)
    last_available = jnp.sum(usable[DEVICES - 1].astype(jnp.int32))
    counts = counts.at[DEVICES - 1].set(jnp.minimum(last_available, NI))
    return (jnp.clip(picked, 0, DEVICES - 1).astype(jnp.int32), counts.astype(jnp.int32))


def draw_points(key, part):
    inside = jax.random.uniform(key, (3, NPTS), jnp.float32)
    upper_edge = float(max(4, NL // 1024))
    leaf_ids = jnp.arange(NPTS) // LEAF
    across = (leaf_ids % sheet_columns).astype(jnp.float32)
    along = (leaf_ids // sheet_columns).astype(jnp.float32)
    coord_x = sheet_scale * across + inside[0]
    coord_y = sheet_scale * along + inside[1]
    coord_z = sheet_depth * inside[2]
    return jnp.clip(jnp.stack([coord_x, coord_y, coord_z]), 0.0, upper_edge)


def draw_near_list(key, part):
    return near_tables(key)[0]


def draw_near_count(key, part):
    return near_tables(key)[1]


def draw_inter_list(key, part):
    return local_tables(key)[0]


def draw_inter_count(key, part):
    return local_tables(key)[1]


def draw_upper_list(key, part):
    return upper_tables(key)[0]


def draw_upper_count(key, part):
    return upper_tables(key)[1]


def block_scale(key, shape, pieces, smallest, largest):
    factor_of = 1.0
    for dim, blocks in pieces:
        draws = jax.random.uniform(jax.random.fold_in(jax.random.fold_in(key, 6), dim), (blocks,), jnp.float32, smallest / len(pieces), largest / len(pieces))
        factor_of = factor_of * jnp.repeat(jnp.exp(draws), shape[dim] // blocks).reshape((-1,) + (1,) * (len(shape) - 1 - dim))
    return factor_of


def gaussian(rng, dims, scale, reach, pieces=(), kind=jnp.bfloat16):
    factor_of = block_scale(rng, dims, pieces, -0.22, 0.18) if pieces else 1.0
    values = jax.random.normal(rng, dims, jnp.float32) * scale * factor_of
    return jnp.minimum(jnp.maximum(values, -reach), reach).astype(kind)


def setup_inputs(seed: int = 0) -> dict:
    streams_of = jax.random.split(jax.random.key(seed), 14)
    return {
        "right_sides": gaussian(streams_of[0], (RHS, NPTS), 1.0, 6.0, ((1, 256),), jnp.float32),
        "points": draw_points(jax.random.fold_in(streams_of[13], 71), 0),
        "basis": gaussian(streams_of[2], (NL, RANK, LEAF), LEAF ** -0.5, 0.375, ((0, 256),), jnp.float32),
        "transfer": gaussian(streams_of[3], (LNODES, RANK, RANK), (2 * RANK) ** -0.5, 0.5, ((0, 256),), jnp.float32),
        "skeleton": jnp.clip(2.0 * jax.random.uniform(streams_of[4], (LNODES, 3, RANK), jnp.float32) ** block_scale(streams_of[4], (LNODES, 3, RANK), ((0, 256),), -0.2, 0.2), 0.0, 2.0),
        "near_list": draw_near_list(jax.random.fold_in(streams_of[13], 71), 0),
        "near_count": draw_near_count(jax.random.fold_in(streams_of[13], 71), 0),
        "inter_list": draw_inter_list(jax.random.fold_in(streams_of[13], 71), 0),
        "inter_count": draw_inter_count(jax.random.fold_in(streams_of[13], 71), 0),
        "upper_transfer": gaussian(streams_of[9], (DEVICES, RANK, RANK), (2 * RANK) ** -0.5, 0.5, (), jnp.float32),
        "upper_skeleton": jnp.clip(jax.random.uniform(streams_of[10], (DEVICES, 3, RANK), jnp.float32, 0.0, 2.0), 0.0, 2.0),
        "upper_list": draw_upper_list(jax.random.fold_in(streams_of[13], 71), 0),
        "upper_count": draw_upper_count(jax.random.fold_in(streams_of[13], 71), 0),
    }


FULL_PRECISION = lax.Precision.HIGHEST
AMPLITUDE = 0.2
KERNEL_RATE = 2.0
SOFTENING = 0.01
NUGGET = 0.5

def matern(source_pts, target_pts):
    delta_x = source_pts[..., 0, :, None] - target_pts[..., 0, None, :]
    delta_y = source_pts[..., 1, :, None] - target_pts[..., 1, None, :]
    delta_z = source_pts[..., 2, :, None] - target_pts[..., 2, None, :]
    spread = jnp.sqrt(delta_x * delta_x + delta_y * delta_y + delta_z * delta_z + SOFTENING)
    scaled = KERNEL_RATE * spread
    return AMPLITUDE * (1.0 + scaled) * jnp.exp(-scaled)

def near_terms(own_points, own_rows, far_points, far_rows, weights):
    self_kernel = matern(own_points, own_points)
    result = jnp.einsum('brq,bqp->brp', own_rows, self_kernel, precision=FULL_PRECISION) + NUGGET * own_rows
    cross_kernel = matern(far_points, own_points[:, None])
    masked = far_rows * weights[:, :, None, None]
    return result + jnp.einsum('bnrq,bnqp->brp', masked, cross_kernel, precision=FULL_PRECISION)

def couple(skeleton_table, coef_table, positions, target_skeleton, counts):
    source_skeleton = jnp.take(skeleton_table, positions, axis=0)
    source_coefs = jnp.take(coef_table, positions, axis=0)
    kernel = matern(source_skeleton, target_skeleton[:, None])
    active = (jnp.arange(positions.shape[1])[None, :] < counts[:, None]).astype(jnp.float32)
    weighted = source_coefs * active[:, :, None, None]
    return jnp.einsum('nsri,nsij->nrj', weighted, kernel, precision=FULL_PRECISION)

def reference(right_sides, points, basis, transfer, skeleton, near_list, near_count, inter_list, inter_count, upper_transfer, upper_skeleton, upper_list, upper_count):
    points_leaf = points.reshape(3, NL, LEAF).transpose(1, 0, 2)
    rows_leaf = right_sides.reshape(RHS, NL, LEAF).transpose(1, 0, 2)
    weights = (jnp.arange(NEAR)[None, :] < near_count[:, None]).astype(jnp.float32)

    def near_block(first_leaf):
        own_points = lax.dynamic_slice_in_dim(points_leaf, first_leaf, LPD, 0)
        own_rows = lax.dynamic_slice_in_dim(rows_leaf, first_leaf, LPD, 0)
        source_ids = lax.dynamic_slice_in_dim(near_list, first_leaf, LPD, 0)
        block_weights = lax.dynamic_slice_in_dim(weights, first_leaf, LPD, 0)
        return near_terms(own_points, own_rows, jnp.take(points_leaf, source_ids, axis=0), jnp.take(rows_leaf, source_ids, axis=0), block_weights)
    near_part = lax.map(near_block, jnp.arange(0, NL, LPD, dtype=jnp.int32)).reshape(NL, RHS, LEAF)
    slot_count = 2 * LPD - 1
    transfer_dev = transfer.reshape(DEVICES, slot_count, RANK, RANK)
    skeleton_dev = skeleton.reshape(DEVICES, slot_count, 3, RANK)
    list_dev = inter_list.reshape(DEVICES, slot_count, NI)
    count_dev = inter_count.reshape(DEVICES, slot_count)
    level_total = LPD.bit_length()

    def level_portion(values, level_index):
        node_count = LPD >> level_index
        offset = 2 * LPD - 2 * node_count
        portion = values[:, offset:offset + node_count]
        return portion.reshape((DEVICES * node_count,) + portion.shape[2:])
    coefficients = [jnp.einsum('lrp,lkp->lrk', rows_leaf, basis, precision=FULL_PRECISION)]
    for level_index in range(level_total - 1):
        lifted = jnp.einsum('nrk,nkq->nrq', coefficients[-1], level_portion(transfer_dev, level_index), precision=FULL_PRECISION)
        coefficients.append(lifted.reshape(-1, 2, RHS, RANK).sum(axis=1))
    root_transfer = transfer_dev[:, slot_count - 1]
    root_terms = jnp.einsum('nrk,nkq->nrq', coefficients[-1], root_transfer, precision=FULL_PRECISION)
    local_fields = []
    for level_index in range(level_total):
        skeleton_here = level_portion(skeleton_dev, level_index)
        local_fields.append(couple(skeleton_here, coefficients[level_index], level_portion(list_dev, level_index), skeleton_here, level_portion(count_dev, level_index)))
    tree_depth = DEVICES.bit_length() - 1
    level_coef = root_terms.reshape(-1, 2, RHS, RANK).sum(axis=1)
    heap_parts = []
    for level_index in range(tree_depth - 1, 0, -1):
        heap_parts.insert(0, level_coef)
        if level_index > 1:
            lifted = jnp.einsum('nrk,nkq->nrq', level_coef, upper_transfer[1 << level_index:2 << level_index], precision=FULL_PRECISION)
            level_coef = lifted.reshape(-1, 2, RHS, RANK).sum(axis=1)
    heap_coefs = jnp.concatenate([jnp.zeros((2, RHS, RANK), jnp.float32)] + heap_parts, axis=0)
    upper_fields = couple(upper_skeleton, heap_coefs, upper_list, upper_skeleton, upper_count)
    downward = upper_fields[2:4]
    for level_index in range(2, tree_depth):
        parent = jnp.repeat(downward, 2, axis=0)
        downward = upper_fields[1 << level_index:2 << level_index] + jnp.einsum('nrq,nkq->nrk', parent, upper_transfer[1 << level_index:2 << level_index], precision=FULL_PRECISION)
    incoming = jnp.einsum('nrq,nkq->nrk', jnp.repeat(downward, 2, axis=0), root_transfer, precision=FULL_PRECISION)
    local_fields[-1] = local_fields[-1] + incoming
    for level_index in range(level_total - 2, -1, -1):
        parent = jnp.repeat(local_fields[level_index + 1], 2, axis=0)
        local_fields[level_index] = local_fields[level_index] + jnp.einsum('nrq,nkq->nrk', parent, level_portion(transfer_dev, level_index), precision=FULL_PRECISION)
    far_part = jnp.einsum('lrk,lkp->rlp', local_fields[0], basis, precision=FULL_PRECISION)
    combined = far_part + near_part.transpose(1, 0, 2)
    return combined.reshape(RHS, NPTS)
```

```python
import functools
import math

import jax
import jax.numpy as jnp
from jax import lax
from jax.experimental import pallas as pl
from jax.experimental.pallas import tpu as pltpu
from jax.sharding import PartitionSpec as P

F32 = jnp.float32
BF16 = jnp.bfloat16
MESH = pl.DeviceIdType.MESH
NN = (((1,), (0,)), ((), ()))
NT = (((1,), (1,)), ((), ()))

ALPHA = 2.0 / math.log(2.0)
KAPPA = 0.2 * math.log(2.0)
SHIFT = 1.0 / math.log(2.0)
SOFT = 0.01 * ALPHA * ALPHA
CENTER = 2.0
NUGGET = 0.5
FEATS = 48
UPPER = (32, 16, 8, 4, 2, 4, 2)
UPPER_AT = (0, 32, 48, 56, 60, 62, 66)


def dot(a, b, dims=NN):
    return lax.dot_general(a, b, dims, preferred_element_type=F32)


def halves(x):
    high = x.astype(BF16)
    return high, (x - high.astype(F32)).astype(BF16)


def matmul(a, high, low, dims=NN):
    m = a.shape[0]
    a_high, a_low = halves(a)
    both = dot(jnp.concatenate([a_high, a_low], axis=0), high, dims)
    return both[:m] + both[m:] + dot(a_high, low, dims)


def kern(w):
    y = w * lax.rsqrt(w)
    return halves((SHIFT + y) * jnp.exp2(-y))


def in_three(x):
    one = x.astype(BF16).astype(F32)
    rest = x - one
    two = rest.astype(BF16).astype(F32)
    return one, two, (rest - two).astype(BF16).astype(F32)


def scaled(x):
    return ALPHA * (x - CENTER)


def features(u, sides="st"):
    row = lax.broadcasted_iota(jnp.int32, u.shape, 0)
    square = jnp.sum(u * u, axis=0, keepdims=True)
    out = []
    if "s" in sides:
        s = jnp.where(row < 3, -2.0 * u, jnp.where(row == 3, square, jnp.where(row == 4, 1.0, 0.0)))
        a, b, c = in_three(s)
        out.append(jnp.concatenate([a, a, b, b, a, c], axis=0))
    if "t" in sides:
        t = jnp.where(row < 3, u, jnp.where(row == 3, 1.0, jnp.where(row == 4, square + SOFT, 0.0)))
        a, b, c = in_three(t)
        out.append(jnp.concatenate([a, b, a, b, c, a], axis=0).astype(BF16))
    return out


def as_rows(f):
    return f.T.astype(BF16)


def usable(values, counts):
    slot = lax.broadcasted_iota(jnp.int32, values.shape, 1)
    return jnp.where(slot < counts, values, -1000)


def counted(ref, rows, width):
    row = lax.broadcasted_iota(jnp.int32, (rows, width), 0)
    out = jnp.zeros((rows, width), jnp.int32)
    for t in range(rows):
        out = jnp.where(row == t, ref[t], out)
    return out


def mask(lists, ids):
    out = jnp.zeros((lists.shape[0], ids.shape[1]), F32)
    for i in range(lists.shape[1]):
        out += jnp.where(lists[:, i : i + 1] == ids, 1.0, 0.0)
    return out


def lanes(n):
    return lax.broadcasted_iota(jnp.int32, (1, n), 1)


def low_lanes(rows):
    return lax.broadcasted_iota(jnp.int32, (rows, 128), 1) < 64


def couple(rows, feats, coefs, masks):
    kh, kl = kern(dot(rows, feats))
    weighted = [coefs * (m * KAPPA) for m in masks]
    weighted = weighted[0] if len(weighted) == 1 else jnp.concatenate(weighted, axis=0)
    return matmul(weighted, kh, kl, NT)


def beside(pair):
    return jnp.where(low_lanes(32), pair[:32], pair[32:])


def kernel(
    rs, pts, basis, transfer, skel, near_list, near_count, inter_list, inter_count,
    up_t, up_s, up_list, up_count, out,
    xe, acc, f, ft, t1, t2, bb_h, bb_l, bl_h, bl_l, bu_h, bu_l,
    ce, lh, rh, ftl, eu, us, su, fu, tu, zbuf, gc, tc, qh, ql,
    in_sem, near_send, near_recv, coef_send, coef_recv, z_send, z_recv, y_send, y_recv, x_send, x_recv,
):
    g = lax.axis_index("group")
    b = lax.axis_index("bulk")
    z = lax.rem(lax.div(b, 2), 8)
    y = lax.div(b, 16)
    r = lax.rem(b, 16)
    dev = g * 64 + b

    def at(d):
        d = lax.rem(d + 256, 256)
        return (lax.div(d, 64), lax.rem(d, 64))

    right, left = at(dev + 1), at(dev - 1)

    loads = [pltpu.make_async_copy(rs, xe.at[0:32, 1024:3072], in_sem.at[0])]
    spans = (
        (128 + 32 * g + 8 * y, 8, 0),
        (64 + 16 * g + 4 * y, 4, 8),
        (32 + 8 * g + 2 * y, 2, 12),
        (16 + 4 * g, 4, 14),
        (8 + 2 * g, 2, 18),
        (4, 4, 20),
    )
    for i, (first, n, to) in enumerate(spans):
        loads.append(pltpu.make_async_copy(up_t.at[pl.ds(first, n)], eu.at[to : to + n], in_sem.at[1 + i]))
    firsts = (128 + 32 * g, 64 + 16 * g, 32 + 8 * g, 16 + 4 * g, 8 + 2 * g, 4, 2)
    for i, (first, n, to) in enumerate(zip(firsts, UPPER, UPPER_AT)):
        loads.append(pltpu.make_async_copy(up_s.at[pl.ds(first, n)], us.at[to : to + n], in_sem.at[7 + i]))
    for load in loads:
        load.start()

    barrier = pltpu.get_barrier_semaphore()

    def greet(device):
        pl.semaphore_signal(barrier, inc=1, device_id=device, device_id_type=MESH)

    greet(right)
    greet(left)

    def greet_row(k, _):
        greet((g, y * 16 + lax.rem(r + k, 16)))
        return 0

    lax.fori_loop(1, 16, greet_row, 0)
    for k in range(1, 4):
        greet((g, lax.rem(y + k, 4) * 16 + r))
        greet((lax.rem(g + k, 4), b))

    xe[32:40, 1024:3072] = jnp.zeros((8, 2048), F32)
    xe[32:35, 1024:3072] = scaled(pts[...])
    ce[32:40, :] = jnp.zeros((8, 1024), F32)
    order = ((0, 1), (2, 3), (8, 9), (12, 13), (14, 14), (10, 11), (4, 5), (6, 7))
    for i, (m, n) in enumerate(order):
        ce[32:35, i * 128 : i * 128 + 128] = scaled(jnp.concatenate([skel[m], skel[n]], axis=1))
    loads[0].wait()
    pl.semaphore_wait(barrier, 23)

    near_copies = [
        pltpu.make_async_remote_copy(
            xe.at[:, 2048:3072], xe.at[:, 0:1024], near_send.at[0], near_recv.at[0],
            device_id=right, device_id_type=MESH,
        ),
        pltpu.make_async_remote_copy(
            xe.at[:, 1024:2048], xe.at[:, 3072:4096], near_send.at[1], near_recv.at[1],
            device_id=left, device_id_type=MESH,
        ),
    ]
    for copy in near_copies:
        copy.start()

    bb_h[...], bb_l[...] = halves(basis[...])
    low128 = low_lanes(128)

    def put(to_h, to_l, at_row, value):
        n = value.shape[0]
        to_h[at_row : at_row + n, :], to_l[at_row : at_row + n, :] = halves(value)

    def twice(e):
        return jnp.concatenate([e, e], axis=1)

    for q in range(3):
        for h in range(2):
            e = twice(transfer[q * 256 + h * 128 : q * 256 + h * 128 + 128, :])
            keep = low128 if h == 0 else jnp.logical_not(low128)
            put(bl_h, bl_l, q * 256 + h * 128, jnp.where(keep, e, 0.0))
    put(bl_h, bl_l, 768, twice(transfer[768:896, :]))
    root_e = transfer[896:960, :]
    put(bl_h, bl_l, 896, twice(root_e))

    leaf = []
    for j in range(4):
        two = jnp.concatenate(
            [xe[0:32, 1024 + 512 * j : 1280 + 512 * j], xe[0:32, 1280 + 512 * j : 1536 + 512 * j]], axis=0
        )
        leaf.append(beside(matmul(two, bb_h[128 * j : 128 * j + 128, :], bb_l[128 * j : 128 * j + 128, :], NT)))

    def lift(values, h, low, first):
        joined = values[0] if len(values) == 1 else jnp.concatenate(values, axis=1)
        n = joined.shape[1]
        return matmul(joined, h[first : first + n, :], low[first : first + n, :])

    mid_a = lift(leaf[0:2], bl_h, bl_l, 0)
    mid_b = lift(leaf[2:4], bl_h, bl_l, 256)
    top = lift([mid_a, mid_b], bl_h, bl_l, 512)
    root = lift([top], bl_h, bl_l, 768)
    term = lift([root[:, 0:64]], bl_h, bl_l, 896)
    zbuf[r] = jnp.where(low_lanes(16), term[0:16], term[16:32])

    def row_copy(k, sender):
        to = lax.rem(r + k, 16)
        slot = r if sender else to
        return pltpu.make_async_remote_copy(
            zbuf.at[slot], zbuf.at[slot], z_send.at[k], z_recv.at[slot],
            device_id=(g, y * 16 + to), device_id_type=MESH,
        )

    def send_row(k, _):
        row_copy(k, True).start()
        return 0

    lax.fori_loop(1, 16, send_row, 0)
    for i, value in enumerate((leaf[0], leaf[1], mid_a, top, root, mid_b, leaf[2], leaf[3])):
        ce[0:32, i * 128 : i * 128 + 128] = value
    coef_copies = [
        pltpu.make_async_remote_copy(
            ce.at[:, 384:1024], lh, coef_send.at[0], coef_recv.at[0], device_id=right, device_id_type=MESH
        ),
        pltpu.make_async_remote_copy(
            ce.at[:, 0:640], rh, coef_send.at[1], coef_recv.at[1], device_id=left, device_id_type=MESH
        ),
    ]
    for copy in coef_copies:
        copy.start()

    near = usable(near_list[...], counted(near_count, 8, 8))
    t2[...] = mask(near, lanes(4096) // 256 + (dev * 8 - 4)) * KAPPA
    ext = lax.broadcasted_iota(jnp.int32, (16, 8), 0)
    ext_row = lax.broadcasted_iota(jnp.int32, (16, 1), 0)
    for t in range(8):
        found = jnp.where(near[t : t + 1, :] == ext + (dev * 8 - 4), 1.0, 0.0)
        column = jnp.sum(found, axis=1, keepdims=True) + jnp.where(ext_row == t + 4, 1.0, 0.0)
        t1[:, t * 256 : t * 256 + 256] = jnp.broadcast_to(column * KAPPA, (16, 256))
    t1[:, 2048:3072] = jnp.zeros((16, 1024), F32)
    acc[:, 0:2048] = NUGGET * xe[0:32, 1024:3072]
    acc[:, 2048:3072] = jnp.zeros((32, 1024), F32)
    src, tgt = features(xe[32:40, 1024:3072])
    f[:, 1024:3072] = tgt
    ft[1024:3072, :] = as_rows(src)

    def near_block(i, _):
        here = pl.multiple_of(i * 256, 256)
        x_high, x_low = halves(xe[0:32, pl.ds(here + 1024, 256)])
        x_both = jnp.concatenate([x_high, x_low], axis=0)
        m_high, m_low = halves(xe[0:32, pl.ds(here + 1280, 1024)] * t2[pl.ds(i, 1), pl.ds(here + 1280, 1024)])
        m_both = jnp.concatenate([m_high, m_low], axis=0)
        rows = ft[pl.ds(here + 1024, 256), :]
        own = jnp.zeros((32, 256), F32)
        for j in range(5):
            kh, kl = kern(dot(rows, f[:, pl.ds(here + 1024 + j * 256, 256)]))
            both = dot(x_both, kh)
            to_them = both[:32] + both[32:] + dot(x_high, kl)
            there = pl.ds(here + j * 256, 256)
            acc[:, there] += to_them * t1[pl.ds(i + 4, 1), there]
            if j > 0:
                part = slice((j - 1) * 256, j * 256)
                both = dot(m_both[:, part], kh, NT)
                own += both[:32] + both[32:] + dot(m_high[:, part], kl, NT)
        acc[:, pl.ds(here, 256)] += own
        return 0

    lax.fori_loop(0, 4, near_block, 0)

    for load in loads[1:]:
        load.wait()

    def stacked(first, n):
        return eu[first : first + n].reshape(n * 64, 64)

    for first, to in ((0, 0), (4, 256), (8, 512), (14, 896), (20, 1280)):
        for h in range(2):
            keep = low128 if h == 0 else jnp.logical_not(low128)
            put(bu_h, bu_l, to + h * 128, jnp.where(keep, twice(stacked(first + 2 * h, 2)), 0.0))
    put(bu_h, bu_l, 768, twice(stacked(12, 2)))
    put(bu_h, bu_l, 1152, twice(stacked(18, 2)))
    su[...] = jnp.zeros((8, 4352), F32)
    for i in range(34):
        su[0:3, i * 128 : i * 128 + 128] = scaled(jnp.concatenate([us[2 * i], us[2 * i + 1]], axis=1))
    fu[...] = features(su[...], "t")[0]
    places = (y * 8 + z, 32 + 4 * y + lax.div(z, 2), 48 + 2 * y + lax.div(z, 4), 56 + y, 60 + lax.div(y, 2), 62 + g, 66 + lax.div(g, 2))
    picked = jnp.concatenate(
        [jnp.concatenate([us[places[m]], us[places[n]]], axis=1) for m, n in ((0, 1), (2, 3), (4, 5), (6, 6))], axis=1
    )
    tu[...] = jnp.zeros((8, 512), F32)
    tu[0:3, :] = scaled(picked)
    ftu = as_rows(features(tu[...], "s")[0])

    def take_row(k, _):
        row_copy(k, False).wait_recv()
        return 0

    lax.fori_loop(1, 16, take_row, 0)
    low16 = low_lanes(16)
    level7 = []
    for j in range(4):
        one = zbuf[4 * j] + zbuf[4 * j + 1]
        two = zbuf[4 * j + 2] + zbuf[4 * j + 3]
        level7.append(
            jnp.concatenate(
                [jnp.where(low16, one, pltpu.roll(two, 64, 1)), jnp.where(low16, pltpu.roll(one, 64, 1), two)], axis=0
            )
        )
    level6 = [lift(level7[0:2], bu_h, bu_l, 0), lift(level7[2:4], bu_h, bu_l, 256)]
    level5 = lift(level6, bu_h, bu_l, 512)
    level4 = lift([level5], bu_h, bu_l, 768)
    for i, value in enumerate((*level7, *level6, level5, level4)):
        gc[y, :, i * 128 : i * 128 + 128] = value

    def plane_copy(k, sender):
        to = lax.rem(y + k, 4)
        slot = y if sender else to
        return pltpu.make_async_remote_copy(
            gc.at[slot], gc.at[slot], y_send.at[k], y_recv.at[slot], device_id=(g, to * 16 + r), device_id_type=MESH
        )

    for k in range(1, 4):
        plane_copy(k, True).start()

    for copy in near_copies:
        copy.wait_recv()
    src, tgt = features(xe[32:40, 0:1024])
    ft[0:1024, :] = as_rows(src)
    src, tgt = features(xe[32:40, 3072:4096])
    f[:, 3072:4096] = tgt
    lax.fori_loop(4, 8, near_block, 0)

    for k in range(1, 4):
        plane_copy(k, False).wait_recv()
    low32 = low_lanes(32)
    level4 = [
        jnp.where(low32, gc[0, :, 896:1024], gc[1, :, 896:1024]),
        jnp.where(low32, gc[2, :, 896:1024], gc[3, :, 896:1024]),
    ]
    level3 = lift(level4, bu_h, bu_l, 896)
    tc[g] = lift([level3], bu_h, bu_l, 1152)

    def group_copy(k, sender):
        to = lax.rem(g + k, 4)
        slot = g if sender else to
        return pltpu.make_async_remote_copy(
            tc.at[slot], tc.at[slot], x_send.at[k], x_recv.at[slot], device_id=(to, b), device_id_type=MESH
        )

    for k in range(1, 4):
        group_copy(k, True).start()

    for e in range(4):
        x_high, x_low = halves(xe[0:32, e * 256 : e * 256 + 256])
        x_both = jnp.concatenate([x_high, x_low], axis=0)
        for t in range(e + 1):
            kh, kl = kern(dot(ft[e * 256 : e * 256 + 256, :], f[:, 1024 + t * 256 : 1280 + t * 256]))
            both = dot(x_both, kh)
            there = slice(t * 256, t * 256 + 256)
            acc[:, there] += (both[:32] + both[32:] + dot(x_high, kl)) * t1[e : e + 1, there]

    for copy in coef_copies:
        copy.wait_recv()
    ftl[...] = as_rows(features(ce[32:40, :], "s")[0])
    inter = usable(inter_list[...], counted(inter_count, 15, 8))
    table = jnp.concatenate([lh[:, 384:640], ce[:, 0:256], ce[:, 768:1024], rh[:, 0:256]], axis=1)
    feats = features(table[32:40], "t")[0]
    found = mask(inter[0:8], lanes(1024) // 64 + (dev * 8 - 4))
    field0 = []
    for j, at_lane in enumerate((0, 128, 768, 896)):
        part = slice(j * 128, j * 128 + 640)
        masks = [found[2 * j : 2 * j + 1, part], found[2 * j + 1 : 2 * j + 2, part]]
        field0.append(beside(couple(ftl[at_lane : at_lane + 128, :], feats[:, part], table[0:32, part], masks)))
    table = jnp.concatenate([lh[:, 256:384], ce[:, 256:384], ce[:, 640:768], rh[:, 256:384]], axis=1)
    feats = features(table[32:40], "t")[0]
    found = mask(inter[8:12], lanes(512) // 64 + (dev * 4 - 2))
    field1 = []
    for j, at_lane in enumerate((256, 640)):
        part = slice(j * 128, j * 128 + 384)
        masks = [found[2 * j : 2 * j + 1, part], found[2 * j + 1 : 2 * j + 2, part]]
        field1.append(beside(couple(ftl[at_lane : at_lane + 128, :], feats[:, part], table[0:32, part], masks)))
    table = jnp.concatenate([lh[:, 0:128], ce[:, 384:512], rh[:, 384:512]], axis=1)
    feats = features(table[32:40], "t")[0]
    found = mask(inter[12:14], lanes(384) // 64 + (dev * 2 - 2))
    field2 = beside(couple(ftl[384:512, :], feats, table[0:32], [found[0:1], found[1:2]]))
    table = jnp.concatenate([lh[:, 128:256], ce[:, 512:640], rh[:, 512:640]], axis=1)
    feats = features(table[32:40], "t")[0]
    spot = lanes(384)
    ids = jnp.where(lax.rem(spot, 128) < 64, spot // 128 + (dev - 1), -1)
    found = mask(inter[14:15], ids)
    field3 = beside(couple(ftl[512:640, :], feats, table[0:32], [found, found]))

    path = (z, 8 + lax.div(z, 2), 12 + lax.div(z, 4), 14 + y, 18 + lax.div(y, 2), 20 + g)
    product = jnp.concatenate([root_e, root_e], axis=0)
    for i in range(7):
        if i > 0:
            product = matmul(product, *halves(eu[path[i - 1]]))
        qh[i], ql[i] = halves(product)

    def path_field(i, coefs):
        h = firsts[i] + places[i] - UPPER_AT[i]
        first, n = UPPER_AT[i] * 64, UPPER[i] * 64
        listed = usable(up_list[pl.ds(h, 1), :], up_count[h])
        found = mask(listed, lanes(n) // 64 + firsts[i])
        field = couple(ftu[i * 64 : i * 64 + 64, :], fu[:, first : first + n], coefs, [found])
        return matmul(field, qh[i], ql[i], NT)

    incoming = path_field(0, jnp.concatenate([gc[k, :, 0:512] for k in range(4)], axis=1))
    incoming += path_field(1, jnp.concatenate([gc[k, :, 512:768] for k in range(4)], axis=1))
    incoming += path_field(2, jnp.concatenate([gc[k, :, 768:896] for k in range(4)], axis=1))
    incoming += path_field(3, jnp.concatenate(level4, axis=1))
    incoming += path_field(4, level3)
    for k in range(1, 4):
        group_copy(k, False).wait_recv()
    level2 = [jnp.where(low32, tc[0], tc[1]), jnp.where(low32, tc[2], tc[3])]
    incoming += path_field(5, jnp.concatenate(level2, axis=1))
    incoming += path_field(6, lift(level2, bu_h, bu_l, 1280))

    def lower(value, first, n):
        return matmul(value, bl_h[first : first + n, :], bl_l[first : first + n, :], NT)

    down3 = jnp.where(low32, field3 + incoming, 0.0)
    down2 = field2 + lower(down3, 768, 128)
    down1 = lower(down2, 512, 256)
    down1 = [field1[0] + down1[:, 0:128], field1[1] + down1[:, 128:256]]
    for q in range(2):
        down0 = lower(down1[q], q * 256, 256)
        for h in range(2):
            j = 2 * q + h
            pair = field0[j] + down0[:, h * 128 : h * 128 + 128]
            two = jnp.concatenate([jnp.where(low32, pair, 0.0), jnp.where(low32, 0.0, pair)], axis=0)
            far = matmul(two, bb_h[128 * j : 128 * j + 128, :], bb_l[128 * j : 128 * j + 128, :])
            for k in range(2):
                part = slice((2 * j + k) * 256, (2 * j + k) * 256 + 256)
                out[:, part] = acc[:, part] + far[32 * k : 32 * k + 32]

    for copy in near_copies + coef_copies:
        copy.wait_send()

    def sent_row(k, _):
        row_copy(k, True).wait_send()
        return 0

    lax.fori_loop(1, 16, sent_row, 0)
    for k in range(1, 4):
        plane_copy(k, True).wait_send()
        group_copy(k, True).wait_send()


def on_device(
    rs, pts, basis, transfer, skel, near_list, near_count, inter_list, inter_count, up_t, up_s, up_list, up_count
):
    vmem = pl.BlockSpec(memory_space=pltpu.VMEM)
    smem = pl.BlockSpec(memory_space=pltpu.SMEM)
    anywhere = pl.BlockSpec(memory_space=pl.ANY)
    dma = pltpu.SemaphoreType.DMA
    return pl.pallas_call(
        kernel,
        out_shape=jax.ShapeDtypeStruct((32, 2048), F32),
        in_specs=[anywhere, vmem, vmem, vmem, vmem, vmem, smem, vmem, smem, anywhere, anywhere, vmem, smem],
        out_specs=vmem,
        scratch_shapes=[
            pltpu.VMEM((40, 4096), F32),
            pltpu.VMEM((32, 3072), F32),
            pltpu.VMEM((FEATS, 4096), BF16),
            pltpu.VMEM((3072, FEATS), BF16),
            pltpu.VMEM((16, 3072), F32),
            pltpu.VMEM((8, 4096), F32),
            pltpu.VMEM((512, 256), BF16),
            pltpu.VMEM((512, 256), BF16),
            pltpu.VMEM((960, 128), BF16),
            pltpu.VMEM((960, 128), BF16),
            pltpu.VMEM((1536, 128), BF16),
            pltpu.VMEM((1536, 128), BF16),
            pltpu.VMEM((40, 1024), F32),
            pltpu.VMEM((40, 640), F32),
            pltpu.VMEM((40, 640), F32),
            pltpu.VMEM((1024, FEATS), BF16),
            pltpu.VMEM((24, 64, 64), F32),
            pltpu.VMEM((68, 3, 64), F32),
            pltpu.VMEM((8, 4352), F32),
            pltpu.VMEM((FEATS, 4352), BF16),
            pltpu.VMEM((8, 512), F32),
            pltpu.VMEM((16, 16, 128), F32),
            pltpu.VMEM((4, 32, 1024), F32),
            pltpu.VMEM((4, 32, 128), F32),
            pltpu.VMEM((7, 128, 64), BF16),
            pltpu.VMEM((7, 128, 64), BF16),
            dma((14,)),
            dma((2,)), dma((2,)), dma((2,)), dma((2,)),
            dma((16,)), dma((16,)), dma((4,)), dma((4,)), dma((4,)), dma((4,)),
        ],
        compiler_params=pltpu.CompilerParams(
            collective_id=0, has_side_effects=True, vmem_limit_bytes=48 * 2**20
        ),
    )(
        rs, pts, basis.reshape(512, 256), transfer.reshape(960, 64), skel, near_list, near_count, inter_list,
        inter_count, up_t, up_s, up_list, up_count,
    )


def solution(mesh):
    both = ("group", "bulk")
    in_specs = (
        P(None, both),
        P(None, both),
        P(both, None, None),
        P(both, None, None),
        P(both, None, None),
        P(both, None),
        P(both),
        P(both, None),
        P(both),
        P(),
        P(),
        P(),
        P(),
    )
    return jax.shard_map(
        on_device, mesh=mesh, in_specs=in_specs, out_specs=P(None, both), check_vma=False
    )
```

```python
import functools
import math

import jax
import jax.numpy as jnp
from jax import lax
from jax.experimental import pallas as pl
from jax.experimental.pallas import tpu as pltpu
from jax.sharding import PartitionSpec as P

F32 = jnp.float32
BF16 = jnp.bfloat16
MESH = pl.DeviceIdType.MESH
NN = (((1,), (0,)), ((), ()))
NT = (((1,), (1,)), ((), ()))

ALPHA = 2.0 / math.log(2.0)
KAPPA = 0.2 * math.log(2.0)
SHIFT = 1.0 / math.log(2.0)
SOFT = 0.01 * ALPHA * ALPHA
CENTER = 2.0
NUGGET = 0.5
FEATS = 48
UPPER = (32, 16, 8, 4, 2, 4, 2)


def dot(a, b, dims=NN):
    return lax.dot_general(a, b, dims, preferred_element_type=F32)


def halves(x):
    high = x.astype(BF16)
    return high, (x - high.astype(F32)).astype(BF16)


def matmul(a, high, low, dims=NN):
    m = a.shape[0]
    a_high, a_low = halves(a)
    both = dot(jnp.concatenate([a_high, a_low], axis=0), high, dims)
    return both[:m] + both[m:] + dot(a_high, low, dims)


def kern(w):
    y = w * lax.rsqrt(w)
    return halves((SHIFT + y) * jnp.exp2(-y))


def in_three(x):
    one = x.astype(BF16).astype(F32)
    rest = x - one
    two = rest.astype(BF16).astype(F32)
    return one, two, (rest - two).astype(BF16).astype(F32)


def scaled(x):
    return ALPHA * (x - CENTER)


def features(u, sides="st"):
    row = lax.broadcasted_iota(jnp.int32, u.shape, 0)
    square = jnp.sum(u * u, axis=0, keepdims=True)
    out = []
    if "s" in sides:
        s = jnp.where(row < 3, -2.0 * u, jnp.where(row == 3, square, jnp.where(row == 4, 1.0, 0.0)))
        a, b, c = in_three(s)
        out.append(jnp.concatenate([a, a, b, b, a, c], axis=0))
    if "t" in sides:
        t = jnp.where(row < 3, u, jnp.where(row == 3, 1.0, jnp.where(row == 4, square + SOFT, 0.0)))
        a, b, c = in_three(t)
        out.append(jnp.concatenate([a, b, a, b, c, a], axis=0).astype(BF16))
    return out


def as_rows(f):
    return f.T.astype(BF16)


def usable(values, counts):
    slot = lax.broadcasted_iota(jnp.int32, values.shape, 1)
    return jnp.where(slot < counts, values, -1000)


def counted(ref, rows, width):
    row = lax.broadcasted_iota(jnp.int32, (rows, width), 0)
    out = jnp.zeros((rows, width), jnp.int32)
    for t in range(rows):
        out = jnp.where(row == t, ref[t], out)
    return out


def mask(lists, ids):
    out = jnp.zeros((lists.shape[0], ids.shape[1]), F32)
    for i in range(lists.shape[1]):
        out += jnp.where(lists[:, i : i + 1] == ids, 1.0, 0.0)
    return out


def lanes(n):
    return lax.broadcasted_iota(jnp.int32, (1, n), 1)


def low_lanes(rows):
    return lax.broadcasted_iota(jnp.int32, (rows, 128), 1) < 64


def couple(rows, feats, coefs, masks):
    kh, kl = kern(dot(rows, feats))
    weighted = [coefs * (m * KAPPA) for m in masks]
    weighted = weighted[0] if len(weighted) == 1 else jnp.concatenate(weighted, axis=0)
    return matmul(weighted, kh, kl, NT)


def beside(pair):
    return jnp.where(low_lanes(32), pair[:32], pair[32:])


def kernel(
    rs, pts_in, basis_in, transfer_in, skel_in, near_list_in, near_count_in, inter_list_in, inter_count_in,
    up_t, up_s, up_list_in, up_count_in, out,
    xe, acc, f, ft, t2, bb_h, bb_l, bl_h, bl_l, bu_h, bu_l,
    ce, lh, rh, ftl, ev, et, sv, st, su, fu, tu, zbuf, gc, tc, qh, ql,
    pts, basis, transfer, skel, near_list, near_count, inter_list, inter_count, up_list, up_count,
    in_sem, near_send, near_recv, coef_send, coef_recv, z_send, z_recv, y_send, y_recv, x_send, x_recv,
):
    g = lax.axis_index("group")
    b = lax.axis_index("bulk")
    z = lax.rem(lax.div(b, 2), 8)
    y = lax.div(b, 16)
    r = lax.rem(b, 16)
    dev = g * 64 + b

    def at(d):
        d = lax.rem(d + 256, 256)
        return (lax.div(d, 64), lax.rem(d, 64))

    right, left = at(dev + 1), at(dev - 1)

    pairs = (
        (rs, xe.at[0:32, 1024:3072]),
        (pts_in, pts),
        (skel_in, skel),
        (basis_in, basis),
        (transfer_in, transfer),
        (near_list_in, near_list),
        (near_count_in, near_count),
        (inter_list_in, inter_list),
        (inter_count_in, inter_count),
        (up_list_in, up_list),
        (up_count_in, up_count),
        (up_s, sv),
        (up_t.at[:, 128:256], ev.at[0:4096]),
        (up_t.at[:, 0:128], ev.at[4096:8192]),
    )
    loads = [pltpu.make_async_copy(of, to, in_sem.at[i]) for i, (of, to) in enumerate(pairs)]
    for load in loads:
        load.start()
    firsts = (128 + 32 * g, 64 + 16 * g, 32 + 8 * g, 16 + 4 * g, 8 + 2 * g, 4, 2)

    barrier = pltpu.get_barrier_semaphore()

    def greet(device):
        pl.semaphore_signal(barrier, inc=1, device_id=device, device_id_type=MESH)

    greet(right)
    greet(left)

    def greet_row(k, _):
        greet((g, y * 16 + lax.rem(r + k, 16)))
        return 0

    lax.fori_loop(1, 16, greet_row, 0)
    for k in range(1, 4):
        greet((g, lax.rem(y + k, 4) * 16 + r))
        greet((lax.rem(g + k, 4), b))

    xe[32:40, 1024:3072] = jnp.zeros((8, 2048), F32)
    loads[1].wait()
    loads[2].wait()
    xe[32:35, 1024:3072] = scaled(pts[...])
    ce[32:40, :] = jnp.zeros((8, 1024), F32)
    order = ((0, 1), (2, 3), (8, 9), (12, 13), (14, 14), (10, 11), (4, 5), (6, 7))
    for i, (m, n) in enumerate(order):
        ce[32:35, i * 128 : i * 128 + 128] = scaled(jnp.concatenate([skel[:, m, :], skel[:, n, :]], axis=1))
    loads[0].wait()
    pl.semaphore_wait(barrier, 23)

    near_copies = [
        pltpu.make_async_remote_copy(
            xe.at[:, 2048:3072], xe.at[:, 0:1024], near_send.at[0], near_recv.at[0],
            device_id=right, device_id_type=MESH,
        ),
        pltpu.make_async_remote_copy(
            xe.at[:, 1024:2048], xe.at[:, 3072:4096], near_send.at[1], near_recv.at[1],
            device_id=left, device_id_type=MESH,
        ),
    ]
    for copy in near_copies:
        copy.start()

    loads[3].wait()
    loads[4].wait()
    bb_h[...], bb_l[...] = halves(basis[...])
    low128 = low_lanes(128)

    def put(to_h, to_l, at_row, value):
        n = value.shape[0]
        to_h[at_row : at_row + n, :], to_l[at_row : at_row + n, :] = halves(value)

    def twice(e):
        return jnp.concatenate([e, e], axis=1)

    for q in range(3):
        for h in range(2):
            e = twice(transfer[q * 256 + h * 128 : q * 256 + h * 128 + 128, :])
            keep = low128 if h == 0 else jnp.logical_not(low128)
            put(bl_h, bl_l, q * 256 + h * 128, jnp.where(keep, e, 0.0))
    put(bl_h, bl_l, 768, twice(transfer[768:896, :]))
    root_e = transfer[896:960, :]
    put(bl_h, bl_l, 896, twice(root_e))

    leaf = []
    for j in range(4):
        two = jnp.concatenate(
            [xe[0:32, 1024 + 512 * j : 1280 + 512 * j], xe[0:32, 1280 + 512 * j : 1536 + 512 * j]], axis=0
        )
        leaf.append(beside(matmul(two, bb_h[128 * j : 128 * j + 128, :], bb_l[128 * j : 128 * j + 128, :], NT)))

    def lift(values, h, low, first):
        joined = values[0] if len(values) == 1 else jnp.concatenate(values, axis=1)
        n = joined.shape[1]
        return matmul(joined, h[first : first + n, :], low[first : first + n, :])

    mid_a = lift(leaf[0:2], bl_h, bl_l, 0)
    mid_b = lift(leaf[2:4], bl_h, bl_l, 256)
    top = lift([mid_a, mid_b], bl_h, bl_l, 512)
    root = lift([top], bl_h, bl_l, 768)
    term = lift([root[:, 0:64]], bl_h, bl_l, 896)
    zbuf[r] = jnp.where(low_lanes(16), term[0:16], term[16:32])

    def row_copy(k, sender):
        to = lax.rem(r + k, 16)
        slot = r if sender else to
        return pltpu.make_async_remote_copy(
            zbuf.at[slot], zbuf.at[slot], z_send.at[k], z_recv.at[slot],
            device_id=(g, y * 16 + to), device_id_type=MESH,
        )

    def send_row(k, _):
        row_copy(k, True).start()
        return 0

    lax.fori_loop(1, 16, send_row, 0)
    for i, value in enumerate((leaf[0], leaf[1], mid_a, top, root, mid_b, leaf[2], leaf[3])):
        ce[0:32, i * 128 : i * 128 + 128] = value
    coef_copies = [
        pltpu.make_async_remote_copy(
            ce.at[:, 384:1024], lh, coef_send.at[0], coef_recv.at[0], device_id=right, device_id_type=MESH
        ),
        pltpu.make_async_remote_copy(
            ce.at[:, 0:640], rh, coef_send.at[1], coef_recv.at[1], device_id=left, device_id_type=MESH
        ),
    ]
    for copy in coef_copies:
        copy.start()

    for load in loads[5:11]:
        load.wait()
    near = usable(near_list[...], counted(near_count, 8, 8))
    ids = lanes(4096) // 256
    itself = lax.broadcasted_iota(jnp.int32, (8, 1), 0) + 4 == ids
    t2[...] = (mask(near, ids + (dev * 8 - 4)) + jnp.where(itself, 1.0, 0.0)) * KAPPA
    src, tgt = features(xe[32:40, 1024:3072])
    f[...] = tgt
    ft[1024:3072, :] = as_rows(src)

    def near_leaf(t, first, last):
        targets = f[:, t * 256 : t * 256 + 256]
        total = jnp.zeros((32, 256), F32)
        for e in range(first, last):
            part = slice(e * 256, e * 256 + 256)
            x_high, x_low = halves(xe[0:32, part] * t2[t : t + 1, part])
            kh, kl = kern(dot(ft[part, :], targets))
            both = dot(jnp.concatenate([x_high, x_low], axis=0), kh)
            total += both[:32] + both[32:] + dot(x_high, kl)
        return total

    def own_leaf(t):
        part = slice(t * 256, t * 256 + 256)
        nugget = NUGGET * xe[0:32, t * 256 + 1024 : t * 256 + 1280]
        acc[:, part] = nugget + near_leaf(t, max(t, 4), min(t + 9, 12))

    with jax.named_scope("near_a"):
        for t in range(4):
            own_leaf(t)

    for load in loads[11:14]:
        load.wait()

    with jax.named_scope("upper_weights"):
        def turn(i, _):
            half, k = lax.div(i, 32), lax.rem(i, 32)
            first = pl.multiple_of(half * 4096 + k * 64, 64)
            block = jnp.concatenate([ev[pl.ds(first, 64), :], ev[pl.ds(first + 2048, 64), :]], axis=0)
            et[pl.ds(pl.multiple_of(i * 128, 128), 128), :] = block.T
            return 0

        lax.fori_loop(0, 64, turn, 0, unroll=4)

        def edge(h, half):
            two = et[pl.ds(half * 4096 + h - (128 if half == 0 else 0), 32, stride=128), :]
            other = pltpu.roll(two, 64, 1)
            low = low_lanes(32)
            return jnp.concatenate([jnp.where(low, two, other), jnp.where(low, other, two)], axis=0)

        nodes = (
            (128 + 32 * g + 8 * y, 0, 0),
            (132 + 32 * g + 8 * y, 0, 256),
            (64 + 16 * g + 4 * y, 1, 512),
            (16 + 4 * g, 1, 896),
            (4, 1, 1280),
        )
        low64 = low_lanes(64)
        for first, half, to in nodes:
            for n in range(4):
                keep = low64 if n < 2 else jnp.logical_not(low64)
                put(bu_h, bu_l, to + n * 64, jnp.where(keep, edge(first + n, half), 0.0))
        for first, to in ((32 + 8 * g + 2 * y, 768), (8 + 2 * g, 1152)):
            for n in range(2):
                put(bu_h, bu_l, to + n * 64, edge(first + n, 1))
    with jax.named_scope("upper_skeletons"):
        su[...] = jnp.zeros((8, 4352), F32)
        for c in range(3):
            for h in range(2):
                first = h * 128
                block = jnp.concatenate([sv[c * 64 : c * 64 + 64, first : first + 128]] * 2, axis=0)
                st[c, first : first + 128, :] = block.T
        at_lane = 0
        for first, n in zip(firsts, UPPER):
            for i in range(n // 2):
                one, two = st[:, pl.ds(first + 2 * i, 1), :], st[:, pl.ds(first + 2 * i + 1, 1), :]
                pair = jnp.where(lax.broadcasted_iota(jnp.int32, (3, 1, 128), 2) < 64, one, two)
                su[0:3, at_lane : at_lane + 128] = scaled(pair.reshape(3, 128))
                at_lane += 128
        fu[...] = features(su[...], "t")[0]
        heap = [lax.div(256 + dev, 2 ** (i + 1)) for i in range(7)]
        tu[...] = jnp.zeros((8, 512), F32)
        for i, (m, n) in enumerate(((0, 1), (2, 3), (4, 5), (6, 6))):
            one, two = st[:, pl.ds(heap[m], 1), :], st[:, pl.ds(heap[n], 1), :]
            pair = jnp.where(lax.broadcasted_iota(jnp.int32, (3, 1, 128), 2) < 64, one, two)
            tu[0:3, i * 128 : i * 128 + 128] = scaled(pair.reshape(3, 128))
        ftu = as_rows(features(tu[...], "s")[0])

    with jax.named_scope("near_b"):
        for t in range(4, 8):
            own_leaf(t)

    def take_row(k, _):
        row_copy(k, False).wait_recv()
        return 0

    lax.fori_loop(1, 16, take_row, 0)
    low16 = low_lanes(16)
    level7 = []
    for j in range(4):
        one = zbuf[4 * j] + zbuf[4 * j + 1]
        two = zbuf[4 * j + 2] + zbuf[4 * j + 3]
        level7.append(
            jnp.concatenate(
                [jnp.where(low16, one, pltpu.roll(two, 64, 1)), jnp.where(low16, pltpu.roll(one, 64, 1), two)], axis=0
            )
        )
    level6 = [lift(level7[0:2], bu_h, bu_l, 0), lift(level7[2:4], bu_h, bu_l, 256)]
    level5 = lift(level6, bu_h, bu_l, 512)
    level4 = lift([level5], bu_h, bu_l, 768)
    for i, value in enumerate((*level7, *level6, level5, level4)):
        gc[y, :, i * 128 : i * 128 + 128] = value

    def plane_copy(k, sender):
        to = lax.rem(y + k, 4)
        slot = y if sender else to
        return pltpu.make_async_remote_copy(
            gc.at[slot], gc.at[slot], y_send.at[k], y_recv.at[slot], device_id=(g, to * 16 + r), device_id_type=MESH
        )

    for k in range(1, 4):
        plane_copy(k, True).start()

    for copy in near_copies:
        copy.wait_recv()
    with jax.named_scope("near_c"):
        src = features(xe[32:40, 0:1024], "s")[0]
        ft[0:1024, :] = as_rows(src)
        src = features(xe[32:40, 3072:4096], "s")[0]
        ft[3072:4096, :] = as_rows(src)
        for t in range(4):
            acc[:, t * 256 : t * 256 + 256] += near_leaf(t, t, 4)

    for k in range(1, 4):
        plane_copy(k, False).wait_recv()
    low32 = low_lanes(32)
    level4 = [
        jnp.where(low32, gc[0, :, 896:1024], gc[1, :, 896:1024]),
        jnp.where(low32, gc[2, :, 896:1024], gc[3, :, 896:1024]),
    ]
    level3 = lift(level4, bu_h, bu_l, 896)
    tc[g] = lift([level3], bu_h, bu_l, 1152)

    def group_copy(k, sender):
        to = lax.rem(g + k, 4)
        slot = g if sender else to
        return pltpu.make_async_remote_copy(
            tc.at[slot], tc.at[slot], x_send.at[k], x_recv.at[slot], device_id=(to, b), device_id_type=MESH
        )

    for k in range(1, 4):
        group_copy(k, True).start()

    with jax.named_scope("near_d"):
        for t in range(4, 8):
            acc[:, t * 256 : t * 256 + 256] += near_leaf(t, 12, t + 9)

    for copy in coef_copies:
        copy.wait_recv()
    ftl[...] = as_rows(features(ce[32:40, :], "s")[0])
    spot = lax.broadcasted_iota(jnp.int32, (8, 15), 1)
    slot = lax.broadcasted_iota(jnp.int32, (8, 15), 0)
    counts = jnp.zeros((8, 15), jnp.int32)
    for n in range(15):
        counts = jnp.where(spot == n, inter_count[n], counts)
    inter = jnp.where(slot < counts, inter_list[...], -1000)

    def listed(n, ids):
        return jnp.sum(jnp.where(inter[:, n : n + 1] == ids, 1.0, 0.0), axis=0, keepdims=True)

    table = jnp.concatenate([lh[:, 384:640], ce[:, 0:256], ce[:, 768:1024], rh[:, 0:256]], axis=1)
    feats = features(table[32:40], "t")[0]
    ids = lanes(1024) // 64 + (dev * 8 - 4)
    field0 = []
    for j, at_lane in enumerate((0, 128, 768, 896)):
        part = slice(j * 128, j * 128 + 640)
        masks = [listed(2 * j, ids[:, part]), listed(2 * j + 1, ids[:, part])]
        field0.append(beside(couple(ftl[at_lane : at_lane + 128, :], feats[:, part], table[0:32, part], masks)))
    table = jnp.concatenate([lh[:, 256:384], ce[:, 256:384], ce[:, 640:768], rh[:, 256:384]], axis=1)
    feats = features(table[32:40], "t")[0]
    ids = lanes(512) // 64 + (dev * 4 - 2)
    field1 = []
    for j, at_lane in enumerate((256, 640)):
        part = slice(j * 128, j * 128 + 384)
        masks = [listed(8 + 2 * j, ids[:, part]), listed(9 + 2 * j, ids[:, part])]
        field1.append(beside(couple(ftl[at_lane : at_lane + 128, :], feats[:, part], table[0:32, part], masks)))
    table = jnp.concatenate([lh[:, 0:128], ce[:, 384:512], rh[:, 384:512]], axis=1)
    feats = features(table[32:40], "t")[0]
    ids = lanes(384) // 64 + (dev * 2 - 2)
    field2 = beside(couple(ftl[384:512, :], feats, table[0:32], [listed(12, ids), listed(13, ids)]))
    table = jnp.concatenate([lh[:, 128:256], ce[:, 512:640], rh[:, 512:640]], axis=1)
    feats = features(table[32:40], "t")[0]
    spot = lanes(384)
    ids = jnp.where(lax.rem(spot, 128) < 64, spot // 128 + (dev - 1), -1)
    found = listed(14, ids)
    field3 = beside(couple(ftl[512:640, :], feats, table[0:32], [found, found]))

    product = jnp.concatenate([root_e, root_e], axis=0)
    for i in range(7):
        if i > 0:
            product = matmul(product, *halves(edge(heap[i - 1], 0 if i == 1 else 1)[:, 0:64]))
        qh[i], ql[i] = halves(product)
    node = lax.broadcasted_iota(jnp.int32, (8, 256), 1)
    up_slots = lax.broadcasted_iota(jnp.int32, (8, 1), 0)
    up_lists = up_list[...].astype(F32)

    def path_field(i, coefs):
        h = heap[i]
        first, n = sum(UPPER[:i]) * 64, UPPER[i] * 64
        column = jnp.sum(jnp.where(node == h, up_lists, 0.0), axis=1, keepdims=True)
        column = jnp.where(up_slots < up_count[h], column, -1000.0)
        ids = (lanes(n) // 64 + firsts[i]).astype(F32)
        found = jnp.sum(jnp.where(column == ids, 1.0, 0.0), axis=0, keepdims=True)
        field = couple(ftu[i * 64 : i * 64 + 64, :], fu[:, first : first + n], coefs, [found])
        return matmul(field, qh[i], ql[i], NT)

    incoming = path_field(0, jnp.concatenate([gc[k, :, 0:512] for k in range(4)], axis=1))
    incoming += path_field(1, jnp.concatenate([gc[k, :, 512:768] for k in range(4)], axis=1))
    incoming += path_field(2, jnp.concatenate([gc[k, :, 768:896] for k in range(4)], axis=1))
    incoming += path_field(3, jnp.concatenate(level4, axis=1))
    incoming += path_field(4, level3)
    for k in range(1, 4):
        group_copy(k, False).wait_recv()
    level2 = [jnp.where(low32, tc[0], tc[1]), jnp.where(low32, tc[2], tc[3])]
    incoming += path_field(5, jnp.concatenate(level2, axis=1))
    incoming += path_field(6, lift(level2, bu_h, bu_l, 1280))

    def lower(value, first, n):
        return matmul(value, bl_h[first : first + n, :], bl_l[first : first + n, :], NT)

    down3 = jnp.where(low32, field3 + incoming, 0.0)
    down2 = field2 + lower(down3, 768, 128)
    down1 = lower(down2, 512, 256)
    down1 = [field1[0] + down1[:, 0:128], field1[1] + down1[:, 128:256]]
    for q in range(2):
        down0 = lower(down1[q], q * 256, 256)
        for h in range(2):
            j = 2 * q + h
            pair = field0[j] + down0[:, h * 128 : h * 128 + 128]
            two = jnp.concatenate([jnp.where(low32, pair, 0.0), jnp.where(low32, 0.0, pair)], axis=0)
            far = matmul(two, bb_h[128 * j : 128 * j + 128, :], bb_l[128 * j : 128 * j + 128, :])
            for k in range(2):
                part = slice((2 * j + k) * 256, (2 * j + k) * 256 + 256)
                out[:, part] = acc[:, part] + far[32 * k : 32 * k + 32]

    for copy in near_copies + coef_copies:
        copy.wait_send()

    def sent_row(k, _):
        row_copy(k, True).wait_send()
        return 0

    lax.fori_loop(1, 16, sent_row, 0)
    for k in range(1, 4):
        plane_copy(k, True).wait_send()
        group_copy(k, True).wait_send()


def on_device(
    rs, pts, basis, transfer, skel, near_list, near_count, inter_list, inter_count, up_t, up_s, up_list, up_count
):
    vmem = pl.BlockSpec(memory_space=pltpu.VMEM)
    anywhere = pl.BlockSpec(memory_space=pl.ANY)
    dma = pltpu.SemaphoreType.DMA
    return pl.pallas_call(
        kernel,
        out_shape=jax.ShapeDtypeStruct((32, 2048), F32),
        in_specs=[anywhere] * 13,
        out_specs=vmem,
        scratch_shapes=[
            pltpu.VMEM((40, 4096), F32),
            pltpu.VMEM((32, 2048), F32),
            pltpu.VMEM((FEATS, 2048), BF16),
            pltpu.VMEM((4096, FEATS), BF16),
            pltpu.VMEM((8, 4096), F32),
            pltpu.VMEM((512, 256), BF16),
            pltpu.VMEM((512, 256), BF16),
            pltpu.VMEM((960, 128), BF16),
            pltpu.VMEM((960, 128), BF16),
            pltpu.VMEM((1536, 128), BF16),
            pltpu.VMEM((1536, 128), BF16),
            pltpu.VMEM((40, 1024), F32),
            pltpu.VMEM((40, 640), F32),
            pltpu.VMEM((40, 640), F32),
            pltpu.VMEM((1024, FEATS), BF16),
            pltpu.VMEM((8192, 128), F32),
            pltpu.VMEM((8192, 128), F32),
            pltpu.VMEM((192, 256), F32),
            pltpu.VMEM((3, 256, 128), F32),
            pltpu.VMEM((8, 4352), F32),
            pltpu.VMEM((FEATS, 4352), BF16),
            pltpu.VMEM((8, 512), F32),
            pltpu.VMEM((16, 16, 128), F32),
            pltpu.VMEM((4, 32, 1024), F32),
            pltpu.VMEM((4, 32, 128), F32),
            pltpu.VMEM((7, 128, 64), BF16),
            pltpu.VMEM((7, 128, 64), BF16),
            pltpu.VMEM((3, 2048), F32),
            pltpu.VMEM((512, 256), F32),
            pltpu.VMEM((960, 64), F32),
            pltpu.VMEM((3, 15, 64), F32),
            pltpu.VMEM((8, 8), jnp.int32),
            pltpu.SMEM((8,), jnp.int32),
            pltpu.VMEM((8, 15), jnp.int32),
            pltpu.SMEM((15,), jnp.int32),
            pltpu.VMEM((8, 256), jnp.int32),
            pltpu.SMEM((256,), jnp.int32),
            dma((14,)),
            dma((2,)), dma((2,)), dma((2,)), dma((2,)),
            dma((16,)), dma((16,)), dma((4,)), dma((4,)), dma((4,)), dma((4,)),
        ],
        compiler_params=pltpu.CompilerParams(
            collective_id=0, has_side_effects=True, vmem_limit_bytes=60 * 2**20
        ),
    )(
        rs, pts, basis.reshape(512, 256), transfer.reshape(960, 64), skel.transpose(1, 0, 2), near_list, near_count,
        inter_list.T, inter_count, up_t.transpose(1, 2, 0).reshape(4096, 256), up_s.transpose(1, 2, 0).reshape(192, 256),
        up_list.T, up_count,
    )


def solution(mesh):
    both = ("group", "bulk")
    in_specs = (
        P(None, both),
        P(None, both),
        P(both, None, None),
        P(both, None, None),
        P(both, None, None),
        P(both, None),
        P(both),
        P(both, None),
        P(both),
        P(),
        P(),
        P(),
        P(),
    )
    return jax.shard_map(
        on_device, mesh=mesh, in_specs=in_specs, out_specs=P(None, both), check_vma=False
    )
```

```python
import functools
import math

import jax
import jax.numpy as jnp
from jax import lax
from jax.experimental import pallas as pl
from jax.experimental.pallas import tpu as pltpu
from jax.sharding import PartitionSpec as P

F32 = jnp.float32
BF16 = jnp.bfloat16
MESH = pl.DeviceIdType.MESH
NN = (((1,), (0,)), ((), ()))
NT = (((1,), (1,)), ((), ()))

ALPHA = 2.0 / math.log(2.0)
KAPPA = 0.2 * math.log(2.0)
SHIFT = 1.0 / math.log(2.0)
SOFT = 0.01 * ALPHA * ALPHA
CENTER = 2.0
NUGGET = 0.5
FEATS = 48
UPPER = (32, 16, 8, 4, 2, 4, 2)


def dot(a, b, dims=NN):
    return lax.dot_general(a, b, dims, preferred_element_type=F32)


def halves(x):
    high = x.astype(BF16)
    return high, (x - high.astype(F32)).astype(BF16)


def matmul(a, high, low, dims=NN):
    m = a.shape[0]
    a_high, a_low = halves(a)
    both = dot(jnp.concatenate([a_high, a_low], axis=0), high, dims)
    return both[:m] + both[m:] + dot(a_high, low, dims)


def kern(w):
    y = w * lax.rsqrt(w)
    return halves((SHIFT + y) * jnp.exp2(-y))


def in_three(x):
    one = x.astype(BF16).astype(F32)
    rest = x - one
    two = rest.astype(BF16).astype(F32)
    return one, two, (rest - two).astype(BF16).astype(F32)


def scaled(x):
    return ALPHA * (x - CENTER)


def features(u, sides="st"):
    row = lax.broadcasted_iota(jnp.int32, u.shape, 0)
    square = jnp.sum(u * u, axis=0, keepdims=True)
    out = []
    if "s" in sides:
        s = jnp.where(row < 3, -2.0 * u, jnp.where(row == 3, square, jnp.where(row == 4, 1.0, 0.0)))
        a, b, c = in_three(s)
        out.append(jnp.concatenate([a, a, b, b, a, c], axis=0))
    if "t" in sides:
        t = jnp.where(row < 3, u, jnp.where(row == 3, 1.0, jnp.where(row == 4, square + SOFT, 0.0)))
        a, b, c = in_three(t)
        out.append(jnp.concatenate([a, b, a, b, c, a], axis=0).astype(BF16))
    return out


def as_rows(f):
    return f.T.astype(BF16)


def usable(values, counts):
    slot = lax.broadcasted_iota(jnp.int32, values.shape, 1)
    return jnp.where(slot < counts, values, -1000)


def counted(ref, rows, width):
    row = lax.broadcasted_iota(jnp.int32, (rows, width), 0)
    out = jnp.zeros((rows, width), jnp.int32)
    for t in range(rows):
        out = jnp.where(row == t, ref[t], out)
    return out


def mask(lists, ids):
    out = jnp.zeros((lists.shape[0], ids.shape[1]), F32)
    for i in range(lists.shape[1]):
        out += jnp.where(lists[:, i : i + 1] == ids, 1.0, 0.0)
    return out


def lanes(n):
    return lax.broadcasted_iota(jnp.int32, (1, n), 1)


def low_lanes(rows):
    return lax.broadcasted_iota(jnp.int32, (rows, 128), 1) < 64


def couple(rows, feats, coefs, masks):
    kh, kl = kern(dot(rows, feats))
    weighted = [coefs * (m * KAPPA) for m in masks]
    weighted = weighted[0] if len(weighted) == 1 else jnp.concatenate(weighted, axis=0)
    return matmul(weighted, kh, kl, NT)


def beside(pair):
    return jnp.where(low_lanes(32), pair[:32], pair[32:])


def kernel(
    rs, pts_in, basis_in, transfer_in, skel_in, near_list_in, near_count_in, inter_list_in, inter_count_in,
    up_t, up_s, up_list_in, up_count_in, out,
    xe, acc, f, ft, t2, bb_h, bb_l, bl_h, bl_l, bu_h, bu_l,
    ce, lh, rh, ftl, ev, et, sv, st, su, fu, tu, ftu, zbuf, gc, tc, qh, ql,
    pts, basis, transfer, skel, near_list, near_count, inter_list, inter_count, up_list, up_count,
    in_sem, near_send, near_recv, coef_send, coef_recv, z_send, z_recv, y_send, y_recv, x_send, x_recv,
):
    g = lax.axis_index("group")
    b = lax.axis_index("bulk")
    z = lax.rem(lax.div(b, 2), 8)
    y = lax.div(b, 16)
    r = lax.rem(b, 16)
    dev = g * 64 + b

    def at(d):
        d = lax.rem(d + 256, 256)
        return (lax.div(d, 64), lax.rem(d, 64))

    right, left = at(dev + 1), at(dev - 1)

    pairs = (
        (rs, xe.at[0:32, 1024:3072]),
        (pts_in, pts),
        (skel_in, skel),
        (basis_in, basis),
        (transfer_in, transfer),
        (near_list_in, near_list),
        (near_count_in, near_count),
        (inter_list_in, inter_list),
        (inter_count_in, inter_count),
        (up_list_in, up_list),
        (up_count_in, up_count),
        (up_s, sv),
        (up_t.at[:, 128:256], ev.at[0:4096]),
        (up_t.at[:, 0:128], ev.at[4096:8192]),
    )
    loads = [pltpu.make_async_copy(of, to, in_sem.at[i]) for i, (of, to) in enumerate(pairs)]
    for load in loads:
        load.start()
    firsts = (128 + 32 * g, 64 + 16 * g, 32 + 8 * g, 16 + 4 * g, 8 + 2 * g, 4, 2)

    barrier = pltpu.get_barrier_semaphore()

    def greet(device):
        pl.semaphore_signal(barrier, inc=1, device_id=device, device_id_type=MESH)

    greet(right)
    greet(left)

    def greet_row(k, _):
        greet((g, y * 16 + lax.rem(r + k, 16)))
        return 0

    lax.fori_loop(1, 16, greet_row, 0)
    for k in range(1, 4):
        greet((g, lax.rem(y + k, 4) * 16 + r))
        greet((lax.rem(g + k, 4), b))

    xe[32:40, 1024:3072] = jnp.zeros((8, 2048), F32)
    loads[1].wait()
    loads[2].wait()
    xe[32:35, 1024:3072] = scaled(pts[...])
    ce[32:40, :] = jnp.zeros((8, 1024), F32)
    order = ((0, 1), (2, 3), (8, 9), (12, 13), (14, 14), (10, 11), (4, 5), (6, 7))
    for i, (m, n) in enumerate(order):
        ce[32:35, i * 128 : i * 128 + 128] = scaled(jnp.concatenate([skel[:, m, :], skel[:, n, :]], axis=1))
    loads[0].wait()
    pl.semaphore_wait(barrier, 23)

    near_copies = [
        pltpu.make_async_remote_copy(
            xe.at[:, 2048:3072], xe.at[:, 0:1024], near_send.at[0], near_recv.at[0],
            device_id=right, device_id_type=MESH,
        ),
        pltpu.make_async_remote_copy(
            xe.at[:, 1024:2048], xe.at[:, 3072:4096], near_send.at[1], near_recv.at[1],
            device_id=left, device_id_type=MESH,
        ),
    ]
    for copy in near_copies:
        copy.start()

    loads[3].wait()
    loads[4].wait()
    bb_h[...], bb_l[...] = halves(basis[...])
    low128 = low_lanes(128)

    def put(to_h, to_l, at_row, value):
        n = value.shape[0]
        to_h[at_row : at_row + n, :], to_l[at_row : at_row + n, :] = halves(value)

    def twice(e):
        return jnp.concatenate([e, e], axis=1)

    for q in range(3):
        for h in range(2):
            e = twice(transfer[q * 256 + h * 128 : q * 256 + h * 128 + 128, :])
            keep = low128 if h == 0 else jnp.logical_not(low128)
            put(bl_h, bl_l, q * 256 + h * 128, jnp.where(keep, e, 0.0))
    put(bl_h, bl_l, 768, twice(transfer[768:896, :]))
    root_e = transfer[896:960, :]
    put(bl_h, bl_l, 896, twice(root_e))

    leaf = []
    for j in range(4):
        two = jnp.concatenate(
            [xe[0:32, 1024 + 512 * j : 1280 + 512 * j], xe[0:32, 1280 + 512 * j : 1536 + 512 * j]], axis=0
        )
        leaf.append(beside(matmul(two, bb_h[128 * j : 128 * j + 128, :], bb_l[128 * j : 128 * j + 128, :], NT)))

    def lift(values, h, low, first):
        joined = values[0] if len(values) == 1 else jnp.concatenate(values, axis=1)
        n = joined.shape[1]
        return matmul(joined, h[first : first + n, :], low[first : first + n, :])

    mid_a = lift(leaf[0:2], bl_h, bl_l, 0)
    mid_b = lift(leaf[2:4], bl_h, bl_l, 256)
    top = lift([mid_a, mid_b], bl_h, bl_l, 512)
    root = lift([top], bl_h, bl_l, 768)
    term = lift([root[:, 0:64]], bl_h, bl_l, 896)
    zbuf[r] = jnp.where(low_lanes(16), term[0:16], term[16:32])

    def row_copy(k, sender):
        to = lax.rem(r + k, 16)
        slot = r if sender else to
        return pltpu.make_async_remote_copy(
            zbuf.at[slot], zbuf.at[slot], z_send.at[k], z_recv.at[slot],
            device_id=(g, y * 16 + to), device_id_type=MESH,
        )

    def send_row(k, _):
        row_copy(k, True).start()
        return 0

    lax.fori_loop(1, 16, send_row, 0)
    for i, value in enumerate((leaf[0], leaf[1], mid_a, top, root, mid_b, leaf[2], leaf[3])):
        ce[0:32, i * 128 : i * 128 + 128] = value
    coef_copies = [
        pltpu.make_async_remote_copy(
            ce.at[:, 384:1024], lh, coef_send.at[0], coef_recv.at[0], device_id=right, device_id_type=MESH
        ),
        pltpu.make_async_remote_copy(
            ce.at[:, 0:640], rh, coef_send.at[1], coef_recv.at[1], device_id=left, device_id_type=MESH
        ),
    ]
    for copy in coef_copies:
        copy.start()

    for load in loads[5:11]:
        load.wait()
    near = usable(near_list[...], counted(near_count, 8, 8))
    ids = lanes(4096) // 256
    itself = lax.broadcasted_iota(jnp.int32, (8, 1), 0) + 4 == ids
    t2[...] = (mask(near, ids + (dev * 8 - 4)) + jnp.where(itself, 1.0, 0.0)) * KAPPA
    src, tgt = features(xe[32:40, 1024:3072])
    f[...] = tgt
    ft[1024:3072, :] = as_rows(src)

    def near_leaf(t, first, last, between):
        targets = f[:, t * 256 : t * 256 + 256]
        total = jnp.zeros((32, 256), F32)
        for e in range(first, last):
            part = slice(e * 256, e * 256 + 256)
            x_high, x_low = halves(xe[0:32, part] * t2[t : t + 1, part])
            kh, kl = kern(dot(ft[part, :], targets))
            both = dot(jnp.concatenate([x_high, x_low], axis=0), kh)
            total += both[:32] + both[32:] + dot(x_high, kl)
            between()
        return total

    def spread(chores, blocks):
        state = [0, 0]

        def between():
            state[0] += 1
            until = len(chores) * state[0] // blocks
            for chore in chores[state[1] : until]:
                chore()
            state[1] = until

        return between

    def own_leaf(t, between):
        part = slice(t * 256, t * 256 + 256)
        nugget = NUGGET * xe[0:32, t * 256 + 1024 : t * 256 + 1280]
        acc[:, part] = nugget + near_leaf(t, max(t, 4), min(t + 9, 12), between)

    for load in loads[11:14]:
        load.wait()

    def turn(i):
        first = i // 32 * 4096 + i % 32 * 64
        block = jnp.concatenate([ev[first : first + 64, :], ev[first + 2048 : first + 2112, :]], axis=0)
        et[i * 128 : i * 128 + 128, :] = block.T

    def edge(h, half):
        two = et[pl.ds(half * 4096 + h - (128 if half == 0 else 0), 32, stride=128), :]
        other = pltpu.roll(two, 64, 1)
        low = low_lanes(32)
        return jnp.concatenate([jnp.where(low, two, other), jnp.where(low, other, two)], axis=0)

    low64 = low_lanes(64)

    def put_edge(h, half, to, keep):
        value = edge(h, half)
        put(bu_h, bu_l, to, value if keep is None else jnp.where(keep, value, 0.0))

    nodes = (
        (128 + 32 * g + 8 * y, 0, 0),
        (132 + 32 * g + 8 * y, 0, 256),
        (64 + 16 * g + 4 * y, 1, 512),
        (16 + 4 * g, 1, 896),
        (4, 1, 1280),
    )
    chores = [functools.partial(turn, i) for i in range(64)]
    for first, half, to in nodes:
        for n in range(4):
            keep = low64 if n < 2 else jnp.logical_not(low64)
            chores.append(functools.partial(put_edge, first + n, half, to + n * 64, keep))
    for first, to in ((32 + 8 * g + 2 * y, 768), (8 + 2 * g, 1152)):
        for n in range(2):
            chores.append(functools.partial(put_edge, first + n, 1, to + n * 64, None))
    between = spread(chores, 26)
    for t in range(4):
        own_leaf(t, between)

    def take_row(k, _):
        row_copy(k, False).wait_recv()
        return 0

    lax.fori_loop(1, 16, take_row, 0)
    low16 = low_lanes(16)
    level7 = []
    for j in range(4):
        one = zbuf[4 * j] + zbuf[4 * j + 1]
        two = zbuf[4 * j + 2] + zbuf[4 * j + 3]
        level7.append(
            jnp.concatenate(
                [jnp.where(low16, one, pltpu.roll(two, 64, 1)), jnp.where(low16, pltpu.roll(one, 64, 1), two)], axis=0
            )
        )
    level6 = [lift(level7[0:2], bu_h, bu_l, 0), lift(level7[2:4], bu_h, bu_l, 256)]
    level5 = lift(level6, bu_h, bu_l, 512)
    level4 = lift([level5], bu_h, bu_l, 768)
    for i, value in enumerate((*level7, *level6, level5, level4)):
        gc[y, :, i * 128 : i * 128 + 128] = value

    def plane_copy(k, sender):
        to = lax.rem(y + k, 4)
        slot = y if sender else to
        return pltpu.make_async_remote_copy(
            gc.at[slot], gc.at[slot], y_send.at[k], y_recv.at[slot], device_id=(g, to * 16 + r), device_id_type=MESH
        )

    for k in range(1, 4):
        plane_copy(k, True).start()

    heap = [lax.div(256 + dev, 2 ** (i + 1)) for i in range(7)]
    low3 = lax.broadcasted_iota(jnp.int32, (3, 1, 128), 2) < 64

    def turn_skeleton(c, h):
        block = jnp.concatenate([sv[c * 64 : c * 64 + 64, h * 128 : h * 128 + 128]] * 2, axis=0)
        st[c, h * 128 : h * 128 + 128, :] = block.T

    def put_skeletons(ref, m, n, at_lane):
        pair = jnp.where(low3, st[:, pl.ds(m, 1), :], st[:, pl.ds(n, 1), :])
        ref[0:3, at_lane : at_lane + 128] = scaled(pair.reshape(3, 128))

    def put_features():
        fu[...] = features(su[...], "t")[0]
        ftu[...] = as_rows(features(tu[...], "s")[0])

    last = [jnp.concatenate([root_e, root_e], axis=0)]

    def path_product(i):
        if i > 0:
            last[0] = matmul(last[0], *halves(edge(heap[i - 1], 0 if i == 1 else 1)[:, 0:64]))
        qh[i], ql[i] = halves(last[0])

    su[...] = jnp.zeros((8, 4352), F32)
    tu[...] = jnp.zeros((8, 512), F32)
    skeletons = [functools.partial(turn_skeleton, c, h) for c in range(3) for h in range(2)]
    at_lane = 0
    for first, n in zip(firsts, UPPER):
        for i in range(n // 2):
            skeletons.append(functools.partial(put_skeletons, su, first + 2 * i, first + 2 * i + 1, at_lane))
            at_lane += 128
    for i, (m, n) in enumerate(((0, 1), (2, 3), (4, 5), (6, 6))):
        skeletons.append(functools.partial(put_skeletons, tu, heap[m], heap[n], i * 128))
    skeletons.append(put_features)
    products = [functools.partial(path_product, i) for i in range(7)]
    chores = []
    for i, chore in enumerate(skeletons):
        chores.append(chore)
        if i % 6 == 5 and products:
            chores.append(products.pop(0))
    chores += products
    between = spread(chores, 26)
    for t in range(4, 8):
        own_leaf(t, between)

    for k in range(1, 4):
        plane_copy(k, False).wait_recv()
    low32 = low_lanes(32)
    level4 = [
        jnp.where(low32, gc[0, :, 896:1024], gc[1, :, 896:1024]),
        jnp.where(low32, gc[2, :, 896:1024], gc[3, :, 896:1024]),
    ]
    level3 = lift(level4, bu_h, bu_l, 896)
    tc[g] = lift([level3], bu_h, bu_l, 1152)

    def group_copy(k, sender):
        to = lax.rem(g + k, 4)
        slot = g if sender else to
        return pltpu.make_async_remote_copy(
            tc.at[slot], tc.at[slot], x_send.at[k], x_recv.at[slot], device_id=(to, b), device_id_type=MESH
        )

    for k in range(1, 4):
        group_copy(k, True).start()

    for copy in near_copies + coef_copies:
        copy.wait_recv()
    src = features(xe[32:40, 0:1024], "s")[0]
    ft[0:1024, :] = as_rows(src)
    src = features(xe[32:40, 3072:4096], "s")[0]
    ft[3072:4096, :] = as_rows(src)
    ftl[...] = as_rows(features(ce[32:40, :], "s")[0])
    spot = lax.broadcasted_iota(jnp.int32, (8, 15), 1)
    slot = lax.broadcasted_iota(jnp.int32, (8, 15), 0)
    counts = jnp.zeros((8, 15), jnp.int32)
    for n in range(15):
        counts = jnp.where(spot == n, inter_count[n], counts)
    inter = jnp.where(slot < counts, inter_list[...], -1000)

    def listed(n, ids):
        return jnp.sum(jnp.where(inter[:, n : n + 1] == ids, 1.0, 0.0), axis=0, keepdims=True)

    one_ids = jnp.where(lax.rem(lanes(384), 128) < 64, lanes(384) // 128 + (dev - 1), -1)
    tables = (
        ([lh[:, 384:640], ce[:, 0:256], ce[:, 768:1024], rh[:, 0:256]], lanes(1024) // 64 + (dev * 8 - 4)),
        ([lh[:, 256:384], ce[:, 256:384], ce[:, 640:768], rh[:, 256:384]], lanes(512) // 64 + (dev * 4 - 2)),
        ([lh[:, 0:128], ce[:, 384:512], rh[:, 384:512]], lanes(384) // 64 + (dev * 2 - 2)),
        ([lh[:, 128:256], ce[:, 512:640], rh[:, 512:640]], one_ids),
    )
    tables = [(jnp.concatenate(parts, axis=1), ids) for parts, ids in tables]
    tables = [(table[0:32], features(table[32:40], "t")[0], ids) for table, ids in tables]
    fields = {}

    def local_field(level, m, n, at_lane, first, width):
        coefs, feats, ids = tables[level]
        part = slice(first, first + width)
        masks = [listed(m, ids[:, part]), listed(n, ids[:, part])]
        fields[at_lane] = beside(couple(ftl[at_lane : at_lane + 128, :], feats[:, part], coefs[:, part], masks))

    node = lax.broadcasted_iota(jnp.int32, (8, 256), 1)
    up_slots = lax.broadcasted_iota(jnp.int32, (8, 1), 0)
    up_lists = up_list[...].astype(F32)
    path = {}

    def path_kernel(i):
        first, n = sum(UPPER[:i]) * 64, UPPER[i] * 64
        column = jnp.sum(jnp.where(node == heap[i], up_lists, 0.0), axis=1, keepdims=True)
        column = jnp.where(up_slots < up_count[heap[i]], column, -1000.0)
        ids = (lanes(n) // 64 + firsts[i]).astype(F32)
        found = jnp.sum(jnp.where(column == ids, 1.0, 0.0), axis=0, keepdims=True)
        path[i] = (found * KAPPA, *kern(dot(ftu[i * 64 : i * 64 + 64, :], fu[:, first : first + n])))

    def path_field(i, coefs):
        found, kh, kl = path[i]
        return matmul(matmul(coefs * found, kh, kl, NT), qh[i], ql[i], NT)

    incoming = []

    def path_step(i, coefs):
        path_kernel(i)
        incoming.append(path_field(i, coefs()))

    def group_lanes(first, last):
        return lambda: jnp.concatenate([gc[k, :, first:last] for k in range(4)], axis=1)

    chores = [
        functools.partial(path_kernel, 5),
        functools.partial(path_kernel, 6),
        functools.partial(path_step, 0, group_lanes(0, 512)),
        functools.partial(path_step, 1, group_lanes(512, 768)),
        functools.partial(path_step, 2, group_lanes(768, 896)),
        functools.partial(path_step, 3, lambda: jnp.concatenate(level4, axis=1)),
        functools.partial(path_step, 4, lambda: level3),
        functools.partial(local_field, 3, 14, 14, 512, 0, 384),
        functools.partial(local_field, 2, 12, 13, 384, 0, 384),
        functools.partial(local_field, 1, 8, 9, 256, 0, 384),
        functools.partial(local_field, 1, 10, 11, 640, 128, 384),
    ]
    for j, at_lane in enumerate((0, 128, 768, 896)):
        chores.append(functools.partial(local_field, 0, 2 * j, 2 * j + 1, at_lane, j * 128, 640))
    between = spread(chores, 20)
    for t in range(4):
        acc[:, t * 256 : t * 256 + 256] += near_leaf(t, t, 4, between)
    for t in range(4, 8):
        acc[:, t * 256 : t * 256 + 256] += near_leaf(t, 12, t + 9, between)

    for k in range(1, 4):
        group_copy(k, False).wait_recv()
    level2 = [jnp.where(low32, tc[0], tc[1]), jnp.where(low32, tc[2], tc[3])]
    incoming.append(path_field(5, jnp.concatenate(level2, axis=1)))
    incoming.append(path_field(6, lift(level2, bu_h, bu_l, 1280)))
    incoming = sum(incoming[1:], incoming[0])
    field0 = [fields[0], fields[128], fields[768], fields[896]]
    field1 = [fields[256], fields[640]]
    field2, field3 = fields[384], fields[512]

    def lower(value, first, n):
        return matmul(value, bl_h[first : first + n, :], bl_l[first : first + n, :], NT)

    down3 = jnp.where(low32, field3 + incoming, 0.0)
    down2 = field2 + lower(down3, 768, 128)
    down1 = lower(down2, 512, 256)
    down1 = [field1[0] + down1[:, 0:128], field1[1] + down1[:, 128:256]]
    for q in range(2):
        down0 = lower(down1[q], q * 256, 256)
        for h in range(2):
            j = 2 * q + h
            pair = field0[j] + down0[:, h * 128 : h * 128 + 128]
            two = jnp.concatenate([jnp.where(low32, pair, 0.0), jnp.where(low32, 0.0, pair)], axis=0)
            far = matmul(two, bb_h[128 * j : 128 * j + 128, :], bb_l[128 * j : 128 * j + 128, :])
            for k in range(2):
                part = slice((2 * j + k) * 256, (2 * j + k) * 256 + 256)
                out[:, part] = acc[:, part] + far[32 * k : 32 * k + 32]

    for copy in near_copies + coef_copies:
        copy.wait_send()

    def sent_row(k, _):
        row_copy(k, True).wait_send()
        return 0

    lax.fori_loop(1, 16, sent_row, 0)
    for k in range(1, 4):
        plane_copy(k, True).wait_send()
        group_copy(k, True).wait_send()


def on_device(
    rs, pts, basis, transfer, skel, near_list, near_count, inter_list, inter_count, up_t, up_s, up_list, up_count
):
    vmem = pl.BlockSpec(memory_space=pltpu.VMEM)
    anywhere = pl.BlockSpec(memory_space=pl.ANY)
    dma = pltpu.SemaphoreType.DMA
    return pl.pallas_call(
        kernel,
        out_shape=jax.ShapeDtypeStruct((32, 2048), F32),
        in_specs=[anywhere] * 13,
        out_specs=vmem,
        scratch_shapes=[
            pltpu.VMEM((40, 4096), F32),
            pltpu.VMEM((32, 2048), F32),
            pltpu.VMEM((FEATS, 2048), BF16),
            pltpu.VMEM((4096, FEATS), BF16),
            pltpu.VMEM((8, 4096), F32),
            pltpu.VMEM((512, 256), BF16),
            pltpu.VMEM((512, 256), BF16),
            pltpu.VMEM((960, 128), BF16),
            pltpu.VMEM((960, 128), BF16),
            pltpu.VMEM((1536, 128), BF16),
            pltpu.VMEM((1536, 128), BF16),
            pltpu.VMEM((40, 1024), F32),
            pltpu.VMEM((40, 640), F32),
            pltpu.VMEM((40, 640), F32),
            pltpu.VMEM((1024, FEATS), BF16),
            pltpu.VMEM((8192, 128), F32),
            pltpu.VMEM((8192, 128), F32),
            pltpu.VMEM((192, 256), F32),
            pltpu.VMEM((3, 256, 128), F32),
            pltpu.VMEM((8, 4352), F32),
            pltpu.VMEM((FEATS, 4352), BF16),
            pltpu.VMEM((8, 512), F32),
            pltpu.VMEM((512, FEATS), BF16),
            pltpu.VMEM((16, 16, 128), F32),
            pltpu.VMEM((4, 32, 1024), F32),
            pltpu.VMEM((4, 32, 128), F32),
            pltpu.VMEM((7, 128, 64), BF16),
            pltpu.VMEM((7, 128, 64), BF16),
            pltpu.VMEM((3, 2048), F32),
            pltpu.VMEM((512, 256), F32),
            pltpu.VMEM((960, 64), F32),
            pltpu.VMEM((3, 15, 64), F32),
            pltpu.VMEM((8, 8), jnp.int32),
            pltpu.SMEM((8,), jnp.int32),
            pltpu.VMEM((8, 15), jnp.int32),
            pltpu.SMEM((15,), jnp.int32),
            pltpu.VMEM((8, 256), jnp.int32),
            pltpu.SMEM((256,), jnp.int32),
            dma((14,)),
            dma((2,)), dma((2,)), dma((2,)), dma((2,)),
            dma((16,)), dma((16,)), dma((4,)), dma((4,)), dma((4,)), dma((4,)),
        ],
        compiler_params=pltpu.CompilerParams(
            collective_id=0, has_side_effects=True, vmem_limit_bytes=60 * 2**20
        ),
    )(
        rs, pts, basis.reshape(512, 256), transfer.reshape(960, 64), skel.transpose(1, 0, 2), near_list, near_count,
        inter_list.T, inter_count, up_t.transpose(1, 2, 0).reshape(4096, 256), up_s.transpose(1, 2, 0).reshape(192, 256),
        up_list.T, up_count,
    )


def solution(mesh):
    both = ("group", "bulk")
    in_specs = (
        P(None, both),
        P(None, both),
        P(both, None, None),
        P(both, None, None),
        P(both, None, None),
        P(both, None),
        P(both),
        P(both, None),
        P(both),
        P(),
        P(),
        P(),
        P(),
    )
    return jax.shard_map(
        on_device, mesh=mesh, in_specs=in_specs, out_specs=P(None, both), check_vma=False
    )
```

```python
import functools
import math

import jax
import jax.numpy as jnp
from jax import lax
from jax.experimental import pallas as pl
from jax.experimental.pallas import tpu as pltpu
from jax.sharding import PartitionSpec as P

F32 = jnp.float32
BF16 = jnp.bfloat16
MESH = pl.DeviceIdType.MESH
NN = (((1,), (0,)), ((), ()))
NT = (((1,), (1,)), ((), ()))

ALPHA = 2.0 / math.log(2.0)
KAPPA = 0.2 * math.log(2.0)
SHIFT = 1.0 / math.log(2.0)
SOFT = 0.01 * ALPHA * ALPHA
CENTER = 2.0
NUGGET = 0.5
FEATS = 48
UPPER = (32, 16, 8, 4, 2, 4, 2)


def dot(a, b, dims=NN):
    return lax.dot_general(a, b, dims, preferred_element_type=F32)


def halves(x):
    high = x.astype(BF16)
    return high, (x - high.astype(F32)).astype(BF16)


def matmul(a, high, low, dims=NN):
    m = a.shape[0]
    a_high, a_low = halves(a)
    both = dot(jnp.concatenate([a_high, a_low], axis=0), high, dims)
    return both[:m] + both[m:] + dot(a_high, low, dims)


def kern(w):
    y = w * lax.rsqrt(w)
    return halves((SHIFT + y) * jnp.exp2(-y))


def in_three(x):
    one = x.astype(BF16).astype(F32)
    rest = x - one
    two = rest.astype(BF16).astype(F32)
    return one, two, (rest - two).astype(BF16).astype(F32)


def scaled(x):
    return ALPHA * (x - CENTER)


def features(u, sides="st"):
    row = lax.broadcasted_iota(jnp.int32, u.shape, 0)
    square = jnp.sum(u * u, axis=0, keepdims=True)
    out = []
    if "s" in sides:
        s = jnp.where(row < 3, -2.0 * u, jnp.where(row == 3, square, jnp.where(row == 4, 1.0, 0.0)))
        a, b, c = in_three(s)
        out.append(jnp.concatenate([a, a, b, b, a, c], axis=0))
    if "t" in sides:
        t = jnp.where(row < 3, u, jnp.where(row == 3, 1.0, jnp.where(row == 4, square + SOFT, 0.0)))
        a, b, c = in_three(t)
        out.append(jnp.concatenate([a, b, a, b, c, a], axis=0).astype(BF16))
    return out


def as_rows(f):
    return f.T.astype(BF16)


def usable(values, counts):
    slot = lax.broadcasted_iota(jnp.int32, values.shape, 1)
    return jnp.where(slot < counts, values, -1000)


def counted(ref, rows, width):
    row = lax.broadcasted_iota(jnp.int32, (rows, width), 0)
    out = jnp.zeros((rows, width), jnp.int32)
    for t in range(rows):
        out = jnp.where(row == t, ref[t], out)
    return out


def mask(lists, ids):
    out = jnp.zeros((lists.shape[0], ids.shape[1]), F32)
    for i in range(lists.shape[1]):
        out += jnp.where(lists[:, i : i + 1] == ids, 1.0, 0.0)
    return out


def lanes(n):
    return lax.broadcasted_iota(jnp.int32, (1, n), 1)


def low_lanes(rows):
    return lax.broadcasted_iota(jnp.int32, (rows, 128), 1) < 64


def couple(rows, feats, coefs, masks):
    kh, kl = kern(dot(rows, feats))
    weighted = [coefs * (m * KAPPA) for m in masks]
    weighted = weighted[0] if len(weighted) == 1 else jnp.concatenate(weighted, axis=0)
    return matmul(weighted, kh, kl, NT)


def beside(pair):
    return jnp.where(low_lanes(32), pair[:32], pair[32:])


def kernel(
    rs, pts_in, basis_in, transfer_in, skel_in, near_list_in, near_count_in, inter_list_in, inter_count_in,
    up_t, up_s, up_list_in, up_count_in, out,
    xe, acc, f, ft, t2, bb_h, bb_l, bl_h, bl_l, bu_h, bu_l,
    ce, lh, rh, ftl, ev, et, sv, st, su, fu, tu, ftu, mine, other, zbuf, gc, hc, tc, qh, ql,
    pts, basis, transfer, skel, near_list, near_count, inter_list, inter_count, up_list, up_count,
    in_sem, near_send, near_recv, coef_send, coef_recv, c_send, c_recv, z_send, z_recv, h_send, h_recv,
    y_send, y_recv, x_send, x_recv,
):
    g = lax.axis_index("group")
    b = lax.axis_index("bulk")
    z = lax.rem(lax.div(b, 2), 8)
    y = lax.div(b, 16)
    r = lax.rem(b, 16)
    core = lax.rem(b, 2)
    dev = g * 64 + b

    def at(d):
        d = lax.rem(d + 256, 256)
        return (lax.div(d, 64), lax.rem(d, 64))

    right, left = at(dev + 1), at(dev - 1)

    pairs = (
        (rs, xe.at[0:32, 1024:3072]),
        (pts_in, pts),
        (skel_in, skel),
        (basis_in, basis),
        (transfer_in, transfer),
        (near_list_in, near_list),
        (near_count_in, near_count),
        (inter_list_in, inter_list),
        (inter_count_in, inter_count),
        (up_list_in, up_list),
        (up_count_in, up_count),
        (up_s, sv),
        (up_t.at[:, 128:256], ev.at[0:4096]),
        (up_t.at[:, 0:128], ev.at[4096:8192]),
    )
    loads = [pltpu.make_async_copy(of, to, in_sem.at[i]) for i, (of, to) in enumerate(pairs)]
    for load in loads:
        load.start()
    firsts = (128 + 32 * g, 64 + 16 * g, 32 + 8 * g, 16 + 4 * g, 8 + 2 * g, 4, 2)

    barrier = pltpu.get_barrier_semaphore()

    def greet(device):
        pl.semaphore_signal(barrier, inc=1, device_id=device, device_id_type=MESH)

    greet(right)
    greet(left)

    partner = (g, b + 1 - 2 * core)
    greet(partner)

    def along_z(k):
        return lax.rem(z + k, 8)

    for k in range(1, 8):
        greet((g, y * 16 + along_z(k) * 2 + core))
    for k in range(1, 4):
        greet((g, lax.rem(y + k, 4) * 16 + r))
        greet((lax.rem(g + k, 4), b))

    xe[32:40, 1024:3072] = jnp.zeros((8, 2048), F32)
    loads[1].wait()
    loads[2].wait()
    xe[32:35, 1024:3072] = scaled(pts[...])
    ce[32:40, :] = jnp.zeros((8, 1024), F32)
    order = ((0, 1), (2, 3), (8, 9), (12, 13), (14, 14), (10, 11), (4, 5), (6, 7))
    for i, (m, n) in enumerate(order):
        ce[32:35, i * 128 : i * 128 + 128] = scaled(jnp.concatenate([skel[:, m, :], skel[:, n, :]], axis=1))
    loads[0].wait()
    pl.semaphore_wait(barrier, 16)

    near_copies = [
        pltpu.make_async_remote_copy(
            xe.at[:, 2048:3072], xe.at[:, 0:1024], near_send.at[0], near_recv.at[0],
            device_id=right, device_id_type=MESH,
        ),
        pltpu.make_async_remote_copy(
            xe.at[:, 1024:2048], xe.at[:, 3072:4096], near_send.at[1], near_recv.at[1],
            device_id=left, device_id_type=MESH,
        ),
    ]

    loads[3].wait()
    loads[4].wait()
    bb_h[...], bb_l[...] = halves(basis[...])
    low128 = low_lanes(128)

    def put(to_h, to_l, at_row, value):
        n = value.shape[0]
        to_h[at_row : at_row + n, :], to_l[at_row : at_row + n, :] = halves(value)

    def twice(e):
        return jnp.concatenate([e, e], axis=1)

    for q in range(3):
        for h in range(2):
            e = twice(transfer[q * 256 + h * 128 : q * 256 + h * 128 + 128, :])
            keep = low128 if h == 0 else jnp.logical_not(low128)
            put(bl_h, bl_l, q * 256 + h * 128, jnp.where(keep, e, 0.0))
    put(bl_h, bl_l, 768, twice(transfer[768:896, :]))
    root_e = transfer[896:960, :]
    put(bl_h, bl_l, 896, twice(root_e))

    leaf = []
    for j in range(4):
        two = jnp.concatenate(
            [xe[0:32, 1024 + 512 * j : 1280 + 512 * j], xe[0:32, 1280 + 512 * j : 1536 + 512 * j]], axis=0
        )
        leaf.append(beside(matmul(two, bb_h[128 * j : 128 * j + 128, :], bb_l[128 * j : 128 * j + 128, :], NT)))

    def lift(values, h, low, first):
        joined = values[0] if len(values) == 1 else jnp.concatenate(values, axis=1)
        n = joined.shape[1]
        return matmul(joined, h[first : first + n, :], low[first : first + n, :])

    mid_a = lift(leaf[0:2], bl_h, bl_l, 0)
    mid_b = lift(leaf[2:4], bl_h, bl_l, 256)
    top = lift([mid_a, mid_b], bl_h, bl_l, 512)
    root = lift([top], bl_h, bl_l, 768)
    term = lift([root[:, 0:64]], bl_h, bl_l, 896)
    mine[...] = jnp.where(low_lanes(16), term[0:16], term[16:32])
    core_copy = pltpu.make_async_remote_copy(
        mine, other, c_send, c_recv, device_id=partner, device_id_type=MESH
    )
    core_copy.start()
    for i, value in enumerate((leaf[0], leaf[1], mid_a, top, root, mid_b, leaf[2], leaf[3])):
        ce[0:32, i * 128 : i * 128 + 128] = value
    coef_copies = [
        pltpu.make_async_remote_copy(
            ce.at[:, 384:1024], lh, coef_send.at[0], coef_recv.at[0], device_id=right, device_id_type=MESH
        ),
        pltpu.make_async_remote_copy(
            ce.at[:, 0:640], rh, coef_send.at[1], coef_recv.at[1], device_id=left, device_id_type=MESH
        ),
    ]
    for load in loads[5:11]:
        load.wait()
    near = usable(near_list[...], counted(near_count, 8, 8))
    ids = lanes(4096) // 256
    itself = lax.broadcasted_iota(jnp.int32, (8, 1), 0) + 4 == ids
    t2[...] = (mask(near, ids + (dev * 8 - 4)) + jnp.where(itself, 1.0, 0.0)) * KAPPA
    src, tgt = features(xe[32:40, 1024:3072])
    f[...] = tgt
    ft[1024:3072, :] = as_rows(src)

    core_copy.wait_recv()
    zbuf[z] = mine[...] + other[...]

    def row_copy(k, sender):
        slot = z if sender else along_z(k)
        return pltpu.make_async_remote_copy(
            zbuf.at[slot], zbuf.at[slot], z_send.at[k], z_recv.at[slot],
            device_id=(g, y * 16 + along_z(k) * 2 + core), device_id_type=MESH,
        )

    for k in (4, 3, 5, 2, 6, 1, 7):
        row_copy(k, True).start()
    for copy in coef_copies:
        copy.start()

    def near_leaf(t, first, last, between):
        targets = f[:, t * 256 : t * 256 + 256]
        total = jnp.zeros((32, 256), F32)
        for e in range(first, last):
            part = slice(e * 256, e * 256 + 256)
            x_high, x_low = halves(xe[0:32, part] * t2[t : t + 1, part])
            kh, kl = kern(dot(ft[part, :], targets))
            both = dot(jnp.concatenate([x_high, x_low], axis=0), kh)
            total += both[:32] + both[32:] + dot(x_high, kl)
            between()
        return total

    def spread(chores, blocks):
        state = [0, 0]

        def between():
            state[0] += 1
            until = len(chores) * state[0] // blocks
            for chore in chores[state[1] : until]:
                chore()
            state[1] = until

        return between

    def own_leaf(t, between):
        part = slice(t * 256, t * 256 + 256)
        nugget = NUGGET * xe[0:32, t * 256 + 1024 : t * 256 + 1280]
        acc[:, part] = nugget + near_leaf(t, max(t, 4), min(t + 9, 12), between)

    for load in loads[11:14]:
        load.wait()

    def turn(i):
        first = i // 32 * 4096 + i % 32 * 64
        block = jnp.concatenate([ev[first : first + 64, :], ev[first + 2048 : first + 2112, :]], axis=0)
        et[i * 128 : i * 128 + 128, :] = block.T

    def edge(h, half):
        two = et[pl.ds(half * 4096 + h - (128 if half == 0 else 0), 32, stride=128), :]
        other = pltpu.roll(two, 64, 1)
        low = low_lanes(32)
        return jnp.concatenate([jnp.where(low, two, other), jnp.where(low, other, two)], axis=0)

    low64 = low_lanes(64)

    def put_edge(h, half, to, keep):
        value = edge(h, half)
        put(bu_h, bu_l, to, value if keep is None else jnp.where(keep, value, 0.0))

    nodes = (
        (128 + 32 * g + 8 * y, 0, 0),
        (132 + 32 * g + 8 * y, 0, 256),
        (64 + 16 * g + 4 * y, 1, 512),
        (16 + 4 * g, 1, 896),
        (4, 1, 1280),
    )
    chores = [functools.partial(turn, i) for i in range(64)]
    for first, half, to in nodes:
        for n in range(4):
            keep = low64 if n < 2 else jnp.logical_not(low64)
            chores.append(functools.partial(put_edge, first + n, half, to + n * 64, keep))
    for first, to in ((32 + 8 * g + 2 * y, 768), (8 + 2 * g, 1152)):
        for n in range(2):
            chores.append(functools.partial(put_edge, first + n, 1, to + n * 64, None))
    between = spread(chores, 18)
    for t in range(3):
        own_leaf(t, between)

    for k in range(1, 8):
        row_copy(k, False).wait_recv()
    low16 = low_lanes(16)
    level7 = []
    for j in range(4):
        one, two = zbuf[2 * j], zbuf[2 * j + 1]
        level7.append(
            jnp.concatenate(
                [jnp.where(low16, one, pltpu.roll(two, 64, 1)), jnp.where(low16, pltpu.roll(one, 64, 1), two)], axis=0
            )
        )
    level6 = [lift(level7[0:2], bu_h, bu_l, 0), lift(level7[2:4], bu_h, bu_l, 256)]
    level5 = lift(level6, bu_h, bu_l, 512)
    level4 = lift([level5], bu_h, bu_l, 768)
    hc[y] = level4

    def fourth_copy(k, sender):
        to = lax.rem(y + k, 4)
        slot = y if sender else to
        return pltpu.make_async_remote_copy(
            hc.at[slot], hc.at[slot], h_send.at[k], h_recv.at[slot], device_id=(g, to * 16 + r), device_id_type=MESH
        )

    for k in (2, 1, 3):
        fourth_copy(k, True).start()
    for i, value in enumerate((*level7, *level6, level5)):
        gc[y, :, i * 128 : i * 128 + 128] = value

    def plane_copy(k, sender):
        to = lax.rem(y + k, 4)
        slot = y if sender else to
        return pltpu.make_async_remote_copy(
            gc.at[slot], gc.at[slot], y_send.at[k], y_recv.at[slot], device_id=(g, to * 16 + r), device_id_type=MESH
        )

    for k in (2, 1, 3):
        plane_copy(k, True).start()
    for copy in near_copies:
        copy.start()

    heap = [lax.div(256 + dev, 2 ** (i + 1)) for i in range(7)]
    low3 = lax.broadcasted_iota(jnp.int32, (3, 1, 128), 2) < 64

    def turn_skeleton(c, h):
        block = jnp.concatenate([sv[c * 64 : c * 64 + 64, h * 128 : h * 128 + 128]] * 2, axis=0)
        st[c, h * 128 : h * 128 + 128, :] = block.T

    def put_skeletons(ref, m, n, at_lane):
        pair = jnp.where(low3, st[:, pl.ds(m, 1), :], st[:, pl.ds(n, 1), :])
        ref[0:3, at_lane : at_lane + 128] = scaled(pair.reshape(3, 128))

    def put_features():
        fu[...] = features(su[...], "t")[0]
        ftu[...] = as_rows(features(tu[...], "s")[0])

    last = [jnp.concatenate([root_e, root_e], axis=0)]

    def path_product(i):
        if i > 0:
            last[0] = matmul(last[0], *halves(edge(heap[i - 1], 0 if i == 1 else 1)[:, 0:64]))
        qh[i], ql[i] = halves(last[0])

    su[...] = jnp.zeros((8, 4352), F32)
    tu[...] = jnp.zeros((8, 512), F32)
    skeletons = [functools.partial(turn_skeleton, c, h) for c in range(3) for h in range(2)]
    at_lane = 0
    for first, n in zip(firsts, UPPER):
        for i in range(n // 2):
            skeletons.append(functools.partial(put_skeletons, su, first + 2 * i, first + 2 * i + 1, at_lane))
            at_lane += 128
    for i, (m, n) in enumerate(((0, 1), (2, 3), (4, 5), (6, 6))):
        skeletons.append(functools.partial(put_skeletons, tu, heap[m], heap[n], i * 128))
    skeletons.append(put_features)
    products = [functools.partial(path_product, i) for i in range(7)]
    chores = []
    for i, chore in enumerate(skeletons):
        chores.append(chore)
        if i % 6 == 5 and products:
            chores.append(products.pop(0))
    chores += products
    between = spread(chores, 16)
    for t in range(3, 5):
        own_leaf(t, between)

    for k in range(1, 4):
        fourth_copy(k, False).wait_recv()
    low32 = low_lanes(32)
    level4 = [
        jnp.where(low32, hc[0], hc[1]),
        jnp.where(low32, hc[2], hc[3]),
    ]
    level3 = lift(level4, bu_h, bu_l, 896)
    tc[g] = lift([level3], bu_h, bu_l, 1152)

    def group_copy(k, sender):
        to = lax.rem(g + k, 4)
        slot = g if sender else to
        return pltpu.make_async_remote_copy(
            tc.at[slot], tc.at[slot], x_send.at[k], x_recv.at[slot], device_id=(to, b), device_id_type=MESH
        )

    for k in range(1, 4):
        group_copy(k, True).start()

    for copy in near_copies + coef_copies:
        copy.wait_recv()
    src = features(xe[32:40, 0:1024], "s")[0]
    ft[0:1024, :] = as_rows(src)
    src = features(xe[32:40, 3072:4096], "s")[0]
    ft[3072:4096, :] = as_rows(src)
    ftl[...] = as_rows(features(ce[32:40, :], "s")[0])
    spot = lax.broadcasted_iota(jnp.int32, (8, 15), 1)
    slot = lax.broadcasted_iota(jnp.int32, (8, 15), 0)
    counts = jnp.zeros((8, 15), jnp.int32)
    for n in range(15):
        counts = jnp.where(spot == n, inter_count[n], counts)
    inter = jnp.where(slot < counts, inter_list[...], -1000)

    def listed(n, ids):
        return jnp.sum(jnp.where(inter[:, n : n + 1] == ids, 1.0, 0.0), axis=0, keepdims=True)

    one_ids = jnp.where(lax.rem(lanes(384), 128) < 64, lanes(384) // 128 + (dev - 1), -1)
    tables = (
        ([lh[:, 384:640], ce[:, 0:256], ce[:, 768:1024], rh[:, 0:256]], lanes(1024) // 64 + (dev * 8 - 4)),
        ([lh[:, 256:384], ce[:, 256:384], ce[:, 640:768], rh[:, 256:384]], lanes(512) // 64 + (dev * 4 - 2)),
        ([lh[:, 0:128], ce[:, 384:512], rh[:, 384:512]], lanes(384) // 64 + (dev * 2 - 2)),
        ([lh[:, 128:256], ce[:, 512:640], rh[:, 512:640]], one_ids),
    )
    tables = [(jnp.concatenate(parts, axis=1), ids) for parts, ids in tables]
    tables = [(table[0:32], features(table[32:40], "t")[0], ids) for table, ids in tables]
    fields = {}

    def local_field(level, m, n, at_lane, first, width):
        coefs, feats, ids = tables[level]
        part = slice(first, first + width)
        masks = [listed(m, ids[:, part]), listed(n, ids[:, part])]
        fields[at_lane] = beside(couple(ftl[at_lane : at_lane + 128, :], feats[:, part], coefs[:, part], masks))

    node = lax.broadcasted_iota(jnp.int32, (8, 256), 1)
    up_slots = lax.broadcasted_iota(jnp.int32, (8, 1), 0)
    up_lists = up_list[...].astype(F32)
    path = {}

    def path_kernel(i):
        first, n = sum(UPPER[:i]) * 64, UPPER[i] * 64
        column = jnp.sum(jnp.where(node == heap[i], up_lists, 0.0), axis=1, keepdims=True)
        column = jnp.where(up_slots < up_count[heap[i]], column, -1000.0)
        ids = (lanes(n) // 64 + firsts[i]).astype(F32)
        found = jnp.sum(jnp.where(column == ids, 1.0, 0.0), axis=0, keepdims=True)
        path[i] = (found * KAPPA, *kern(dot(ftu[i * 64 : i * 64 + 64, :], fu[:, first : first + n])))

    def path_field(i, coefs):
        found, kh, kl = path[i]
        return matmul(matmul(coefs * found, kh, kl, NT), qh[i], ql[i], NT)

    incoming = []

    def path_step(i, coefs):
        path_kernel(i)
        incoming.append(path_field(i, coefs()))

    def group_lanes(first, last):
        return lambda: jnp.concatenate([gc[k, :, first:last] for k in range(4)], axis=1)

    chores = [functools.partial(path_kernel, i) for i in (5, 6, 0, 1, 2)] + [
        functools.partial(path_step, 3, lambda: jnp.concatenate(level4, axis=1)),
        functools.partial(path_step, 4, lambda: level3),
        functools.partial(local_field, 3, 14, 14, 512, 0, 384),
        functools.partial(local_field, 2, 12, 13, 384, 0, 384),
        functools.partial(local_field, 1, 8, 9, 256, 0, 384),
        functools.partial(local_field, 1, 10, 11, 640, 128, 384),
    ]
    for j, at_lane in enumerate((0, 128, 768, 896)):
        chores.append(functools.partial(local_field, 0, 2 * j, 2 * j + 1, at_lane, j * 128, 640))
    between = spread(chores, 38)
    for t in range(5, 8):
        own_leaf(t, between)
    for t in range(4):
        acc[:, t * 256 : t * 256 + 256] += near_leaf(t, t, 4, between)
    for t in range(4, 8):
        acc[:, t * 256 : t * 256 + 256] += near_leaf(t, 12, t + 9, between)

    for k in range(1, 4):
        group_copy(k, False).wait_recv()
    level2 = [jnp.where(low32, tc[0], tc[1]), jnp.where(low32, tc[2], tc[3])]
    level1 = lift(level2, bu_h, bu_l, 1280)
    for k in range(1, 4):
        plane_copy(k, False).wait_recv()
    incoming.append(path_field(5, jnp.concatenate(level2, axis=1)))
    incoming.append(path_field(6, level1))
    incoming.append(path_field(0, group_lanes(0, 512)()))
    incoming.append(path_field(1, group_lanes(512, 768)()))
    incoming.append(path_field(2, group_lanes(768, 896)()))
    incoming = sum(incoming[1:], incoming[0])
    field0 = [fields[0], fields[128], fields[768], fields[896]]
    field1 = [fields[256], fields[640]]
    field2, field3 = fields[384], fields[512]

    def lower(value, first, n):
        return matmul(value, bl_h[first : first + n, :], bl_l[first : first + n, :], NT)

    down3 = jnp.where(low32, field3 + incoming, 0.0)
    down2 = field2 + lower(down3, 768, 128)
    down1 = lower(down2, 512, 256)
    down1 = [field1[0] + down1[:, 0:128], field1[1] + down1[:, 128:256]]
    for q in range(2):
        down0 = lower(down1[q], q * 256, 256)
        for h in range(2):
            j = 2 * q + h
            pair = field0[j] + down0[:, h * 128 : h * 128 + 128]
            two = jnp.concatenate([jnp.where(low32, pair, 0.0), jnp.where(low32, 0.0, pair)], axis=0)
            far = matmul(two, bb_h[128 * j : 128 * j + 128, :], bb_l[128 * j : 128 * j + 128, :])
            for k in range(2):
                part = slice((2 * j + k) * 256, (2 * j + k) * 256 + 256)
                out[:, part] = acc[:, part] + far[32 * k : 32 * k + 32]

    for copy in near_copies + coef_copies:
        copy.wait_send()

    core_copy.wait_send()
    for k in range(1, 8):
        row_copy(k, True).wait_send()
    for k in range(1, 4):
        fourth_copy(k, True).wait_send()
        plane_copy(k, True).wait_send()
        group_copy(k, True).wait_send()


def on_device(
    rs, pts, basis, transfer, skel, near_list, near_count, inter_list, inter_count, up_t, up_s, up_list, up_count
):
    vmem = pl.BlockSpec(memory_space=pltpu.VMEM)
    anywhere = pl.BlockSpec(memory_space=pl.ANY)
    dma = pltpu.SemaphoreType.DMA
    return pl.pallas_call(
        kernel,
        out_shape=jax.ShapeDtypeStruct((32, 2048), F32),
        in_specs=[anywhere] * 13,
        out_specs=vmem,
        scratch_shapes=[
            pltpu.VMEM((40, 4096), F32),
            pltpu.VMEM((32, 2048), F32),
            pltpu.VMEM((FEATS, 2048), BF16),
            pltpu.VMEM((4096, FEATS), BF16),
            pltpu.VMEM((8, 4096), F32),
            pltpu.VMEM((512, 256), BF16),
            pltpu.VMEM((512, 256), BF16),
            pltpu.VMEM((960, 128), BF16),
            pltpu.VMEM((960, 128), BF16),
            pltpu.VMEM((1536, 128), BF16),
            pltpu.VMEM((1536, 128), BF16),
            pltpu.VMEM((40, 1024), F32),
            pltpu.VMEM((40, 640), F32),
            pltpu.VMEM((40, 640), F32),
            pltpu.VMEM((1024, FEATS), BF16),
            pltpu.VMEM((8192, 128), F32),
            pltpu.VMEM((8192, 128), F32),
            pltpu.VMEM((192, 256), F32),
            pltpu.VMEM((3, 256, 128), F32),
            pltpu.VMEM((8, 4352), F32),
            pltpu.VMEM((FEATS, 4352), BF16),
            pltpu.VMEM((8, 512), F32),
            pltpu.VMEM((512, FEATS), BF16),
            pltpu.VMEM((16, 128), F32),
            pltpu.VMEM((16, 128), F32),
            pltpu.VMEM((8, 16, 128), F32),
            pltpu.VMEM((4, 32, 896), F32),
            pltpu.VMEM((4, 32, 128), F32),
            pltpu.VMEM((4, 32, 128), F32),
            pltpu.VMEM((7, 128, 64), BF16),
            pltpu.VMEM((7, 128, 64), BF16),
            pltpu.VMEM((3, 2048), F32),
            pltpu.VMEM((512, 256), F32),
            pltpu.VMEM((960, 64), F32),
            pltpu.VMEM((3, 15, 64), F32),
            pltpu.VMEM((8, 8), jnp.int32),
            pltpu.SMEM((8,), jnp.int32),
            pltpu.VMEM((8, 15), jnp.int32),
            pltpu.SMEM((15,), jnp.int32),
            pltpu.VMEM((8, 256), jnp.int32),
            pltpu.SMEM((256,), jnp.int32),
            dma((14,)),
            dma((2,)), dma((2,)), dma((2,)), dma((2,)),
            dma, dma, dma((8,)), dma((8,)), dma((4,)), dma((4,)), dma((4,)), dma((4,)), dma((4,)), dma((4,)),
        ],
        compiler_params=pltpu.CompilerParams(
            collective_id=0, has_side_effects=True, vmem_limit_bytes=58 * 2**20
        ),
    )(
        rs, pts, basis.reshape(512, 256), transfer.reshape(960, 64), skel.transpose(1, 0, 2), near_list, near_count,
        inter_list.T, inter_count, up_t.transpose(1, 2, 0).reshape(4096, 256), up_s.transpose(1, 2, 0).reshape(192, 256),
        up_list.T, up_count,
    )


def solution(mesh):
    both = ("group", "bulk")
    in_specs = (
        P(None, both),
        P(None, both),
        P(both, None, None),
        P(both, None, None),
        P(both, None, None),
        P(both, None),
        P(both),
        P(both, None),
        P(both),
        P(),
        P(),
        P(),
        P(),
    )
    return jax.shard_map(
        on_device, mesh=mesh, in_specs=in_specs, out_specs=P(None, both), check_vma=False
    )
```

```python
import functools
import math

import jax
import jax.numpy as jnp
from jax import lax
from jax.experimental import pallas as pl
from jax.experimental.pallas import tpu as pltpu
from jax.sharding import PartitionSpec as P

F32 = jnp.float32
BF16 = jnp.bfloat16
MESH = pl.DeviceIdType.MESH
NN = (((1,), (0,)), ((), ()))
NT = (((1,), (1,)), ((), ()))

ALPHA = 2.0 / math.log(2.0)
KAPPA = 0.2 * math.log(2.0)
SHIFT = 1.0 / math.log(2.0)
SOFT = 0.01 * ALPHA * ALPHA
CENTER = 2.0
NUGGET = 0.5
FEATS = 48
UPPER = (32, 16, 8, 4, 2, 4, 2)


def dot(a, b, dims=NN):
    return lax.dot_general(a, b, dims, preferred_element_type=F32)


def halves(x):
    high = x.astype(BF16)
    return high, (x - high.astype(F32)).astype(BF16)


def matmul(a, high, low, dims=NN):
    m = a.shape[0]
    a_high, a_low = halves(a)
    both = dot(jnp.concatenate([a_high, a_low], axis=0), high, dims)
    return both[:m] + both[m:] + dot(a_high, low, dims)


def kern(w):
    y = w * lax.rsqrt(w)
    return halves((SHIFT + y) * jnp.exp2(-y))


def in_three(x):
    one = x.astype(BF16).astype(F32)
    rest = x - one
    two = rest.astype(BF16).astype(F32)
    return one, two, (rest - two).astype(BF16).astype(F32)


def scaled(x):
    return ALPHA * (x - CENTER)


def features(u, sides="st"):
    row = lax.broadcasted_iota(jnp.int32, u.shape, 0)
    square = jnp.sum(u * u, axis=0, keepdims=True)
    out = []
    if "s" in sides:
        s = jnp.where(row < 3, -2.0 * u, jnp.where(row == 3, square, jnp.where(row == 4, 1.0, 0.0)))
        a, b, c = in_three(s)
        out.append(jnp.concatenate([a, a, b, b, a, c], axis=0))
    if "t" in sides:
        t = jnp.where(row < 3, u, jnp.where(row == 3, 1.0, jnp.where(row == 4, square + SOFT, 0.0)))
        a, b, c = in_three(t)
        out.append(jnp.concatenate([a, b, a, b, c, a], axis=0).astype(BF16))
    return out


def as_rows(f):
    return f.T.astype(BF16)


def usable(values, counts):
    slot = lax.broadcasted_iota(jnp.int32, values.shape, 1)
    return jnp.where(slot < counts, values, -1000)


def counted(ref, rows, width):
    row = lax.broadcasted_iota(jnp.int32, (rows, width), 0)
    out = jnp.zeros((rows, width), jnp.int32)
    for t in range(rows):
        out = jnp.where(row == t, ref[t], out)
    return out


def mask(lists, ids):
    out = jnp.zeros((lists.shape[0], ids.shape[1]), F32)
    for i in range(lists.shape[1]):
        out += jnp.where(lists[:, i : i + 1] == ids, 1.0, 0.0)
    return out


def lanes(n):
    return lax.broadcasted_iota(jnp.int32, (1, n), 1)


def low_lanes(rows):
    return lax.broadcasted_iota(jnp.int32, (rows, 128), 1) < 64


def couple(rows, feats, coefs, masks):
    kh, kl = kern(dot(rows, feats))
    weighted = [coefs * (m * KAPPA) for m in masks]
    weighted = weighted[0] if len(weighted) == 1 else jnp.concatenate(weighted, axis=0)
    return matmul(weighted, kh, kl, NT)


def beside(pair):
    return jnp.where(low_lanes(32), pair[:32], pair[32:])


def kernel(
    rs, pts_in, basis_in, transfer_in, skel_in, near_list_in, near_count_in, inter_list_in, inter_count_in,
    up_t, up_s, up_list_in, up_count_in, out,
    xe, acc, f, ft, t2, bb_h, bb_l, bl_h, bl_l, bu_h, bu_l,
    ce, lh, rh, ftl, ev, et, sv, st, su, fu, tu, ftu, mine, other, zbuf, gc, hc, tc, qh, ql,
    pts, basis, transfer, skel, near_list, near_count, inter_list, inter_count, up_list, up_count,
    in_sem, near_send, near_recv, coef_send, coef_recv, c_send, c_recv, z_send, z_recv, h_send, h_recv,
    y_send, y_recv, x_send, x_recv,
):
    g = lax.axis_index("group")
    b = lax.axis_index("bulk")
    z = lax.rem(lax.div(b, 2), 8)
    y = lax.div(b, 16)
    r = lax.rem(b, 16)
    core = lax.rem(b, 2)
    dev = g * 64 + b

    def at(d):
        d = lax.rem(d + 256, 256)
        return (lax.div(d, 64), lax.rem(d, 64))

    right, left = at(dev + 1), at(dev - 1)

    pairs = (
        (rs, xe.at[0:32, 1024:3072]),
        (pts_in, pts),
        (skel_in, skel),
        (basis_in, basis),
        (transfer_in, transfer),
        (near_list_in, near_list),
        (near_count_in, near_count),
        (inter_list_in, inter_list),
        (inter_count_in, inter_count),
        (up_list_in, up_list),
        (up_count_in, up_count),
        (up_s, sv),
        (up_t.at[:, 128:256], ev.at[0:4096]),
        (up_t.at[:, 0:128], ev.at[4096:8192]),
    )
    loads = [pltpu.make_async_copy(of, to, in_sem.at[i]) for i, (of, to) in enumerate(pairs)]
    for load in loads:
        load.start()
    firsts = (128 + 32 * g, 64 + 16 * g, 32 + 8 * g, 16 + 4 * g, 8 + 2 * g, 4, 2)

    barrier = pltpu.get_barrier_semaphore()

    def greet(device):
        pl.semaphore_signal(barrier, inc=1, device_id=device, device_id_type=MESH)

    greet(right)
    greet(left)

    partner = (g, b + 1 - 2 * core)
    greet(partner)

    def along_z(k):
        return lax.rem(z + k, 8)

    for k in range(1, 8):
        greet((g, y * 16 + along_z(k) * 2 + core))
    for k in range(1, 4):
        greet((g, lax.rem(y + k, 4) * 16 + r))
        greet((lax.rem(g + k, 4), b))

    xe[32:40, 1024:3072] = jnp.zeros((8, 2048), F32)
    loads[1].wait()
    loads[2].wait()
    xe[32:35, 1024:3072] = scaled(pts[...])
    ce[32:40, :] = jnp.zeros((8, 1024), F32)
    order = ((0, 1), (2, 3), (8, 9), (12, 13), (14, 14), (10, 11), (4, 5), (6, 7))
    for i, (m, n) in enumerate(order):
        ce[32:35, i * 128 : i * 128 + 128] = scaled(jnp.concatenate([skel[:, m, :], skel[:, n, :]], axis=1))
    loads[0].wait()

    near_copies = [
        pltpu.make_async_remote_copy(
            xe.at[:, 2048:3072], xe.at[:, 0:1024], near_send.at[0], near_recv.at[0],
            device_id=right, device_id_type=MESH,
        ),
        pltpu.make_async_remote_copy(
            xe.at[:, 1024:2048], xe.at[:, 3072:4096], near_send.at[1], near_recv.at[1],
            device_id=left, device_id_type=MESH,
        ),
    ]

    loads[3].wait()
    loads[4].wait()
    bb_h[...], bb_l[...] = halves(basis[...])
    low128 = low_lanes(128)

    def put(to_h, to_l, at_row, value):
        n = value.shape[0]
        to_h[at_row : at_row + n, :], to_l[at_row : at_row + n, :] = halves(value)

    def twice(e):
        return jnp.concatenate([e, e], axis=1)

    for q in range(3):
        for h in range(2):
            e = twice(transfer[q * 256 + h * 128 : q * 256 + h * 128 + 128, :])
            keep = low128 if h == 0 else jnp.logical_not(low128)
            put(bl_h, bl_l, q * 256 + h * 128, jnp.where(keep, e, 0.0))
    put(bl_h, bl_l, 768, twice(transfer[768:896, :]))
    root_e = transfer[896:960, :]
    put(bl_h, bl_l, 896, twice(root_e))

    leaf = []
    for j in range(4):
        two = jnp.concatenate(
            [xe[0:32, 1024 + 512 * j : 1280 + 512 * j], xe[0:32, 1280 + 512 * j : 1536 + 512 * j]], axis=0
        )
        leaf.append(beside(matmul(two, bb_h[128 * j : 128 * j + 128, :], bb_l[128 * j : 128 * j + 128, :], NT)))

    def lift(values, h, low, first):
        joined = values[0] if len(values) == 1 else jnp.concatenate(values, axis=1)
        n = joined.shape[1]
        return matmul(joined, h[first : first + n, :], low[first : first + n, :])

    mid_a = lift(leaf[0:2], bl_h, bl_l, 0)
    mid_b = lift(leaf[2:4], bl_h, bl_l, 256)
    top = lift([mid_a, mid_b], bl_h, bl_l, 512)
    root = lift([top], bl_h, bl_l, 768)
    term = lift([root[:, 0:64]], bl_h, bl_l, 896)
    mine[...] = jnp.where(low_lanes(16), term[0:16], term[16:32])
    core_copy = pltpu.make_async_remote_copy(
        mine, other, c_send, c_recv, device_id=partner, device_id_type=MESH
    )
    pl.semaphore_wait(barrier, 16)
    core_copy.start()
    for i, value in enumerate((leaf[0], leaf[1], mid_a, top, root, mid_b, leaf[2], leaf[3])):
        ce[0:32, i * 128 : i * 128 + 128] = value
    coef_copies = [
        pltpu.make_async_remote_copy(
            ce.at[:, 384:1024], lh, coef_send.at[0], coef_recv.at[0], device_id=right, device_id_type=MESH
        ),
        pltpu.make_async_remote_copy(
            ce.at[:, 0:640], rh, coef_send.at[1], coef_recv.at[1], device_id=left, device_id_type=MESH
        ),
    ]
    for load in loads[5:11]:
        load.wait()
    near = usable(near_list[...], counted(near_count, 8, 8))
    ids = lanes(4096) // 256
    itself = lax.broadcasted_iota(jnp.int32, (8, 1), 0) + 4 == ids
    t2[...] = (mask(near, ids + (dev * 8 - 4)) + jnp.where(itself, 1.0, 0.0)) * KAPPA
    src, tgt = features(xe[32:40, 1024:3072])
    f[...] = tgt
    ft[1024:3072, :] = as_rows(src)

    core_copy.wait_recv()
    zbuf[z] = mine[...] + other[...]

    def row_copy(k, sender):
        slot = z if sender else along_z(k)
        return pltpu.make_async_remote_copy(
            zbuf.at[slot], zbuf.at[slot], z_send.at[k], z_recv.at[slot],
            device_id=(g, y * 16 + along_z(k) * 2 + core), device_id_type=MESH,
        )

    for k in (4, 3, 5, 2, 6, 1, 7):
        row_copy(k, True).start()
    for copy in coef_copies:
        copy.start()

    def near_leaf(t, first, last, between):
        targets = f[:, t * 256 : t * 256 + 256]
        total = jnp.zeros((32, 256), F32)
        for e in range(first, last):
            part = slice(e * 256, e * 256 + 256)
            x_high, x_low = halves(xe[0:32, part] * t2[t : t + 1, part])
            kh, kl = kern(dot(ft[part, :], targets))
            both = dot(jnp.concatenate([x_high, x_low], axis=0), kh)
            total += both[:32] + both[32:] + dot(x_high, kl)
            between()
        return total

    def spread(chores, blocks):
        state = [0, 0]

        def between():
            state[0] += 1
            until = len(chores) * state[0] // blocks
            for chore in chores[state[1] : until]:
                chore()
            state[1] = until

        return between

    def own_leaf(t, between):
        part = slice(t * 256, t * 256 + 256)
        nugget = NUGGET * xe[0:32, t * 256 + 1024 : t * 256 + 1280]
        acc[:, part] = nugget + near_leaf(t, max(t, 4), min(t + 9, 12), between)

    for load in loads[11:14]:
        load.wait()

    def turn(i):
        first = i // 32 * 4096 + i % 32 * 64
        block = jnp.concatenate([ev[first : first + 64, :], ev[first + 2048 : first + 2112, :]], axis=0)
        et[i * 128 : i * 128 + 128, :] = block.T

    def edge(h, half):
        two = et[pl.ds(half * 4096 + h - (128 if half == 0 else 0), 32, stride=128), :]
        other = pltpu.roll(two, 64, 1)
        low = low_lanes(32)
        return jnp.concatenate([jnp.where(low, two, other), jnp.where(low, other, two)], axis=0)

    low64 = low_lanes(64)

    def put_edge(h, half, to, keep):
        value = edge(h, half)
        put(bu_h, bu_l, to, value if keep is None else jnp.where(keep, value, 0.0))

    nodes = (
        (128 + 32 * g + 8 * y, 0, 0),
        (132 + 32 * g + 8 * y, 0, 256),
        (64 + 16 * g + 4 * y, 1, 512),
        (16 + 4 * g, 1, 896),
        (4, 1, 1280),
    )
    chores = [functools.partial(turn, i) for i in range(64)]
    for first, half, to in nodes:
        for n in range(4):
            keep = low64 if n < 2 else jnp.logical_not(low64)
            chores.append(functools.partial(put_edge, first + n, half, to + n * 64, keep))
    for first, to in ((32 + 8 * g + 2 * y, 768), (8 + 2 * g, 1152)):
        for n in range(2):
            chores.append(functools.partial(put_edge, first + n, 1, to + n * 64, None))
    between = spread(chores, 18)
    for t in range(3):
        own_leaf(t, between)

    for k in range(1, 8):
        row_copy(k, False).wait_recv()
    low16 = low_lanes(16)
    level7 = []
    for j in range(4):
        one, two = zbuf[2 * j], zbuf[2 * j + 1]
        level7.append(
            jnp.concatenate(
                [jnp.where(low16, one, pltpu.roll(two, 64, 1)), jnp.where(low16, pltpu.roll(one, 64, 1), two)], axis=0
            )
        )
    level6 = [lift(level7[0:2], bu_h, bu_l, 0), lift(level7[2:4], bu_h, bu_l, 256)]
    level5 = lift(level6, bu_h, bu_l, 512)
    level4 = lift([level5], bu_h, bu_l, 768)
    hc[y] = level4

    def fourth_copy(k, sender):
        to = lax.rem(y + k, 4)
        slot = y if sender else to
        return pltpu.make_async_remote_copy(
            hc.at[slot], hc.at[slot], h_send.at[k], h_recv.at[slot], device_id=(g, to * 16 + r), device_id_type=MESH
        )

    for k in (2, 1, 3):
        fourth_copy(k, True).start()
    for i, value in enumerate((*level7, *level6, level5)):
        gc[y, :, i * 128 : i * 128 + 128] = value

    def plane_copy(k, sender):
        to = lax.rem(y + k, 4)
        slot = y if sender else to
        return pltpu.make_async_remote_copy(
            gc.at[slot], gc.at[slot], y_send.at[k], y_recv.at[slot], device_id=(g, to * 16 + r), device_id_type=MESH
        )

    for k in (2, 1, 3):
        plane_copy(k, True).start()
    for copy in near_copies:
        copy.start()

    heap = [lax.div(256 + dev, 2 ** (i + 1)) for i in range(7)]
    low1 = lanes(128) < 64

    def turn_skeleton(c, h):
        block = jnp.concatenate([sv[c * 64 : c * 64 + 64, h * 128 : h * 128 + 128]] * 2, axis=0)
        st[c, h * 128 : h * 128 + 128, :] = block.T

    def put_skeletons(ref, m, n, at_lane):
        for c in range(3):
            pair = jnp.where(low1, st[c, pl.ds(m, 1), :], st[c, pl.ds(n, 1), :])
            ref[c : c + 1, at_lane : at_lane + 128] = scaled(pair)

    def put_features():
        fu[...] = features(su[...], "t")[0]
        ftu[...] = as_rows(features(tu[...], "s")[0])

    last = [jnp.concatenate([root_e, root_e], axis=0)]

    def path_product(i):
        if i > 0:
            last[0] = matmul(last[0], *halves(edge(heap[i - 1], 0 if i == 1 else 1)[:, 0:64]))
        qh[i], ql[i] = halves(last[0])

    su[...] = jnp.zeros((8, 4352), F32)
    tu[...] = jnp.zeros((8, 512), F32)
    skeletons = [functools.partial(turn_skeleton, c, h) for c in range(3) for h in range(2)]
    at_lane = 0
    for first, n in zip(firsts, UPPER):
        for i in range(n // 2):
            skeletons.append(functools.partial(put_skeletons, su, first + 2 * i, first + 2 * i + 1, at_lane))
            at_lane += 128
    for i, (m, n) in enumerate(((0, 1), (2, 3), (4, 5), (6, 6))):
        skeletons.append(functools.partial(put_skeletons, tu, heap[m], heap[n], i * 128))
    skeletons.append(put_features)
    products = [functools.partial(path_product, i) for i in range(7)]
    chores = []
    for i, chore in enumerate(skeletons):
        chores.append(chore)
        if i % 6 == 5 and products:
            chores.append(products.pop(0))
    chores += products
    between = spread(chores, 16)
    for t in range(3, 5):
        own_leaf(t, between)

    for k in range(1, 4):
        fourth_copy(k, False).wait_recv()
    low32 = low_lanes(32)
    level4 = [
        jnp.where(low32, hc[0], hc[1]),
        jnp.where(low32, hc[2], hc[3]),
    ]
    level3 = lift(level4, bu_h, bu_l, 896)
    tc[g] = lift([level3], bu_h, bu_l, 1152)

    def group_copy(k, sender):
        to = lax.rem(g + k, 4)
        slot = g if sender else to
        return pltpu.make_async_remote_copy(
            tc.at[slot], tc.at[slot], x_send.at[k], x_recv.at[slot], device_id=(to, b), device_id_type=MESH
        )

    for k in range(1, 4):
        group_copy(k, True).start()

    for copy in near_copies + coef_copies:
        copy.wait_recv()
    src = features(xe[32:40, 0:1024], "s")[0]
    ft[0:1024, :] = as_rows(src)
    src = features(xe[32:40, 3072:4096], "s")[0]
    ft[3072:4096, :] = as_rows(src)
    ftl[...] = as_rows(features(ce[32:40, :], "s")[0])
    spot = lax.broadcasted_iota(jnp.int32, (8, 15), 1)
    slot = lax.broadcasted_iota(jnp.int32, (8, 15), 0)
    counts = jnp.zeros((8, 15), jnp.int32)
    for n in range(15):
        counts = jnp.where(spot == n, inter_count[n], counts)
    inter = jnp.where(slot < counts, inter_list[...], -1000)

    def listed(n, ids):
        return jnp.sum(jnp.where(inter[:, n : n + 1] == ids, 1.0, 0.0), axis=0, keepdims=True)

    one_ids = jnp.where(lax.rem(lanes(384), 128) < 64, lanes(384) // 128 + (dev - 1), -1)
    tables = (
        ([lh[:, 384:640], ce[:, 0:256], ce[:, 768:1024], rh[:, 0:256]], lanes(1024) // 64 + (dev * 8 - 4)),
        ([lh[:, 256:384], ce[:, 256:384], ce[:, 640:768], rh[:, 256:384]], lanes(512) // 64 + (dev * 4 - 2)),
        ([lh[:, 0:128], ce[:, 384:512], rh[:, 384:512]], lanes(384) // 64 + (dev * 2 - 2)),
        ([lh[:, 128:256], ce[:, 512:640], rh[:, 512:640]], one_ids),
    )
    tables = [(jnp.concatenate(parts, axis=1), ids) for parts, ids in tables]
    tables = [(table[0:32], features(table[32:40], "t")[0], ids) for table, ids in tables]
    fields = {}

    def local_field(level, m, n, at_lane, first, width):
        coefs, feats, ids = tables[level]
        part = slice(first, first + width)
        masks = [listed(m, ids[:, part]), listed(n, ids[:, part])]
        fields[at_lane] = beside(couple(ftl[at_lane : at_lane + 128, :], feats[:, part], coefs[:, part], masks))

    node = lax.broadcasted_iota(jnp.int32, (8, 256), 1)
    up_slots = lax.broadcasted_iota(jnp.int32, (8, 1), 0)
    up_lists = up_list[...].astype(F32)
    path = {}

    def path_kernel(i):
        first, n = sum(UPPER[:i]) * 64, UPPER[i] * 64
        column = jnp.sum(jnp.where(node == heap[i], up_lists, 0.0), axis=1, keepdims=True)
        column = jnp.where(up_slots < up_count[heap[i]], column, -1000.0)
        ids = (lanes(n) // 64 + firsts[i]).astype(F32)
        found = jnp.sum(jnp.where(column == ids, 1.0, 0.0), axis=0, keepdims=True)
        path[i] = (found * KAPPA, *kern(dot(ftu[i * 64 : i * 64 + 64, :], fu[:, first : first + n])))

    def path_field(i, coefs):
        found, kh, kl = path[i]
        return matmul(matmul(coefs * found, kh, kl, NT), qh[i], ql[i], NT)

    incoming = []

    def path_step(i, coefs):
        path_kernel(i)
        incoming.append(path_field(i, coefs()))

    def group_lanes(first, last):
        return lambda: jnp.concatenate([gc[k, :, first:last] for k in range(4)], axis=1)

    chores = [functools.partial(path_kernel, i) for i in (5, 6, 0, 1, 2)] + [
        functools.partial(path_step, 3, lambda: jnp.concatenate(level4, axis=1)),
        functools.partial(path_step, 4, lambda: level3),
        functools.partial(local_field, 3, 14, 14, 512, 0, 384),
        functools.partial(local_field, 2, 12, 13, 384, 0, 384),
        functools.partial(local_field, 1, 8, 9, 256, 0, 384),
        functools.partial(local_field, 1, 10, 11, 640, 128, 384),
    ]
    for j, at_lane in enumerate((0, 128, 768, 896)):
        chores.append(functools.partial(local_field, 0, 2 * j, 2 * j + 1, at_lane, j * 128, 640))
    between = spread(chores, 38)
    for t in range(5, 8):
        own_leaf(t, between)
    for t in range(4):
        acc[:, t * 256 : t * 256 + 256] += near_leaf(t, t, 4, between)
    for t in range(4, 8):
        acc[:, t * 256 : t * 256 + 256] += near_leaf(t, 12, t + 9, between)

    for k in range(1, 4):
        group_copy(k, False).wait_recv()
    level2 = [jnp.where(low32, tc[0], tc[1]), jnp.where(low32, tc[2], tc[3])]
    level1 = lift(level2, bu_h, bu_l, 1280)
    for k in range(1, 4):
        plane_copy(k, False).wait_recv()
    incoming.append(path_field(5, jnp.concatenate(level2, axis=1)))
    incoming.append(path_field(6, level1))
    incoming.append(path_field(0, group_lanes(0, 512)()))
    incoming.append(path_field(1, group_lanes(512, 768)()))
    incoming.append(path_field(2, group_lanes(768, 896)()))
    incoming = sum(incoming[1:], incoming[0])
    field0 = [fields[0], fields[128], fields[768], fields[896]]
    field1 = [fields[256], fields[640]]
    field2, field3 = fields[384], fields[512]

    def lower(value, first, n):
        return matmul(value, bl_h[first : first + n, :], bl_l[first : first + n, :], NT)

    down3 = jnp.where(low32, field3 + incoming, 0.0)
    down2 = field2 + lower(down3, 768, 128)
    down1 = lower(down2, 512, 256)
    down1 = [field1[0] + down1[:, 0:128], field1[1] + down1[:, 128:256]]
    for q in range(2):
        down0 = lower(down1[q], q * 256, 256)
        for h in range(2):
            j = 2 * q + h
            pair = field0[j] + down0[:, h * 128 : h * 128 + 128]
            two = jnp.concatenate([jnp.where(low32, pair, 0.0), jnp.where(low32, 0.0, pair)], axis=0)
            far = matmul(two, bb_h[128 * j : 128 * j + 128, :], bb_l[128 * j : 128 * j + 128, :])
            for k in range(2):
                part = slice((2 * j + k) * 256, (2 * j + k) * 256 + 256)
                out[:, part] = acc[:, part] + far[32 * k : 32 * k + 32]

    for copy in near_copies + coef_copies:
        copy.wait_send()

    core_copy.wait_send()
    for k in range(1, 8):
        row_copy(k, True).wait_send()
    for k in range(1, 4):
        fourth_copy(k, True).wait_send()
        plane_copy(k, True).wait_send()
        group_copy(k, True).wait_send()


def on_device(
    rs, pts, basis, transfer, skel, near_list, near_count, inter_list, inter_count, up_t, up_s, up_list, up_count
):
    vmem = pl.BlockSpec(memory_space=pltpu.VMEM)
    anywhere = pl.BlockSpec(memory_space=pl.ANY)
    dma = pltpu.SemaphoreType.DMA
    return pl.pallas_call(
        kernel,
        out_shape=jax.ShapeDtypeStruct((32, 2048), F32),
        in_specs=[anywhere] * 13,
        out_specs=vmem,
        scratch_shapes=[
            pltpu.VMEM((40, 4096), F32),
            pltpu.VMEM((32, 2048), F32),
            pltpu.VMEM((FEATS, 2048), BF16),
            pltpu.VMEM((4096, FEATS), BF16),
            pltpu.VMEM((8, 4096), F32),
            pltpu.VMEM((512, 256), BF16),
            pltpu.VMEM((512, 256), BF16),
            pltpu.VMEM((960, 128), BF16),
            pltpu.VMEM((960, 128), BF16),
            pltpu.VMEM((1536, 128), BF16),
            pltpu.VMEM((1536, 128), BF16),
            pltpu.VMEM((40, 1024), F32),
            pltpu.VMEM((40, 640), F32),
            pltpu.VMEM((40, 640), F32),
            pltpu.VMEM((1024, FEATS), BF16),
            pltpu.VMEM((8192, 128), F32),
            pltpu.VMEM((8192, 128), F32),
            pltpu.VMEM((192, 256), F32),
            pltpu.VMEM((3, 256, 128), F32),
            pltpu.VMEM((8, 4352), F32),
            pltpu.VMEM((FEATS, 4352), BF16),
            pltpu.VMEM((8, 512), F32),
            pltpu.VMEM((512, FEATS), BF16),
            pltpu.VMEM((16, 128), F32),
            pltpu.VMEM((16, 128), F32),
            pltpu.VMEM((8, 16, 128), F32),
            pltpu.VMEM((4, 32, 896), F32),
            pltpu.VMEM((4, 32, 128), F32),
            pltpu.VMEM((4, 32, 128), F32),
            pltpu.VMEM((7, 128, 64), BF16),
            pltpu.VMEM((7, 128, 64), BF16),
            pltpu.VMEM((3, 2048), F32),
            pltpu.VMEM((512, 256), F32),
            pltpu.VMEM((960, 64), F32),
            pltpu.VMEM((3, 15, 64), F32),
            pltpu.VMEM((8, 8), jnp.int32),
            pltpu.SMEM((8,), jnp.int32),
            pltpu.VMEM((8, 15), jnp.int32),
            pltpu.SMEM((15,), jnp.int32),
            pltpu.VMEM((8, 256), jnp.int32),
            pltpu.SMEM((256,), jnp.int32),
            dma((14,)),
            dma((2,)), dma((2,)), dma((2,)), dma((2,)),
            dma, dma, dma((8,)), dma((8,)), dma((4,)), dma((4,)), dma((4,)), dma((4,)), dma((4,)), dma((4,)),
        ],
        compiler_params=pltpu.CompilerParams(
            collective_id=0, has_side_effects=True, vmem_limit_bytes=58 * 2**20
        ),
    )(
        rs, pts, basis.reshape(512, 256), transfer.reshape(960, 64), skel.transpose(1, 0, 2), near_list, near_count,
        inter_list.T, inter_count, up_t.transpose(1, 2, 0).reshape(4096, 256), up_s.transpose(1, 2, 0).reshape(192, 256),
        up_list.T, up_count,
    )


def solution(mesh):
    both = ("group", "bulk")
    in_specs = (
        P(None, both),
        P(None, both),
        P(both, None, None),
        P(both, None, None),
        P(both, None, None),
        P(both, None),
        P(both),
        P(both, None),
        P(both),
        P(),
        P(),
        P(),
        P(),
    )
    return jax.shard_map(
        on_device, mesh=mesh, in_specs=in_specs, out_specs=P(None, both), check_vma=False
    )
```

```python
import functools
import math

import jax
import jax.numpy as jnp
from jax import lax
from jax.experimental import pallas as pl
from jax.experimental.pallas import tpu as pltpu
from jax.sharding import PartitionSpec as P

F32 = jnp.float32
BF16 = jnp.bfloat16
MESH = pl.DeviceIdType.MESH
NN = (((1,), (0,)), ((), ()))
NT = (((1,), (1,)), ((), ()))

ALPHA = 2.0 / math.log(2.0)
KAPPA = 0.2 * math.log(2.0)
SHIFT = 1.0 / math.log(2.0)
SOFT = 0.01 * ALPHA * ALPHA
CENTER = 2.0
NUGGET = 0.5
FEATS = 48
UPPER = (32, 16, 8, 4, 2, 4, 2)


def dot(a, b, dims=NN):
    return lax.dot_general(a, b, dims, preferred_element_type=F32)


def halves(x):
    high = x.astype(BF16)
    return high, (x - high.astype(F32)).astype(BF16)


def matmul(a, high, low, dims=NN):
    m = a.shape[0]
    a_high, a_low = halves(a)
    both = dot(jnp.concatenate([a_high, a_low], axis=0), high, dims)
    return both[:m] + both[m:] + dot(a_high, low, dims)


def kern(w):
    y = w * lax.rsqrt(w)
    return halves((SHIFT + y) * jnp.exp2(-y))


def in_three(x):
    one = x.astype(BF16).astype(F32)
    rest = x - one
    two = rest.astype(BF16).astype(F32)
    return one, two, (rest - two).astype(BF16).astype(F32)


def scaled(x):
    return ALPHA * (x - CENTER)


def features(u, sides="st"):
    row = lax.broadcasted_iota(jnp.int32, u.shape, 0)
    square = jnp.sum(u * u, axis=0, keepdims=True)
    out = []
    if "s" in sides:
        s = jnp.where(row < 3, -2.0 * u, jnp.where(row == 3, square, jnp.where(row == 4, 1.0, 0.0)))
        a, b, c = in_three(s)
        out.append(jnp.concatenate([a, a, b, b, a, c], axis=0))
    if "t" in sides:
        t = jnp.where(row < 3, u, jnp.where(row == 3, 1.0, jnp.where(row == 4, square + SOFT, 0.0)))
        a, b, c = in_three(t)
        out.append(jnp.concatenate([a, b, a, b, c, a], axis=0).astype(BF16))
    return out


def as_rows(f):
    return f.T.astype(BF16)


def usable(values, counts):
    slot = lax.broadcasted_iota(jnp.int32, values.shape, 1)
    return jnp.where(slot < counts, values, -1000)


def counted(ref, rows, width):
    row = lax.broadcasted_iota(jnp.int32, (rows, width), 0)
    out = jnp.zeros((rows, width), jnp.int32)
    for t in range(rows):
        out = jnp.where(row == t, ref[t], out)
    return out


def mask(lists, ids):
    out = jnp.zeros((lists.shape[0], ids.shape[1]), F32)
    for i in range(lists.shape[1]):
        out += jnp.where(lists[:, i : i + 1] == ids, 1.0, 0.0)
    return out


def lanes(n):
    return lax.broadcasted_iota(jnp.int32, (1, n), 1)


def low_lanes(rows):
    return lax.broadcasted_iota(jnp.int32, (rows, 128), 1) < 64


def couple(rows, feats, coefs, masks):
    kh, kl = kern(dot(rows, feats))
    weighted = [coefs * (m * KAPPA) for m in masks]
    weighted = weighted[0] if len(weighted) == 1 else jnp.concatenate(weighted, axis=0)
    return matmul(weighted, kh, kl, NT)


def beside(pair):
    return jnp.where(low_lanes(32), pair[:32], pair[32:])


def kernel(
    rs, pts_in, basis_in, transfer_in, skel_in, near_list_in, near_count_in, inter_list_in, inter_count_in,
    up_t, up_s, up_list_in, up_count_in, out,
    xe, acc, f, ft, t2, bb_h, bb_l, bl_h, bl_l, bu_h, bu_l,
    ce, lh, rh, ftl, ev, et, sv, st, su, fu, tu, ftu, mine, other, zbuf, gc, hc, tc, qh, ql,
    pts, basis, transfer, skel, near_list, near_count, inter_list, inter_count, up_list, up_count,
    in_sem, near_send, near_recv, coef_send, coef_recv, c_send, c_recv, z_send, z_recv, h_send, h_recv,
    y_send, y_recv, x_send, x_recv,
):
    g = lax.axis_index("group")
    b = lax.axis_index("bulk")
    z = lax.rem(lax.div(b, 2), 8)
    y = lax.div(b, 16)
    r = lax.rem(b, 16)
    core = lax.rem(b, 2)
    dev = g * 64 + b

    def at(d):
        d = lax.rem(d + 256, 256)
        return (lax.div(d, 64), lax.rem(d, 64))

    right, left = at(dev + 1), at(dev - 1)

    pairs = (
        (rs, xe.at[0:32, 1024:3072]),
        (pts_in, pts),
        (skel_in, skel),
        (basis_in, basis),
        (transfer_in, transfer),
        (near_list_in, near_list),
        (near_count_in, near_count),
        (inter_list_in, inter_list),
        (inter_count_in, inter_count),
        (up_list_in, up_list),
        (up_count_in, up_count),
        (up_s, sv),
        (up_t.at[:, 128:256], ev.at[0:4096]),
        (up_t.at[:, 0:128], ev.at[4096:8192]),
    )
    loads = [pltpu.make_async_copy(of, to, in_sem.at[i]) for i, (of, to) in enumerate(pairs)]
    for load in loads:
        load.start()
    firsts = (128 + 32 * g, 64 + 16 * g, 32 + 8 * g, 16 + 4 * g, 8 + 2 * g, 4, 2)

    barrier = pltpu.get_barrier_semaphore()

    def greet(device):
        pl.semaphore_signal(barrier, inc=1, device_id=device, device_id_type=MESH)

    greet(right)
    greet(left)

    partner = (g, b + 1 - 2 * core)
    greet(partner)

    def along_z(k):
        return lax.rem(z + k, 8)

    for k in range(1, 8):
        greet((g, y * 16 + along_z(k) * 2 + core))
    for k in range(1, 4):
        greet((g, lax.rem(y + k, 4) * 16 + r))
        greet((lax.rem(g + k, 4), b))

    xe[32:40, 1024:3072] = jnp.zeros((8, 2048), F32)
    loads[1].wait()
    loads[2].wait()
    xe[32:35, 1024:3072] = scaled(pts[...])
    ce[32:40, :] = jnp.zeros((8, 1024), F32)
    order = ((0, 1), (2, 3), (8, 9), (12, 13), (14, 14), (10, 11), (4, 5), (6, 7))
    for i, (m, n) in enumerate(order):
        ce[32:35, i * 128 : i * 128 + 128] = scaled(jnp.concatenate([skel[:, m, :], skel[:, n, :]], axis=1))
    loads[0].wait()

    near_copies = [
        pltpu.make_async_remote_copy(
            xe.at[:, 2048:3072], xe.at[:, 0:1024], near_send.at[0], near_recv.at[0],
            device_id=right, device_id_type=MESH,
        ),
        pltpu.make_async_remote_copy(
            xe.at[:, 1024:2048], xe.at[:, 3072:4096], near_send.at[1], near_recv.at[1],
            device_id=left, device_id_type=MESH,
        ),
    ]

    loads[3].wait()
    loads[4].wait()
    bb_h[...], bb_l[...] = halves(basis[...])
    low128 = low_lanes(128)

    def put(to_h, to_l, at_row, value):
        n = value.shape[0]
        to_h[at_row : at_row + n, :], to_l[at_row : at_row + n, :] = halves(value)

    def twice(e):
        return jnp.concatenate([e, e], axis=1)

    for q in range(3):
        for h in range(2):
            e = twice(transfer[q * 256 + h * 128 : q * 256 + h * 128 + 128, :])
            keep = low128 if h == 0 else jnp.logical_not(low128)
            put(bl_h, bl_l, q * 256 + h * 128, jnp.where(keep, e, 0.0))
    put(bl_h, bl_l, 768, twice(transfer[768:896, :]))
    root_e = transfer[896:960, :]
    put(bl_h, bl_l, 896, twice(root_e))

    leaf = []
    for j in range(4):
        two = jnp.concatenate(
            [xe[0:32, 1024 + 512 * j : 1280 + 512 * j], xe[0:32, 1280 + 512 * j : 1536 + 512 * j]], axis=0
        )
        leaf.append(beside(matmul(two, bb_h[128 * j : 128 * j + 128, :], bb_l[128 * j : 128 * j + 128, :], NT)))

    def lift(values, h, low, first):
        joined = values[0] if len(values) == 1 else jnp.concatenate(values, axis=1)
        n = joined.shape[1]
        return matmul(joined, h[first : first + n, :], low[first : first + n, :])

    mid_a = lift(leaf[0:2], bl_h, bl_l, 0)
    mid_b = lift(leaf[2:4], bl_h, bl_l, 256)
    top = lift([mid_a, mid_b], bl_h, bl_l, 512)
    root = lift([top], bl_h, bl_l, 768)
    term = lift([root[:, 0:64]], bl_h, bl_l, 896)
    mine[...] = jnp.where(low_lanes(16), term[0:16], term[16:32])
    core_copy = pltpu.make_async_remote_copy(
        mine, other, c_send, c_recv, device_id=partner, device_id_type=MESH
    )
    pl.semaphore_wait(barrier, 16)
    core_copy.start()
    for i, value in enumerate((leaf[0], leaf[1], mid_a, top, root, mid_b, leaf[2], leaf[3])):
        ce[0:32, i * 128 : i * 128 + 128] = value
    coef_copies = [
        pltpu.make_async_remote_copy(
            ce.at[:, 384:1024], lh, coef_send.at[0], coef_recv.at[0], device_id=right, device_id_type=MESH
        ),
        pltpu.make_async_remote_copy(
            ce.at[:, 0:640], rh, coef_send.at[1], coef_recv.at[1], device_id=left, device_id_type=MESH
        ),
    ]
    for load in loads[5:11]:
        load.wait()
    near = usable(near_list[...], counted(near_count, 8, 8))
    ids = lanes(4096) // 256
    itself = lax.broadcasted_iota(jnp.int32, (8, 1), 0) + 4 == ids
    t2[...] = (mask(near, ids + (dev * 8 - 4)) + jnp.where(itself, 1.0, 0.0)) * KAPPA
    src, tgt = features(xe[32:40, 1024:3072])
    f[...] = tgt
    ft[1024:3072, :] = as_rows(src)

    core_copy.wait_recv()
    zbuf[z] = mine[...] + other[...]

    def row_copy(k, sender):
        slot = z if sender else along_z(k)
        return pltpu.make_async_remote_copy(
            zbuf.at[slot], zbuf.at[slot], z_send.at[k], z_recv.at[slot],
            device_id=(g, y * 16 + along_z(k) * 2 + core), device_id_type=MESH,
        )

    for k in (4, 3, 5, 2, 6, 1, 7):
        row_copy(k, True).start()
    for copy in coef_copies:
        copy.start()

    def near_leaf(t, first, last, between):
        targets = f[:, t * 256 : t * 256 + 256]
        total = jnp.zeros((32, 256), F32)
        for e in range(first, last):
            part = slice(e * 256, e * 256 + 256)
            x_high, x_low = halves(xe[0:32, part] * t2[t : t + 1, part])
            kh, kl = kern(dot(ft[part, :], targets))
            both = dot(jnp.concatenate([x_high, x_low], axis=0), kh)
            total += both[:32] + both[32:] + dot(x_high, kl)
            between()
        return total

    def spread(chores, blocks):
        state = [0, 0]

        def between():
            state[0] += 1
            until = len(chores) * state[0] // blocks
            for chore in chores[state[1] : until]:
                chore()
            state[1] = until

        return between

    def own_leaf(t, between):
        part = slice(t * 256, t * 256 + 256)
        nugget = NUGGET * xe[0:32, t * 256 + 1024 : t * 256 + 1280]
        acc[:, part] = nugget + near_leaf(t, max(t, 4), min(t + 9, 12), between)

    for load in loads[11:14]:
        load.wait()

    def turn(i):
        first = i // 32 * 4096 + i % 32 * 64
        block = jnp.concatenate([ev[first : first + 64, :], ev[first + 2048 : first + 2112, :]], axis=0)
        et[i * 128 : i * 128 + 128, :] = block.T

    def edge(h, half):
        two = et[pl.ds(half * 4096 + h - (128 if half == 0 else 0), 32, stride=128), :]
        other = pltpu.roll(two, 64, 1)
        low = low_lanes(32)
        return jnp.concatenate([jnp.where(low, two, other), jnp.where(low, other, two)], axis=0)

    low64 = low_lanes(64)

    def put_edge(h, half, to, keep):
        value = edge(h, half)
        put(bu_h, bu_l, to, value if keep is None else jnp.where(keep, value, 0.0))

    nodes = (
        (128 + 32 * g + 8 * y, 0, 0),
        (132 + 32 * g + 8 * y, 0, 256),
        (64 + 16 * g + 4 * y, 1, 512),
        (16 + 4 * g, 1, 896),
        (4, 1, 1280),
    )
    chores = [functools.partial(turn, i) for i in range(64)]
    for first, half, to in nodes:
        for n in range(4):
            keep = low64 if n < 2 else jnp.logical_not(low64)
            chores.append(functools.partial(put_edge, first + n, half, to + n * 64, keep))
    for first, to in ((32 + 8 * g + 2 * y, 768), (8 + 2 * g, 1152)):
        for n in range(2):
            chores.append(functools.partial(put_edge, first + n, 1, to + n * 64, None))
    between = spread(chores, 26)
    for t in range(4):
        own_leaf(t, between)

    for k in range(1, 8):
        row_copy(k, False).wait_recv()
    low16 = low_lanes(16)
    level7 = []
    for j in range(4):
        one, two = zbuf[2 * j], zbuf[2 * j + 1]
        level7.append(
            jnp.concatenate(
                [jnp.where(low16, one, pltpu.roll(two, 64, 1)), jnp.where(low16, pltpu.roll(one, 64, 1), two)], axis=0
            )
        )
    level6 = [lift(level7[0:2], bu_h, bu_l, 0), lift(level7[2:4], bu_h, bu_l, 256)]
    level5 = lift(level6, bu_h, bu_l, 512)
    level4 = lift([level5], bu_h, bu_l, 768)
    hc[y] = level4

    def fourth_copy(k, sender):
        to = lax.rem(y + k, 4)
        slot = y if sender else to
        return pltpu.make_async_remote_copy(
            hc.at[slot], hc.at[slot], h_send.at[k], h_recv.at[slot], device_id=(g, to * 16 + r), device_id_type=MESH
        )

    for k in (2, 1, 3):
        fourth_copy(k, True).start()
    for i, value in enumerate((*level7, *level6, level5)):
        gc[y, :, i * 128 : i * 128 + 128] = value

    def plane_copy(k, sender):
        to = lax.rem(y + k, 4)
        slot = y if sender else to
        return pltpu.make_async_remote_copy(
            gc.at[slot], gc.at[slot], y_send.at[k], y_recv.at[slot], device_id=(g, to * 16 + r), device_id_type=MESH
        )

    for k in (2, 1, 3):
        plane_copy(k, True).start()
    for copy in near_copies:
        copy.start()

    heap = [lax.div(256 + dev, 2 ** (i + 1)) for i in range(7)]
    low1 = lanes(128) < 64

    def turn_skeleton(c, h):
        block = jnp.concatenate([sv[c * 64 : c * 64 + 64, h * 128 : h * 128 + 128]] * 2, axis=0)
        st[c, h * 128 : h * 128 + 128, :] = block.T

    def put_skeletons(ref, m, n, at_lane):
        for c in range(3):
            pair = jnp.where(low1, st[c, pl.ds(m, 1), :], st[c, pl.ds(n, 1), :])
            ref[c : c + 1, at_lane : at_lane + 128] = scaled(pair)

    def put_features():
        fu[...] = features(su[...], "t")[0]
        ftu[...] = as_rows(features(tu[...], "s")[0])

    last = [jnp.concatenate([root_e, root_e], axis=0)]

    def path_product(i):
        if i > 0:
            last[0] = matmul(last[0], *halves(edge(heap[i - 1], 0 if i == 1 else 1)[:, 0:64]))
        qh[i], ql[i] = halves(last[0])

    su[...] = jnp.zeros((8, 4352), F32)
    tu[...] = jnp.zeros((8, 512), F32)
    skeletons = [functools.partial(turn_skeleton, c, h) for c in range(3) for h in range(2)]
    at_lane = 0
    for first, n in zip(firsts, UPPER):
        for i in range(n // 2):
            skeletons.append(functools.partial(put_skeletons, su, first + 2 * i, first + 2 * i + 1, at_lane))
            at_lane += 128
    for i, (m, n) in enumerate(((0, 1), (2, 3), (4, 5), (6, 6))):
        skeletons.append(functools.partial(put_skeletons, tu, heap[m], heap[n], i * 128))
    skeletons.append(put_features)
    products = [functools.partial(path_product, i) for i in range(7)]
    chores = []
    for i, chore in enumerate(skeletons):
        chores.append(chore)
        if i % 6 == 5 and products:
            chores.append(products.pop(0))
    chores += products
    between = spread(chores, 15)
    for t in range(4, 6):
        own_leaf(t, between)

    for k in range(1, 4):
        fourth_copy(k, False).wait_recv()
    low32 = low_lanes(32)
    level4 = [
        jnp.where(low32, hc[0], hc[1]),
        jnp.where(low32, hc[2], hc[3]),
    ]
    level3 = lift(level4, bu_h, bu_l, 896)
    tc[g] = lift([level3], bu_h, bu_l, 1152)

    def group_copy(k, sender):
        to = lax.rem(g + k, 4)
        slot = g if sender else to
        return pltpu.make_async_remote_copy(
            tc.at[slot], tc.at[slot], x_send.at[k], x_recv.at[slot], device_id=(to, b), device_id_type=MESH
        )

    for k in range(1, 4):
        group_copy(k, True).start()

    for copy in near_copies + coef_copies:
        copy.wait_recv()
    src = features(xe[32:40, 0:1024], "s")[0]
    ft[0:1024, :] = as_rows(src)
    src = features(xe[32:40, 3072:4096], "s")[0]
    ft[3072:4096, :] = as_rows(src)
    ftl[...] = as_rows(features(ce[32:40, :], "s")[0])
    spot = lax.broadcasted_iota(jnp.int32, (8, 15), 1)
    slot = lax.broadcasted_iota(jnp.int32, (8, 15), 0)
    counts = jnp.zeros((8, 15), jnp.int32)
    for n in range(15):
        counts = jnp.where(spot == n, inter_count[n], counts)
    inter = jnp.where(slot < counts, inter_list[...], -1000)

    def listed(n, ids):
        return jnp.sum(jnp.where(inter[:, n : n + 1] == ids, 1.0, 0.0), axis=0, keepdims=True)

    one_ids = jnp.where(lax.rem(lanes(384), 128) < 64, lanes(384) // 128 + (dev - 1), -1)
    tables = (
        ([lh[:, 384:640], ce[:, 0:256], ce[:, 768:1024], rh[:, 0:256]], lanes(1024) // 64 + (dev * 8 - 4)),
        ([lh[:, 256:384], ce[:, 256:384], ce[:, 640:768], rh[:, 256:384]], lanes(512) // 64 + (dev * 4 - 2)),
        ([lh[:, 0:128], ce[:, 384:512], rh[:, 384:512]], lanes(384) // 64 + (dev * 2 - 2)),
        ([lh[:, 128:256], ce[:, 512:640], rh[:, 512:640]], one_ids),
    )
    tables = [(jnp.concatenate(parts, axis=1), ids) for parts, ids in tables]
    tables = [(table[0:32], features(table[32:40], "t")[0], ids) for table, ids in tables]
    fields = {}

    def local_field(level, m, n, at_lane, first, width):
        coefs, feats, ids = tables[level]
        part = slice(first, first + width)
        masks = [listed(m, ids[:, part]), listed(n, ids[:, part])]
        fields[at_lane] = beside(couple(ftl[at_lane : at_lane + 128, :], feats[:, part], coefs[:, part], masks))

    node = lax.broadcasted_iota(jnp.int32, (8, 256), 1)
    up_slots = lax.broadcasted_iota(jnp.int32, (8, 1), 0)
    up_lists = up_list[...].astype(F32)
    path = {}

    def path_kernel(i):
        first, n = sum(UPPER[:i]) * 64, UPPER[i] * 64
        column = jnp.sum(jnp.where(node == heap[i], up_lists, 0.0), axis=1, keepdims=True)
        column = jnp.where(up_slots < up_count[heap[i]], column, -1000.0)
        ids = (lanes(n) // 64 + firsts[i]).astype(F32)
        found = jnp.sum(jnp.where(column == ids, 1.0, 0.0), axis=0, keepdims=True)
        path[i] = (found * KAPPA, *kern(dot(ftu[i * 64 : i * 64 + 64, :], fu[:, first : first + n])))

    def path_field(i, coefs):
        found, kh, kl = path[i]
        return matmul(matmul(coefs * found, kh, kl, NT), qh[i], ql[i], NT)

    incoming = []

    def path_step(i, coefs):
        path_kernel(i)
        incoming.append(path_field(i, coefs()))

    def group_lanes(first, last):
        return lambda: jnp.concatenate([gc[k, :, first:last] for k in range(4)], axis=1)

    chores = [functools.partial(path_kernel, i) for i in (5, 6, 0, 1, 2)] + [
        functools.partial(path_step, 3, lambda: jnp.concatenate(level4, axis=1)),
        functools.partial(path_step, 4, lambda: level3),
        functools.partial(local_field, 3, 14, 14, 512, 0, 384),
        functools.partial(local_field, 2, 12, 13, 384, 0, 384),
        functools.partial(local_field, 1, 8, 9, 256, 0, 384),
        functools.partial(local_field, 1, 10, 11, 640, 128, 384),
    ]
    for j, at_lane in enumerate((0, 128, 768, 896)):
        chores.append(functools.partial(local_field, 0, 2 * j, 2 * j + 1, at_lane, j * 128, 640))
    between = spread(chores, 31)
    for t in range(6, 8):
        own_leaf(t, between)
    for t in range(4):
        acc[:, t * 256 : t * 256 + 256] += near_leaf(t, t, 4, between)
    for t in range(4, 8):
        acc[:, t * 256 : t * 256 + 256] += near_leaf(t, 12, t + 9, between)

    for k in range(1, 4):
        group_copy(k, False).wait_recv()
    level2 = [jnp.where(low32, tc[0], tc[1]), jnp.where(low32, tc[2], tc[3])]
    level1 = lift(level2, bu_h, bu_l, 1280)
    for k in range(1, 4):
        plane_copy(k, False).wait_recv()
    incoming.append(path_field(5, jnp.concatenate(level2, axis=1)))
    incoming.append(path_field(6, level1))
    incoming.append(path_field(0, group_lanes(0, 512)()))
    incoming.append(path_field(1, group_lanes(512, 768)()))
    incoming.append(path_field(2, group_lanes(768, 896)()))
    incoming = sum(incoming[1:], incoming[0])
    field0 = [fields[0], fields[128], fields[768], fields[896]]
    field1 = [fields[256], fields[640]]
    field2, field3 = fields[384], fields[512]

    def lower(value, first, n):
        return matmul(value, bl_h[first : first + n, :], bl_l[first : first + n, :], NT)

    down3 = jnp.where(low32, field3 + incoming, 0.0)
    down2 = field2 + lower(down3, 768, 128)
    down1 = lower(down2, 512, 256)
    down1 = [field1[0] + down1[:, 0:128], field1[1] + down1[:, 128:256]]
    for q in range(2):
        down0 = lower(down1[q], q * 256, 256)
        for h in range(2):
            j = 2 * q + h
            pair = field0[j] + down0[:, h * 128 : h * 128 + 128]
            two = jnp.concatenate([jnp.where(low32, pair, 0.0), jnp.where(low32, 0.0, pair)], axis=0)
            far = matmul(two, bb_h[128 * j : 128 * j + 128, :], bb_l[128 * j : 128 * j + 128, :])
            for k in range(2):
                part = slice((2 * j + k) * 256, (2 * j + k) * 256 + 256)
                out[:, part] = acc[:, part] + far[32 * k : 32 * k + 32]

    for copy in near_copies + coef_copies:
        copy.wait_send()

    core_copy.wait_send()
    for k in range(1, 8):
        row_copy(k, True).wait_send()
    for k in range(1, 4):
        fourth_copy(k, True).wait_send()
        plane_copy(k, True).wait_send()
        group_copy(k, True).wait_send()


def on_device(
    rs, pts, basis, transfer, skel, near_list, near_count, inter_list, inter_count, up_t, up_s, up_list, up_count
):
    vmem = pl.BlockSpec(memory_space=pltpu.VMEM)
    anywhere = pl.BlockSpec(memory_space=pl.ANY)
    dma = pltpu.SemaphoreType.DMA
    return pl.pallas_call(
        kernel,
        out_shape=jax.ShapeDtypeStruct((32, 2048), F32),
        in_specs=[anywhere] * 13,
        out_specs=vmem,
        scratch_shapes=[
            pltpu.VMEM((40, 4096), F32),
            pltpu.VMEM((32, 2048), F32),
            pltpu.VMEM((FEATS, 2048), BF16),
            pltpu.VMEM((4096, FEATS), BF16),
            pltpu.VMEM((8, 4096), F32),
            pltpu.VMEM((512, 256), BF16),
            pltpu.VMEM((512, 256), BF16),
            pltpu.VMEM((960, 128), BF16),
            pltpu.VMEM((960, 128), BF16),
            pltpu.VMEM((1536, 128), BF16),
            pltpu.VMEM((1536, 128), BF16),
            pltpu.VMEM((40, 1024), F32),
            pltpu.VMEM((40, 640), F32),
            pltpu.VMEM((40, 640), F32),
            pltpu.VMEM((1024, FEATS), BF16),
            pltpu.VMEM((8192, 128), F32),
            pltpu.VMEM((8192, 128), F32),
            pltpu.VMEM((192, 256), F32),
            pltpu.VMEM((3, 256, 128), F32),
            pltpu.VMEM((8, 4352), F32),
            pltpu.VMEM((FEATS, 4352), BF16),
            pltpu.VMEM((8, 512), F32),
            pltpu.VMEM((512, FEATS), BF16),
            pltpu.VMEM((16, 128), F32),
            pltpu.VMEM((16, 128), F32),
            pltpu.VMEM((8, 16, 128), F32),
            pltpu.VMEM((4, 32, 896), F32),
            pltpu.VMEM((4, 32, 128), F32),
            pltpu.VMEM((4, 32, 128), F32),
            pltpu.VMEM((7, 128, 64), BF16),
            pltpu.VMEM((7, 128, 64), BF16),
            pltpu.VMEM((3, 2048), F32),
            pltpu.VMEM((512, 256), F32),
            pltpu.VMEM((960, 64), F32),
            pltpu.VMEM((3, 15, 64), F32),
            pltpu.VMEM((8, 8), jnp.int32),
            pltpu.SMEM((8,), jnp.int32),
            pltpu.VMEM((8, 15), jnp.int32),
            pltpu.SMEM((15,), jnp.int32),
            pltpu.VMEM((8, 256), jnp.int32),
            pltpu.SMEM((256,), jnp.int32),
            dma((14,)),
            dma((2,)), dma((2,)), dma((2,)), dma((2,)),
            dma, dma, dma((8,)), dma((8,)), dma((4,)), dma((4,)), dma((4,)), dma((4,)), dma((4,)), dma((4,)),
        ],
        compiler_params=pltpu.CompilerParams(
            collective_id=0, has_side_effects=True, vmem_limit_bytes=58 * 2**20
        ),
    )(
        rs, pts, basis.reshape(512, 256), transfer.reshape(960, 64), skel.transpose(1, 0, 2), near_list, near_count,
        inter_list.T, inter_count, up_t.transpose(1, 2, 0).reshape(4096, 256), up_s.transpose(1, 2, 0).reshape(192, 256),
        up_list.T, up_count,
    )


def solution(mesh):
    both = ("group", "bulk")
    in_specs = (
        P(None, both),
        P(None, both),
        P(both, None, None),
        P(both, None, None),
        P(both, None, None),
        P(both, None),
        P(both),
        P(both, None),
        P(both),
        P(),
        P(),
        P(),
        P(),
    )
    return jax.shard_map(
        on_device, mesh=mesh, in_specs=in_specs, out_specs=P(None, both), check_vma=False
    )
```

```python
import functools
import math

import jax
import jax.numpy as jnp
from jax import lax
from jax.experimental import pallas as pl
from jax.experimental.pallas import tpu as pltpu
from jax.sharding import PartitionSpec as P

F32 = jnp.float32
BF16 = jnp.bfloat16
MESH = pl.DeviceIdType.MESH
NN = (((1,), (0,)), ((), ()))
NT = (((1,), (1,)), ((), ()))

ALPHA = 2.0 / math.log(2.0)
KAPPA = 0.2 * math.log(2.0)
SHIFT = 1.0 / math.log(2.0)
SOFT = 0.01 * ALPHA * ALPHA
CENTER = 2.0
NUGGET = 0.5
FEATS = 48
UPPER = (32, 16, 8, 4, 2, 4, 2)


def dot(a, b, dims=NN):
    return lax.dot_general(a, b, dims, preferred_element_type=F32)


def halves(x):
    high = x.astype(BF16)
    return high, (x - high.astype(F32)).astype(BF16)


def matmul(a, high, low, dims=NN):
    m = a.shape[0]
    a_high, a_low = halves(a)
    both = dot(jnp.concatenate([a_high, a_low], axis=0), high, dims)
    return both[:m] + both[m:] + dot(a_high, low, dims)


def kern(w):
    y = w * lax.rsqrt(w)
    return halves((SHIFT + y) * jnp.exp2(-y))


def in_three(x):
    one = x.astype(BF16).astype(F32)
    rest = x - one
    two = rest.astype(BF16).astype(F32)
    return one, two, (rest - two).astype(BF16).astype(F32)


def scaled(x):
    return ALPHA * (x - CENTER)


def features(u, sides="st"):
    row = lax.broadcasted_iota(jnp.int32, u.shape, 0)
    square = jnp.sum(u * u, axis=0, keepdims=True)
    out = []
    if "s" in sides:
        s = jnp.where(row < 3, -2.0 * u, jnp.where(row == 3, square, jnp.where(row == 4, 1.0, 0.0)))
        a, b, c = in_three(s)
        out.append(jnp.concatenate([a, a, b, b, a, c], axis=0))
    if "t" in sides:
        t = jnp.where(row < 3, u, jnp.where(row == 3, 1.0, jnp.where(row == 4, square + SOFT, 0.0)))
        a, b, c = in_three(t)
        out.append(jnp.concatenate([a, b, a, b, c, a], axis=0).astype(BF16))
    return out


def as_rows(f):
    return f.T.astype(BF16)


def usable(values, counts):
    slot = lax.broadcasted_iota(jnp.int32, values.shape, 1)
    return jnp.where(slot < counts, values, -1000)


def counted(ref, rows, width):
    row = lax.broadcasted_iota(jnp.int32, (rows, width), 0)
    out = jnp.zeros((rows, width), jnp.int32)
    for t in range(rows):
        out = jnp.where(row == t, ref[t], out)
    return out


def mask(lists, ids):
    out = jnp.zeros((lists.shape[0], ids.shape[1]), F32)
    for i in range(lists.shape[1]):
        out += jnp.where(lists[:, i : i + 1] == ids, 1.0, 0.0)
    return out


def lanes(n):
    return lax.broadcasted_iota(jnp.int32, (1, n), 1)


def low_lanes(rows):
    return lax.broadcasted_iota(jnp.int32, (rows, 128), 1) < 64


def couple(rows, feats, coefs, masks):
    kh, kl = kern(dot(rows, feats))
    weighted = [coefs * (m * KAPPA) for m in masks]
    weighted = weighted[0] if len(weighted) == 1 else jnp.concatenate(weighted, axis=0)
    return matmul(weighted, kh, kl, NT)


def beside(pair):
    return jnp.where(low_lanes(32), pair[:32], pair[32:])


def kernel(
    rs, pts_in, basis_in, transfer_in, skel_in, near_list_in, near_count_in, inter_list_in, inter_count_in,
    up_t, up_s, up_list_in, up_count_in, out,
    xe, acc, f, ft, t2, bb_h, bb_l, bl_h, bl_l, bu_h, bu_l,
    ce, lh, rh, ftl, ev, et, sv, st, su, fu, tu, ftu, mine, other, zbuf, gc, hc, tc, qh, ql,
    pts, basis, transfer, skel, near_list, near_count, inter_list, inter_count, up_list, up_count,
    in_sem, near_send, near_recv, coef_send, coef_recv, c_send, c_recv, z_send, z_recv, h_send, h_recv,
    y_send, y_recv, x_send, x_recv,
):
    g = lax.axis_index("group")
    b = lax.axis_index("bulk")
    z = lax.rem(lax.div(b, 2), 8)
    y = lax.div(b, 16)
    r = lax.rem(b, 16)
    core = lax.rem(b, 2)
    dev = g * 64 + b

    def at(d):
        d = lax.rem(d + 256, 256)
        return (lax.div(d, 64), lax.rem(d, 64))

    right, left = at(dev + 1), at(dev - 1)

    pairs = (
        (rs, xe.at[0:32, 1024:3072]),
        (pts_in, pts),
        (skel_in, skel),
        (basis_in, basis),
        (transfer_in, transfer),
        (near_list_in, near_list),
        (near_count_in, near_count),
        (inter_list_in, inter_list),
        (inter_count_in, inter_count),
        (up_list_in, up_list),
        (up_count_in, up_count),
        (up_s, sv),
        (up_t.at[:, 128:256], ev.at[0:4096]),
        (up_t.at[:, 0:128], ev.at[4096:8192]),
    )
    loads = [pltpu.make_async_copy(of, to, in_sem.at[i]) for i, (of, to) in enumerate(pairs)]
    for load in loads:
        load.start()
    firsts = (128 + 32 * g, 64 + 16 * g, 32 + 8 * g, 16 + 4 * g, 8 + 2 * g, 4, 2)

    barrier = pltpu.get_barrier_semaphore()

    def greet(device):
        pl.semaphore_signal(barrier, inc=1, device_id=device, device_id_type=MESH)

    greet(right)
    greet(left)

    partner = (g, b + 1 - 2 * core)
    greet(partner)

    def along_z(k):
        return lax.rem(z + k, 8)

    for k in range(1, 8):
        greet((g, y * 16 + along_z(k) * 2 + core))
    for k in range(1, 4):
        greet((g, lax.rem(y + k, 4) * 16 + r))
        greet((lax.rem(g + k, 4), b))

    xe[32:40, 1024:3072] = jnp.zeros((8, 2048), F32)
    loads[1].wait()
    loads[2].wait()
    xe[32:35, 1024:3072] = scaled(pts[...])
    ce[32:40, :] = jnp.zeros((8, 1024), F32)
    order = ((0, 1), (2, 3), (8, 9), (12, 13), (14, 14), (10, 11), (4, 5), (6, 7))
    for i, (m, n) in enumerate(order):
        ce[32:35, i * 128 : i * 128 + 128] = scaled(jnp.concatenate([skel[:, m, :], skel[:, n, :]], axis=1))
    loads[0].wait()

    near_copies = [
        pltpu.make_async_remote_copy(
            xe.at[:, 2048:3072], xe.at[:, 0:1024], near_send.at[0], near_recv.at[0],
            device_id=right, device_id_type=MESH,
        ),
        pltpu.make_async_remote_copy(
            xe.at[:, 1024:2048], xe.at[:, 3072:4096], near_send.at[1], near_recv.at[1],
            device_id=left, device_id_type=MESH,
        ),
    ]

    loads[3].wait()
    loads[4].wait()
    bb_h[...], bb_l[...] = halves(basis[...])
    low128 = low_lanes(128)

    def put(to_h, to_l, at_row, value):
        n = value.shape[0]
        to_h[at_row : at_row + n, :], to_l[at_row : at_row + n, :] = halves(value)

    def twice(e):
        return jnp.concatenate([e, e], axis=1)

    for q in range(3):
        for h in range(2):
            e = twice(transfer[q * 256 + h * 128 : q * 256 + h * 128 + 128, :])
            keep = low128 if h == 0 else jnp.logical_not(low128)
            put(bl_h, bl_l, q * 256 + h * 128, jnp.where(keep, e, 0.0))
    put(bl_h, bl_l, 768, twice(transfer[768:896, :]))
    root_e = transfer[896:960, :]
    put(bl_h, bl_l, 896, twice(root_e))

    leaf = []
    for j in range(4):
        two = jnp.concatenate(
            [xe[0:32, 1024 + 512 * j : 1280 + 512 * j], xe[0:32, 1280 + 512 * j : 1536 + 512 * j]], axis=0
        )
        leaf.append(beside(matmul(two, bb_h[128 * j : 128 * j + 128, :], bb_l[128 * j : 128 * j + 128, :], NT)))

    def lift(values, h, low, first):
        joined = values[0] if len(values) == 1 else jnp.concatenate(values, axis=1)
        n = joined.shape[1]
        return matmul(joined, h[first : first + n, :], low[first : first + n, :])

    mid_a = lift(leaf[0:2], bl_h, bl_l, 0)
    mid_b = lift(leaf[2:4], bl_h, bl_l, 256)
    top = lift([mid_a, mid_b], bl_h, bl_l, 512)
    root = lift([top], bl_h, bl_l, 768)
    term = lift([root[:, 0:64]], bl_h, bl_l, 896)
    mine[...] = jnp.where(low_lanes(16), term[0:16], term[16:32])
    core_copy = pltpu.make_async_remote_copy(
        mine, other, c_send, c_recv, device_id=partner, device_id_type=MESH
    )
    pl.semaphore_wait(barrier, 16)
    core_copy.start()
    for i, value in enumerate((leaf[0], leaf[1], mid_a, top, root, mid_b, leaf[2], leaf[3])):
        ce[0:32, i * 128 : i * 128 + 128] = value
    coef_copies = [
        pltpu.make_async_remote_copy(
            ce.at[:, 384:1024], lh, coef_send.at[0], coef_recv.at[0], device_id=right, device_id_type=MESH
        ),
        pltpu.make_async_remote_copy(
            ce.at[:, 0:640], rh, coef_send.at[1], coef_recv.at[1], device_id=left, device_id_type=MESH
        ),
    ]
    for load in loads[5:11]:
        load.wait()
    near = usable(near_list[...], counted(near_count, 8, 8))
    ids = lanes(4096) // 256
    itself = lax.broadcasted_iota(jnp.int32, (8, 1), 0) + 4 == ids
    t2[...] = (mask(near, ids + (dev * 8 - 4)) + jnp.where(itself, 1.0, 0.0)) * KAPPA
    src, tgt = features(xe[32:40, 1024:3072])
    f[...] = tgt
    ft[1024:3072, :] = as_rows(src)

    core_copy.wait_recv()
    zbuf[z] = mine[...] + other[...]

    def row_copy(k, sender):
        slot = z if sender else along_z(k)
        return pltpu.make_async_remote_copy(
            zbuf.at[slot], zbuf.at[slot], z_send.at[k], z_recv.at[slot],
            device_id=(g, y * 16 + along_z(k) * 2 + core), device_id_type=MESH,
        )

    for k in (4, 3, 5, 2, 6, 1, 7):
        row_copy(k, True).start()
    for copy in coef_copies:
        copy.start()

    def near_leaf(t, first, last, between):
        targets = f[:, t * 256 : t * 256 + 256]
        total = jnp.zeros((32, 256), F32)
        for e in range(first, last):
            part = slice(e * 256, e * 256 + 256)
            x_high, x_low = halves(xe[0:32, part] * t2[t : t + 1, part])
            kh, kl = kern(dot(ft[part, :], targets))
            both = dot(jnp.concatenate([x_high, x_low], axis=0), kh)
            total += both[:32] + both[32:] + dot(x_high, kl)
            between()
        return total

    def spread(chores, blocks):
        state = [0, 0]

        def between():
            state[0] += 1
            until = len(chores) * state[0] // blocks
            for chore in chores[state[1] : until]:
                chore()
            state[1] = until

        return between

    def own_leaf(t, between):
        part = slice(t * 256, t * 256 + 256)
        nugget = NUGGET * xe[0:32, t * 256 + 1024 : t * 256 + 1280]
        acc[:, part] = nugget + near_leaf(t, max(t, 4), min(t + 9, 12), between)

    for load in loads[11:14]:
        load.wait()

    def turn(i):
        first = i // 32 * 4096 + i % 32 * 64
        block = jnp.concatenate([ev[first : first + 64, :], ev[first + 2048 : first + 2112, :]], axis=0)
        et[i * 128 : i * 128 + 128, :] = block.T

    def edge(h, half):
        two = et[pl.ds(half * 4096 + h - (128 if half == 0 else 0), 32, stride=128), :]
        other = pltpu.roll(two, 64, 1)
        low = low_lanes(32)
        return jnp.concatenate([jnp.where(low, two, other), jnp.where(low, other, two)], axis=0)

    low64 = low_lanes(64)

    def put_edge(h, half, to, keep):
        value = edge(h, half)
        put(bu_h, bu_l, to, value if keep is None else jnp.where(keep, value, 0.0))

    nodes = (
        (128 + 32 * g + 8 * y, 0, 0),
        (132 + 32 * g + 8 * y, 0, 256),
        (64 + 16 * g + 4 * y, 1, 512),
        (16 + 4 * g, 1, 896),
        (4, 1, 1280),
    )
    chores = [functools.partial(turn, i) for i in range(64)]
    for first, half, to in nodes:
        for n in range(4):
            keep = low64 if n < 2 else jnp.logical_not(low64)
            chores.append(functools.partial(put_edge, first + n, half, to + n * 64, keep))
    for first, to in ((32 + 8 * g + 2 * y, 768), (8 + 2 * g, 1152)):
        for n in range(2):
            chores.append(functools.partial(put_edge, first + n, 1, to + n * 64, None))
    between = spread(chores, 26)
    for t in range(4):
        own_leaf(t, between)

    for k in range(1, 8):
        row_copy(k, False).wait_recv()
    low16 = low_lanes(16)
    level7 = []
    for j in range(4):
        one, two = zbuf[2 * j], zbuf[2 * j + 1]
        level7.append(
            jnp.concatenate(
                [jnp.where(low16, one, pltpu.roll(two, 64, 1)), jnp.where(low16, pltpu.roll(one, 64, 1), two)], axis=0
            )
        )
    level6 = [lift(level7[0:2], bu_h, bu_l, 0), lift(level7[2:4], bu_h, bu_l, 256)]
    level5 = lift(level6, bu_h, bu_l, 512)
    level4 = lift([level5], bu_h, bu_l, 768)
    hc[y] = level4

    def fourth_copy(k, sender):
        to = lax.rem(y + k, 4)
        slot = y if sender else to
        return pltpu.make_async_remote_copy(
            hc.at[slot], hc.at[slot], h_send.at[k], h_recv.at[slot], device_id=(g, to * 16 + r), device_id_type=MESH
        )

    for k in (2, 1, 3):
        fourth_copy(k, True).start()
    for i, value in enumerate((*level7, *level6, level5)):
        gc[y, :, i * 128 : i * 128 + 128] = value

    def plane_copy(k, sender):
        to = lax.rem(y + k, 4)
        slot = y if sender else to
        return pltpu.make_async_remote_copy(
            gc.at[slot], gc.at[slot], y_send.at[k], y_recv.at[slot], device_id=(g, to * 16 + r), device_id_type=MESH
        )

    for k in (2, 1, 3):
        plane_copy(k, True).start()
    for copy in near_copies:
        copy.start()

    heap = [lax.div(256 + dev, 2 ** (i + 1)) for i in range(7)]
    low1 = lanes(128) < 64

    def turn_skeleton(c, h):
        block = jnp.concatenate([sv[c * 64 : c * 64 + 64, h * 128 : h * 128 + 128]] * 2, axis=0)
        st[c, h * 128 : h * 128 + 128, :] = block.T

    def put_skeletons(ref, m, n, at_lane):
        for c in range(3):
            pair = jnp.where(low1, st[c, pl.ds(m, 1), :], st[c, pl.ds(n, 1), :])
            ref[c : c + 1, at_lane : at_lane + 128] = scaled(pair)

    def put_features():
        fu[...] = features(su[...], "t")[0]
        ftu[...] = as_rows(features(tu[...], "s")[0])

    last = [jnp.concatenate([root_e, root_e], axis=0)]

    def path_product(i):
        if i > 0:
            last[0] = matmul(last[0], *halves(edge(heap[i - 1], 0 if i == 1 else 1)[:, 0:64]))
        qh[i], ql[i] = halves(last[0])

    su[...] = jnp.zeros((8, 4352), F32)
    tu[...] = jnp.zeros((8, 512), F32)
    skeletons = [functools.partial(turn_skeleton, c, h) for c in range(3) for h in range(2)]
    at_lane = 0
    for first, n in zip(firsts, UPPER):
        for i in range(n // 2):
            skeletons.append(functools.partial(put_skeletons, su, first + 2 * i, first + 2 * i + 1, at_lane))
            at_lane += 128
    for i, (m, n) in enumerate(((0, 1), (2, 3), (4, 5), (6, 6))):
        skeletons.append(functools.partial(put_skeletons, tu, heap[m], heap[n], i * 128))
    skeletons.append(put_features)
    products = [functools.partial(path_product, i) for i in range(7)]
    chores = []
    for i, chore in enumerate(skeletons):
        chores.append(chore)
        if i % 6 == 5 and products:
            chores.append(products.pop(0))
    chores += products
    between = spread(chores, 15)
    for t in range(4, 6):
        own_leaf(t, between)

    for k in range(1, 4):
        fourth_copy(k, False).wait_recv()
    low32 = low_lanes(32)
    level4 = [
        jnp.where(low32, hc[0], hc[1]),
        jnp.where(low32, hc[2], hc[3]),
    ]
    level3 = lift(level4, bu_h, bu_l, 896)
    tc[g] = lift([level3], bu_h, bu_l, 1152)

    def group_copy(k, sender):
        to = lax.rem(g + k, 4)
        slot = g if sender else to
        return pltpu.make_async_remote_copy(
            tc.at[slot], tc.at[slot], x_send.at[k], x_recv.at[slot], device_id=(to, b), device_id_type=MESH
        )

    for k in range(1, 4):
        group_copy(k, True).start()

    for copy in near_copies + coef_copies:
        copy.wait_recv()
    src = features(xe[32:40, 0:1024], "s")[0]
    ft[0:1024, :] = as_rows(src)
    src = features(xe[32:40, 3072:4096], "s")[0]
    ft[3072:4096, :] = as_rows(src)
    ftl[...] = as_rows(features(ce[32:40, :], "s")[0])
    spot = lax.broadcasted_iota(jnp.int32, (8, 15), 1)
    slot = lax.broadcasted_iota(jnp.int32, (8, 15), 0)
    counts = jnp.zeros((8, 15), jnp.int32)
    for n in range(15):
        counts = jnp.where(spot == n, inter_count[n], counts)
    inter = jnp.where(slot < counts, inter_list[...], -1000)

    def listed(n, ids):
        return jnp.sum(jnp.where(inter[:, n : n + 1] == ids, 1.0, 0.0), axis=0, keepdims=True)

    one_ids = jnp.where(lax.rem(lanes(384), 128) < 64, lanes(384) // 128 + (dev - 1), -1)
    tables = (
        ([lh[:, 384:640], ce[:, 0:256], ce[:, 768:1024], rh[:, 0:256]], lanes(1024) // 64 + (dev * 8 - 4)),
        ([lh[:, 256:384], ce[:, 256:384], ce[:, 640:768], rh[:, 256:384]], lanes(512) // 64 + (dev * 4 - 2)),
        ([lh[:, 0:128], ce[:, 384:512], rh[:, 384:512]], lanes(384) // 64 + (dev * 2 - 2)),
        ([lh[:, 128:256], ce[:, 512:640], rh[:, 512:640]], one_ids),
    )
    tables = [(jnp.concatenate(parts, axis=1), ids) for parts, ids in tables]
    tables = [(table[0:32], features(table[32:40], "t")[0], ids) for table, ids in tables]
    fields = {}

    def local_field(level, m, n, at_lane, first, width):
        coefs, feats, ids = tables[level]
        part = slice(first, first + width)
        masks = [listed(m, ids[:, part]), listed(n, ids[:, part])]
        fields[at_lane] = beside(couple(ftl[at_lane : at_lane + 128, :], feats[:, part], coefs[:, part], masks))

    node = lax.broadcasted_iota(jnp.int32, (8, 256), 1)
    up_slots = lax.broadcasted_iota(jnp.int32, (8, 1), 0)
    up_lists = up_list[...].astype(F32)
    path = {}

    def path_kernel(i):
        first, n = sum(UPPER[:i]) * 64, UPPER[i] * 64
        column = jnp.sum(jnp.where(node == heap[i], up_lists, 0.0), axis=1, keepdims=True)
        column = jnp.where(up_slots < up_count[heap[i]], column, -1000.0)
        ids = (lanes(n) // 64 + firsts[i]).astype(F32)
        found = jnp.sum(jnp.where(column == ids, 1.0, 0.0), axis=0, keepdims=True)
        path[i] = (found * KAPPA, *kern(dot(ftu[i * 64 : i * 64 + 64, :], fu[:, first : first + n])))

    def path_field(i, coefs):
        found, kh, kl = path[i]
        return matmul(matmul(coefs * found, kh, kl, NT), qh[i], ql[i], NT)

    incoming = []

    def path_step(i, coefs):
        path_kernel(i)
        incoming.append(path_field(i, coefs()))

    def group_lanes(first, last):
        return lambda: jnp.concatenate([gc[k, :, first:last] for k in range(4)], axis=1)

    chores = [functools.partial(path_kernel, i) for i in (5, 6, 0, 1, 2)] + [
        functools.partial(path_step, 3, lambda: jnp.concatenate(level4, axis=1)),
        functools.partial(path_step, 4, lambda: level3),
        functools.partial(local_field, 3, 14, 14, 512, 0, 384),
        functools.partial(local_field, 2, 12, 13, 384, 0, 384),
        functools.partial(local_field, 1, 8, 9, 256, 0, 384),
        functools.partial(local_field, 1, 10, 11, 640, 128, 384),
    ]
    for j, at_lane in enumerate((0, 128, 768, 896)):
        chores.append(functools.partial(local_field, 0, 2 * j, 2 * j + 1, at_lane, j * 128, 640))
    between = spread(chores, 31)
    for t in range(6, 8):
        own_leaf(t, between)
    for t in range(4):
        acc[:, t * 256 : t * 256 + 256] += near_leaf(t, t, 4, between)
    for t in range(4, 8):
        acc[:, t * 256 : t * 256 + 256] += near_leaf(t, 12, t + 9, between)

    for k in range(1, 4):
        group_copy(k, False).wait_recv()
    level2 = [jnp.where(low32, tc[0], tc[1]), jnp.where(low32, tc[2], tc[3])]
    level1 = lift(level2, bu_h, bu_l, 1280)
    incoming.append(path_field(5, jnp.concatenate(level2, axis=1)))
    incoming.append(path_field(6, level1))
    for k in range(1, 4):
        plane_copy(k, False).wait_recv()
    incoming.append(path_field(0, group_lanes(0, 512)()))
    incoming.append(path_field(1, group_lanes(512, 768)()))
    incoming.append(path_field(2, group_lanes(768, 896)()))
    incoming = sum(incoming[1:], incoming[0])
    field0 = [fields[0], fields[128], fields[768], fields[896]]
    field1 = [fields[256], fields[640]]
    field2, field3 = fields[384], fields[512]

    def lower(value, first, n):
        return matmul(value, bl_h[first : first + n, :], bl_l[first : first + n, :], NT)

    down3 = jnp.where(low32, field3 + incoming, 0.0)
    down2 = field2 + lower(down3, 768, 128)
    down1 = lower(down2, 512, 256)
    down1 = [field1[0] + down1[:, 0:128], field1[1] + down1[:, 128:256]]
    for q in range(2):
        down0 = lower(down1[q], q * 256, 256)
        for h in range(2):
            j = 2 * q + h
            pair = field0[j] + down0[:, h * 128 : h * 128 + 128]
            two = jnp.concatenate([jnp.where(low32, pair, 0.0), jnp.where(low32, 0.0, pair)], axis=0)
            far = matmul(two, bb_h[128 * j : 128 * j + 128, :], bb_l[128 * j : 128 * j + 128, :])
            for k in range(2):
                part = slice((2 * j + k) * 256, (2 * j + k) * 256 + 256)
                out[:, part] = acc[:, part] + far[32 * k : 32 * k + 32]

    for copy in near_copies + coef_copies:
        copy.wait_send()

    core_copy.wait_send()
    for k in range(1, 8):
        row_copy(k, True).wait_send()
    for k in range(1, 4):
        fourth_copy(k, True).wait_send()
        plane_copy(k, True).wait_send()
        group_copy(k, True).wait_send()


def on_device(
    rs, pts, basis, transfer, skel, near_list, near_count, inter_list, inter_count, up_t, up_s, up_list, up_count
):
    vmem = pl.BlockSpec(memory_space=pltpu.VMEM)
    anywhere = pl.BlockSpec(memory_space=pl.ANY)
    dma = pltpu.SemaphoreType.DMA
    return pl.pallas_call(
        kernel,
        out_shape=jax.ShapeDtypeStruct((32, 2048), F32),
        in_specs=[anywhere] * 13,
        out_specs=vmem,
        scratch_shapes=[
            pltpu.VMEM((40, 4096), F32),
            pltpu.VMEM((32, 2048), F32),
            pltpu.VMEM((FEATS, 2048), BF16),
            pltpu.VMEM((4096, FEATS), BF16),
            pltpu.VMEM((8, 4096), F32),
            pltpu.VMEM((512, 256), BF16),
            pltpu.VMEM((512, 256), BF16),
            pltpu.VMEM((960, 128), BF16),
            pltpu.VMEM((960, 128), BF16),
            pltpu.VMEM((1536, 128), BF16),
            pltpu.VMEM((1536, 128), BF16),
            pltpu.VMEM((40, 1024), F32),
            pltpu.VMEM((40, 640), F32),
            pltpu.VMEM((40, 640), F32),
            pltpu.VMEM((1024, FEATS), BF16),
            pltpu.VMEM((8192, 128), F32),
            pltpu.VMEM((8192, 128), F32),
            pltpu.VMEM((192, 256), F32),
            pltpu.VMEM((3, 256, 128), F32),
            pltpu.VMEM((8, 4352), F32),
            pltpu.VMEM((FEATS, 4352), BF16),
            pltpu.VMEM((8, 512), F32),
            pltpu.VMEM((512, FEATS), BF16),
            pltpu.VMEM((16, 128), F32),
            pltpu.VMEM((16, 128), F32),
            pltpu.VMEM((8, 16, 128), F32),
            pltpu.VMEM((4, 32, 896), F32),
            pltpu.VMEM((4, 32, 128), F32),
            pltpu.VMEM((4, 32, 128), F32),
            pltpu.VMEM((7, 128, 64), BF16),
            pltpu.VMEM((7, 128, 64), BF16),
            pltpu.VMEM((3, 2048), F32),
            pltpu.VMEM((512, 256), F32),
            pltpu.VMEM((960, 64), F32),
            pltpu.VMEM((3, 15, 64), F32),
            pltpu.VMEM((8, 8), jnp.int32),
            pltpu.SMEM((8,), jnp.int32),
            pltpu.VMEM((8, 15), jnp.int32),
            pltpu.SMEM((15,), jnp.int32),
            pltpu.VMEM((8, 256), jnp.int32),
            pltpu.SMEM((256,), jnp.int32),
            dma((14,)),
            dma((2,)), dma((2,)), dma((2,)), dma((2,)),
            dma, dma, dma((8,)), dma((8,)), dma((4,)), dma((4,)), dma((4,)), dma((4,)), dma((4,)), dma((4,)),
        ],
        compiler_params=pltpu.CompilerParams(
            collective_id=0, has_side_effects=True, vmem_limit_bytes=58 * 2**20
        ),
    )(
        rs, pts, basis.reshape(512, 256), transfer.reshape(960, 64), skel.transpose(1, 0, 2), near_list, near_count,
        inter_list.T, inter_count, up_t.transpose(1, 2, 0).reshape(4096, 256), up_s.transpose(1, 2, 0).reshape(192, 256),
        up_list.T, up_count,
    )


def solution(mesh):
    both = ("group", "bulk")
    in_specs = (
        P(None, both),
        P(None, both),
        P(both, None, None),
        P(both, None, None),
        P(both, None, None),
        P(both, None),
        P(both),
        P(both, None),
        P(both),
        P(),
        P(),
        P(),
        P(),
    )
    return jax.shard_map(
        on_device, mesh=mesh, in_specs=in_specs, out_specs=P(None, both), check_vma=False
    )
```
